32 devices in a mesh: slab: 8 (over y, x, core), orb: 4 (over z).
Axes of the slice: x: 2, y: 2, z: 4, core: 2. Of those that a mesh axis runs over, the one named last changes fastest.
Arguments:
- orbitals: float32 [4, 32, 256, 512], P('orb', 'slab'), may hold values from -6 to 6
- potential: float32 [32, 256, 512], P('slab'), may hold values from -1 to 1
- coeffs: float32 [3], replicated, may hold values from 0.4 to 1.2
Outputs:
- density: float32 [32, 256, 512], P('slab', 'orb')
The draws below stay inside these ranges and needn't reach their ends.
All inputs are finite; a program needn't handle non-finite values.
Results may differ from the reference program's by a relative error of at most 0.00002.
Values sent between devices are 32-bit elements; how exact they have to be, the bound alone decides.
No kernel may reach another device: no remote copies, remote signals or barrier semaphores. Data moves between devices by JAX's collectives and lax.ppermute only.
A program may use at most 128 MiB of HBM per device.

```python
import jax
import jax.numpy as jnp

NX = 256
NY = 512
TERMS = 3
NZ = 32
ORBS = 4


def levels(key, shape, cuts, smallest, top_value):
    level, own = 1.0, jax.random.fold_in(key, 6)
    for position, parts in cuts:
        steps = jnp.exp(jax.random.uniform(jax.random.fold_in(own, position), (parts,), jnp.float32, smallest / len(cuts), top_value / len(cuts)))
        level = level * jnp.repeat(steps, shape[position] // parts).reshape([-1 if axis == position else 1 for axis in range(len(shape))])
    return level


def centred(key, extent, scale, most, cuts=(), kind=jnp.bfloat16):
    level = levels(key, extent, cuts, -0.22, 0.18) if cuts else 1.0
    drawn = jax.random.normal(key, extent, jnp.float32) * scale * level
    return jnp.minimum(jnp.maximum(drawn, -most), most).astype(kind)


def setup_inputs(seed: int = 0) -> dict:
    streams_of = jax.random.split(jax.random.key(seed), 4)
    orbitals = centred(streams_of[0], (ORBS, NZ, NX, NY), 1.0, 6.0, ((0, 4), (1, 8)), jnp.float32)
    potential = jnp.clip(jax.random.uniform(streams_of[1], (NZ, NX, NY), jnp.float32, -1.0, 1.0) * levels(streams_of[1], (NZ, NX, NY), ((0, 8),), -0.4, 0.0), -1.0, 1.0)
    coeffs = jnp.clip(jax.random.uniform(streams_of[2], (TERMS,), jnp.float32, 0.4, 1.2), 0.4, 1.2)
    return {"orbitals": orbitals, "potential": potential, "coeffs": coeffs}


def laplace(field):
    total = jnp.zeros_like(field)
    for axis in range(3):
        near = jnp.roll(field, 1, axis) + jnp.roll(field, -1, axis)
        far = jnp.roll(field, 2, axis) + jnp.roll(field, -2, axis)
        total = total + (-2.5 * field + (4.0 / 3.0) * near - (1.0 / 12.0) * far)
    return total


def scaled(field, potential):
    return ((-0.5 * laplace(field) + potential * field) - 4.0 * field) / 5.0


def reference(orbitals, potential, coeffs):
    accum = jnp.zeros(potential.shape, jnp.float32)
    for index in range(ORBS):
        psi = orbitals[index]
        first = scaled(psi, potential)
        second = 2.0 * scaled(first, potential) - psi
        filtered = coeffs[0] * psi + coeffs[1] * first + coeffs[2] * second
        accum = accum + filtered * filtered
    return accum / ORBS
```

```python
import functools

import jax
import jax.numpy as jnp
from jax import lax
from jax.experimental import pallas as pl
from jax.experimental.pallas import tpu as pltpu
from jax.sharding import PartitionSpec as P

NEAR = -2.0 / 15.0
FAR = 1.0 / 120.0
BLOCK = 16


def own(q, odd):
    return jnp.where(odd == 1, 3 - q, q)


def parity():
    return lax.rem(lax.axis_index("slab"), 2)


def with_halo(ref, plane, start, count):
    rows = ref.shape[-2]
    before = pl.multiple_of(lax.rem(start + rows - 8, rows), 8)
    after = pl.multiple_of(lax.rem(start + count, rows), 8)
    return jnp.concatenate(
        [
            ref[plane, pl.ds(before, 8), :],
            ref[plane, pl.ds(start, count), :],
            ref[plane, pl.ds(after, 8), :],
        ],
        axis=0,
    )


def in_plane(ext):
    count, lanes = ext.shape[0] - 16, ext.shape[1]
    mid = ext[8 : 8 + count]
    near = ext[7 : 7 + count] + ext[9 : 9 + count]
    near = near + (pltpu.roll(mid, 1, 1) + pltpu.roll(mid, lanes - 1, 1))
    far = ext[6 : 6 + count] + ext[10 : 10 + count]
    far = far + (pltpu.roll(mid, 2, 1) + pltpu.roll(mid, lanes - 2, 1))
    return mid, near, far


def apply_s(ext, pot, near_z, far_z):
    mid, near, far = in_plane(ext)
    return mid, (
        mid * (0.2 * pot - 0.05) + NEAR * (near + near_z) + FAR * (far + far_z)
    )


def blocks(rows, body):
    def step(i, carry):
        body(pl.multiple_of(i * BLOCK, BLOCK))
        return carry

    lax.fori_loop(0, rows // BLOCK, step, 0)


def start_kernel(psi, pot, g):
    odd = parity()

    def body(r):
        here = pl.ds(r, BLOCK)
        at = [own(q, odd) for q in range(4)]
        e0, e1 = with_halo(psi, at[0], r, BLOCK), with_halo(psi, at[1], r, BLOCK)
        p2, p3 = psi[at[2], here, :], psi[at[3], here, :]
        g[0, here, :] = apply_s(e0, pot[at[0], here, :], e1[8:-8], p2)[1]
        g[1, here, :] = apply_s(e1, pot[at[1], here, :], e0[8:-8] + p2, p3)[1]

    blocks(psi.shape[1], body)


def inner_kernel(c, psi, pot, psi_in, pot_in, g, t, h):
    odd = parity()
    at = [own(q, odd) for q in range(4)]
    base, one, two = c[0] - c[2], c[1], 2.0 * c[2]

    def first(r):
        here = pl.ds(r, BLOCK)
        e2, e3 = with_halo(psi, at[2], r, BLOCK), with_halo(psi, at[3], r, BLOCK)
        p0, p1 = psi[at[0], here, :], psi[at[1], here, :]
        p4, p5 = psi_in[at[0], here, :], psi_in[at[1], here, :]
        t[0, here, :] = apply_s(e2, pot[at[2], here, :], p1 + e3[8:-8], p0 + p4)[1]
        t[1, here, :] = apply_s(e3, pot[at[3], here, :], e2[8:-8] + p4, p1 + p5)[1]

    def second(r):
        here = pl.ds(r, BLOCK)
        e4 = with_halo(psi_in, at[0], r, BLOCK)
        e5 = with_halo(psi_in, at[1], r, BLOCK)
        p2, p3 = psi[at[2], here, :], psi[at[3], here, :]
        p6, p7 = psi_in[at[2], here, :], psi_in[at[3], here, :]
        t4 = apply_s(e4, pot_in[odd, here, :], p3 + e5[8:-8], p2 + p6)[1]
        t5 = apply_s(e5, pot_in[1 - odd, here, :], e4[8:-8] + p6, p3 + p7)[1]
        g0, g1 = g[0, here, :], g[1, here, :]
        e2, e3 = with_halo(t, 0, r, BLOCK), with_halo(t, 1, r, BLOCK)
        t2, s2 = apply_s(e2, pot[at[2], here, :], g1 + e3[8:-8], g0 + t4)
        t3, s3 = apply_s(e3, pot[at[3], here, :], e2[8:-8] + t4, g1 + t5)
        h[0, here, :] = base * p2 + one * t2 + two * s2
        h[1, here, :] = base * p3 + one * t3 + two * s3

    blocks(psi.shape[1], first)
    blocks(psi.shape[1], second)


def halo_terms(halo, band, odd):
    near, far = halo[1 - odd, band], halo[odd, band]
    return NEAR * near + FAR * far, FAR * near


def face_kernel(chunk, halo, g, f):
    odd = parity()
    lo, hi = chunk
    for band in range(halo.shape[1]):
        d0, d1 = halo_terms(halo, band, odd)
        f[0, band] = g[0, band, lo:hi, :] + d0
        f[1, band] = g[1, band, lo:hi, :] + d1


def square(x, bands):
    return x * x * (1.0 / bands)


def back_kernel(chunk, c, halo, h, keep, send):
    odd = parity()
    lo, hi = chunk
    two = 2.0 * c[2]
    me = lax.axis_index("orb")
    bands = halo.shape[1]

    def part(band, out, slot):
        d0, d1 = halo_terms(halo, band, odd)
        v2 = h[0, band, lo:hi, :] + two * (NEAR * d1 + FAR * d0)
        v3 = h[1, band, lo:hi, :] + (two * FAR) * d1
        out[slot, 0] = square(v2, bands)
        out[slot, 1] = square(v3, bands)

    part(me ^ 1, send, 0)
    part(me ^ 2, send, 1)
    part(me, keep, 0)
    part(me ^ 3, keep, 1)


def front_kernel(chunks, c, psi, pot, t, *rest):
    fs, h, scratch = rest[:-2], rest[-2], rest[-1]
    odd = parity()
    at = [own(q, odd) for q in range(2)]
    base, one, two = c[0] - c[2], c[1], 2.0 * c[2]
    rows = psi.shape[1]
    for (lo, hi), f in zip(chunks, fs):
        bands = f.shape[1]
        for band in range(bands):
            first_row = band * (rows // bands)
            for q in range(2):
                scratch[q, first_row + lo : first_row + hi, :] = f[q, band]

    def body(r):
        here = pl.ds(r, BLOCK)
        e0, e1 = with_halo(scratch, 0, r, BLOCK), with_halo(scratch, 1, r, BLOCK)
        t2, t3 = t[0, here, :], t[1, here, :]
        f0, s0 = apply_s(e0, pot[at[0], here, :], e1[8:-8], t2)
        f1, s1 = apply_s(e1, pot[at[1], here, :], e0[8:-8] + t2, t3)
        h[0, here, :] = base * psi[at[0], here, :] + one * f0 + two * s0
        h[1, here, :] = base * psi[at[1], here, :] + one * f1 + two * s1

    blocks(rows, body)


def last_kernel(chunk, c, halo, h, keep, send):
    lo, hi = chunk
    two = 2.0 * c[2]
    me = lax.axis_index("orb")
    bands = halo.shape[1]

    def part(band, out, slot):
        near, far = halo[0, band], halo[1, band]
        v0 = h[0, band, lo:hi, :] + two * (NEAR * near + FAR * far)
        v1 = h[1, band, lo:hi, :] + (two * FAR) * near
        out[slot, 0] = square(v0, bands)
        out[slot, 1] = square(v1, bands)

    part(me ^ 1, send, 0)
    part(me ^ 2, send, 1)
    part(me, keep, 0)
    part(me ^ 3, keep, 1)


def join_kernel(places, *refs):
    out = refs[-1]
    odd = parity()
    for i, (q, (lo, hi)) in enumerate(places):
        keep, came, far = refs[3 * i : 3 * i + 3]
        for j in range(2):
            out[own(q + j, odd), lo:hi, :] = keep[0, j] + came[0, j] + far[j]


def call(kernel, out, args, scalars=0, scratch=(), flops=0):
    vmem = pl.BlockSpec(memory_space=pltpu.VMEM)
    smem = pl.BlockSpec(memory_space=pltpu.SMEM)
    many = isinstance(out, list)
    shapes = [jax.ShapeDtypeStruct(s, jnp.float32) for s in (out if many else [out])]
    total = sum(4 * int(x.size) for x in list(args) + shapes)
    result = pl.pallas_call(
        kernel,
        out_shape=shapes,
        in_specs=[smem] * scalars + [vmem] * (len(args) - scalars),
        out_specs=[vmem] * len(shapes),
        scratch_shapes=list(scratch),
        compiler_params=pltpu.CompilerParams(vmem_limit_bytes=40 * 2**20),
        cost_estimate=pl.CostEstimate(
            flops=flops, bytes_accessed=total, transcendentals=0
        ),
    )(*args)
    return result if many else result[0]


def shards(orbitals, potential, coeffs):
    psi = orbitals[0]
    slabs, bands = lax.axis_size("slab"), lax.axis_size("orb")
    planes, rows, lanes = psi.shape
    wide = rows // bands
    odd = parity()
    me = lax.axis_index("orb")
    chunks = [(0, wide // 2), (wide // 2, wide)]
    face = [(s, s - 1 if s % 2 == 0 else s + 1) for s in range(slabs)]
    face = [(s, d % slabs) for s, d in face]
    partner = [(s, s ^ 1) for s in range(slabs)]

    banded = psi.reshape(planes, bands, wide, lanes)
    halos = []
    for lo, hi in chunks:
        piece = lax.dynamic_slice(
            banded[:, :, lo:hi], (2 * odd, 0, 0, 0), (2, bands, hi - lo, lanes)
        )
        halos.append(lax.ppermute(piece, "slab", face))
    psi_in = lax.ppermute(psi, "slab", partner)
    pot_in = lax.ppermute(
        lax.dynamic_slice(potential, (2 - 2 * odd, 0, 0), (2, rows, lanes)),
        "slab",
        partner,
    )

    plane2 = (2, rows, lanes)
    cells = 2 * rows * lanes
    g = call(start_kernel, plane2, (psi, potential), flops=24 * cells)
    t, h_back = call(
        inner_kernel,
        [plane2, plane2],
        (coeffs, psi, potential, psi_in, pot_in, g),
        scalars=1,
        flops=80 * cells,
    )
    as_bands = lambda x: x.reshape(x.shape[0], bands, wide, lanes)

    def reduced(keep, send):
        near = [(i, i ^ 1) for i in range(bands)]
        far = [(i, i ^ 3) for i in range(bands)]
        came = lax.ppermute(send, "orb", near)
        return keep, came, lax.ppermute(keep[1] + came[1], "orb", far)

    places, pieces, fs, faces = [], [], [], []
    for chunk, halo in zip(chunks, halos):
        shape = halo.shape
        f = call(functools.partial(face_kernel, chunk), shape, (halo, as_bands(g)))
        fs.append(f)
        faces.append(lax.ppermute(f, "slab", face))
        pair = (2, 2) + shape[2:]
        keep, send = call(
            functools.partial(back_kernel, chunk),
            [pair, pair],
            (coeffs, halo, as_bands(h_back)),
            scalars=1,
        )
        places.append((2, chunk))
        pieces += reduced(keep, send)

    h_front = call(
        functools.partial(front_kernel, chunks),
        plane2,
        (coeffs, psi, potential, t, *fs),
        scalars=1,
        scratch=[pltpu.VMEM(plane2, jnp.float32)],
        flops=40 * cells,
    )
    for chunk, halo in zip(chunks, faces):
        pair = (2, 2) + halo.shape[2:]
        keep, send = call(
            functools.partial(last_kernel, chunk),
            [pair, pair],
            (coeffs, halo, as_bands(h_front)),
            scalars=1,
        )
        places.append((0, chunk))
        pieces += reduced(keep, send)
    return call(
        functools.partial(join_kernel, places), (planes, wide, lanes), pieces
    )


def solution(mesh):
    return jax.shard_map(
        shards,
        mesh=mesh,
        in_specs=(P("orb", "slab", None, None), P("slab", None, None), P()),
        out_specs=P("slab", "orb", None),
        check_vma=False,
    )
```

```python
import functools

import jax
import jax.numpy as jnp
from jax import lax
from jax.experimental import pallas as pl
from jax.experimental.pallas import tpu as pltpu
from jax.sharding import PartitionSpec as P

NEAR = -2.0 / 15.0
FAR = 1.0 / 120.0
BLOCK = 16


def own(q, odd):
    return jnp.where(odd == 1, 3 - q, q)


def parity():
    return lax.rem(lax.axis_index("slab"), 2)


def with_halo(ref, plane, start, count):
    rows = ref.shape[-2]
    before = pl.multiple_of(lax.rem(start + rows - 8, rows), 8)
    after = pl.multiple_of(lax.rem(start + count, rows), 8)
    return jnp.concatenate(
        [
            ref[plane, pl.ds(before, 8), :],
            ref[plane, pl.ds(start, count), :],
            ref[plane, pl.ds(after, 8), :],
        ],
        axis=0,
    )


def in_plane(ext):
    count, lanes = ext.shape[0] - 16, ext.shape[1]
    mid = ext[8 : 8 + count]
    near = ext[7 : 7 + count] + ext[9 : 9 + count]
    near = near + (pltpu.roll(mid, 1, 1) + pltpu.roll(mid, lanes - 1, 1))
    far = ext[6 : 6 + count] + ext[10 : 10 + count]
    far = far + (pltpu.roll(mid, 2, 1) + pltpu.roll(mid, lanes - 2, 1))
    return mid, near, far


def apply_s(ext, pot, near_z, far_z):
    mid, near, far = in_plane(ext)
    return mid, (
        mid * (0.2 * pot - 0.05) + NEAR * (near + near_z) + FAR * (far + far_z)
    )


def blocks(rows, body):
    def step(i, carry):
        body(pl.multiple_of(i * BLOCK, BLOCK))
        return carry

    lax.fori_loop(0, rows // BLOCK, step, 0)


def pack_kernel(chunk, psi, out):
    odd = parity()
    lo, hi = chunk
    for q in range(out.shape[0]):
        for band in range(out.shape[1]):
            out[q, band] = psi[2 * odd + q, band, lo:hi, :]


def start_kernel(psi, pot, g):
    odd = parity()

    def body(r):
        here = pl.ds(r, BLOCK)
        at = [own(q, odd) for q in range(4)]
        e0, e1 = with_halo(psi, at[0], r, BLOCK), with_halo(psi, at[1], r, BLOCK)
        p2, p3 = psi[at[2], here, :], psi[at[3], here, :]
        g[0, here, :] = apply_s(e0, pot[at[0], here, :], e1[8:-8], p2)[1]
        g[1, here, :] = apply_s(e1, pot[at[1], here, :], e0[8:-8] + p2, p3)[1]

    blocks(psi.shape[1], body)


def inner_kernel(c, psi, pot, psi_in, pot_in, g, t, h):
    odd = parity()
    at = [own(q, odd) for q in range(4)]
    base, one, two = c[0] - c[2], c[1], 2.0 * c[2]

    def first(r):
        here = pl.ds(r, BLOCK)
        e2, e3 = with_halo(psi, at[2], r, BLOCK), with_halo(psi, at[3], r, BLOCK)
        p0, p1 = psi[at[0], here, :], psi[at[1], here, :]
        p4, p5 = psi_in[at[0], here, :], psi_in[at[1], here, :]
        t[0, here, :] = apply_s(e2, pot[at[2], here, :], p1 + e3[8:-8], p0 + p4)[1]
        t[1, here, :] = apply_s(e3, pot[at[3], here, :], e2[8:-8] + p4, p1 + p5)[1]

    def second(r):
        here = pl.ds(r, BLOCK)
        e4 = with_halo(psi_in, at[0], r, BLOCK)
        e5 = with_halo(psi_in, at[1], r, BLOCK)
        p2, p3 = psi[at[2], here, :], psi[at[3], here, :]
        p6, p7 = psi_in[at[2], here, :], psi_in[at[3], here, :]
        t4 = apply_s(e4, pot_in[at[0], here, :], p3 + e5[8:-8], p2 + p6)[1]
        t5 = apply_s(e5, pot_in[at[1], here, :], e4[8:-8] + p6, p3 + p7)[1]
        g0, g1 = g[0, here, :], g[1, here, :]
        e2, e3 = with_halo(t, 0, r, BLOCK), with_halo(t, 1, r, BLOCK)
        t2, s2 = apply_s(e2, pot[at[2], here, :], g1 + e3[8:-8], g0 + t4)
        t3, s3 = apply_s(e3, pot[at[3], here, :], e2[8:-8] + t4, g1 + t5)
        h[0, here, :] = base * p2 + one * t2 + two * s2
        h[1, here, :] = base * p3 + one * t3 + two * s3

    blocks(psi.shape[1], first)
    blocks(psi.shape[1], second)


def halo_terms(halo, band, odd, rows=slice(None)):
    near, far = halo[1 - odd, band, rows, :], halo[odd, band, rows, :]
    return NEAR * near + FAR * far, FAR * near


def face_kernel(chunk, parts, halo, g, *fs):
    odd = parity()
    for (lo, hi), f in zip(parts, fs):
        in_halo = slice(lo - chunk[0], hi - chunk[0])
        for band in range(halo.shape[1]):
            d0, d1 = halo_terms(halo, band, odd, in_halo)
            f[0, band] = g[0, band, lo:hi, :] + d0
            f[1, band] = g[1, band, lo:hi, :] + d1


def square(x, bands):
    return x * x * (1.0 / bands)


def back_kernel(chunk, c, halo, h, keep, send):
    odd = parity()
    lo, hi = chunk
    two = 2.0 * c[2]
    me = lax.axis_index("orb")
    bands = halo.shape[1]

    def part(band, out, slot):
        d0, d1 = halo_terms(halo, band, odd)
        v2 = h[0, band, lo:hi, :] + two * (NEAR * d1 + FAR * d0)
        v3 = h[1, band, lo:hi, :] + (two * FAR) * d1
        out[slot, 0] = square(v2, bands)
        out[slot, 1] = square(v3, bands)

    part(me ^ 1, send, 0)
    part(me ^ 2, send, 1)
    part(me, keep, 0)
    part(me ^ 3, keep, 1)


def front_kernel(chunks, c, psi, pot, t, *rest):
    fs, h, scratch = rest[:-2], rest[-2], rest[-1]
    odd = parity()
    at = [own(q, odd) for q in range(2)]
    base, one, two = c[0] - c[2], c[1], 2.0 * c[2]
    rows = psi.shape[1]
    for (lo, hi), f in zip(chunks, fs):
        bands = f.shape[1]
        for band in range(bands):
            first_row = band * (rows // bands)
            for q in range(2):
                scratch[q, first_row + lo : first_row + hi, :] = f[q, band]

    def body(r):
        here = pl.ds(r, BLOCK)
        e0, e1 = with_halo(scratch, 0, r, BLOCK), with_halo(scratch, 1, r, BLOCK)
        t2, t3 = t[0, here, :], t[1, here, :]
        f0, s0 = apply_s(e0, pot[at[0], here, :], e1[8:-8], t2)
        f1, s1 = apply_s(e1, pot[at[1], here, :], e0[8:-8] + t2, t3)
        h[0, here, :] = base * psi[at[0], here, :] + one * f0 + two * s0
        h[1, here, :] = base * psi[at[1], here, :] + one * f1 + two * s1

    blocks(rows, body)


def last_kernel(chunk, c, halo, h, keep, send):
    lo, hi = chunk
    two = 2.0 * c[2]
    me = lax.axis_index("orb")
    bands = halo.shape[1]

    def part(band, out, slot):
        near, far = halo[0, band], halo[1, band]
        v0 = h[0, band, lo:hi, :] + two * (NEAR * near + FAR * far)
        v1 = h[1, band, lo:hi, :] + (two * FAR) * near
        out[slot, 0] = square(v0, bands)
        out[slot, 1] = square(v1, bands)

    part(me ^ 1, send, 0)
    part(me ^ 2, send, 1)
    part(me, keep, 0)
    part(me ^ 3, keep, 1)


def add_kernel(keep, came, out):
    out[...] = keep[1] + came[1]


def sum_kernel(keep, came, far, out):
    out[...] = keep[0] + came[0] + far[...]


def join_kernel(places, *refs):
    out = refs[-1]
    odd = parity()
    for (q, (lo, hi)), ref in zip(places[:-1], refs):
        for j in range(2):
            out[own(q + j, odd), lo:hi, :] = ref[j]
    (q, (lo, hi)), (keep, came, far) = places[-1], refs[-4:-1]
    for j in range(2):
        out[own(q + j, odd), lo:hi, :] = keep[0, j] + came[0, j] + far[j]


class Line:
    def __init__(self):
        self.last = []

    def __call__(self, kernel, out, args, scalars=0, scratch=(), flops=0):
        vmem = pl.BlockSpec(memory_space=pltpu.VMEM)
        smem = pl.BlockSpec(memory_space=pltpu.SMEM)
        many = isinstance(out, list)
        shapes = [jax.ShapeDtypeStruct(s, jnp.float32) for s in (out if many else [out])]
        total = sum(4 * int(x.size) for x in list(args) + shapes)
        first, last = len(args), self.last

        def body(*refs):
            kernel(*refs[:first], *refs[first + len(last) :])

        result = pl.pallas_call(
            body,
            out_shape=shapes,
            in_specs=[smem] * scalars
            + [vmem] * (first - scalars)
            + [pl.BlockSpec(memory_space=pl.ANY)] * len(last),
            out_specs=[vmem] * len(shapes),
            scratch_shapes=list(scratch),
            compiler_params=pltpu.CompilerParams(vmem_limit_bytes=40 * 2**20),
            cost_estimate=pl.CostEstimate(
                flops=flops, bytes_accessed=total, transcendentals=0
            ),
        )(*args, *last)
        self.last = [result[0]]
        return result if many else result[0]


def shards(orbitals, potential, coeffs):
    psi = orbitals[0]
    slabs, bands = lax.axis_size("slab"), lax.axis_size("orb")
    planes, rows, lanes = psi.shape
    wide = rows // bands
    half, part = wide // 2, wide // 4
    chunks = [(0, half), (half, wide)]
    cuts = [(0, half), (half, wide - part), (wide - part, wide)]
    face = [(s, (s - 1 if s % 2 == 0 else s + 1) % slabs) for s in range(slabs)]
    partner = [(s, s ^ 1) for s in range(slabs)]
    near = [(i, i ^ 1) for i in range(bands)]
    far = [(i, i ^ 3) for i in range(bands)]
    plane2 = (2, rows, lanes)
    cells = 2 * rows * lanes
    call = Line()

    def as_bands(x):
        return x.reshape(x.shape[0], bands, wide, lanes)

    def slab_shape(chunk):
        return (2, bands, chunk[1] - chunk[0], lanes)

    def pair_shape(chunk):
        return (2, 2, chunk[1] - chunk[0], lanes)

    def add_far(keep, came):
        total = call(add_kernel, keep.shape[1:], (keep, came))
        return keep, came, lax.ppermute(total, "orb", far)

    def face_of(chunk, halo, inside):
        f = call(
            functools.partial(face_kernel, chunk, inside),
            [slab_shape(cut) for cut in inside],
            (halo, as_bands(g)),
        )
        return f, [lax.ppermute(x, "slab", face) for x in f]

    def squares(kernel, chunk, halo, h):
        keep, send = call(
            functools.partial(kernel, chunk),
            [pair_shape(chunk)] * 2,
            (coeffs, halo, as_bands(h)),
            scalars=1,
        )
        return keep, lax.ppermute(send, "orb", near)

    psi_in = lax.ppermute(psi, "slab", partner)
    pot_in = lax.ppermute(potential, "slab", partner)
    halos = []
    for chunk in chunks:
        piece = call(
            functools.partial(pack_kernel, chunk), slab_shape(chunk), (as_bands(psi),)
        )
        halos.append(lax.ppermute(piece, "slab", face))
    g = call(start_kernel, plane2, (psi, potential), flops=24 * cells)
    t, h_back = call(
        inner_kernel,
        [plane2, plane2],
        (coeffs, psi, potential, psi_in, pot_in, g),
        scalars=1,
        flops=80 * cells,
    )

    def summed(keep, came, from_far):
        return call(sum_kernel, from_far.shape, (keep, came, from_far))

    cut_a, cut_b, cut_c = cuts
    f0, (face_a,) = face_of(chunks[0], halos[0], [cut_a])
    back0 = squares(back_kernel, chunks[0], halos[0], h_back)
    back0 = add_far(*back0)
    f1, (face_b, face_c) = face_of(chunks[1], halos[1], [cut_b, cut_c])
    back1 = squares(back_kernel, chunks[1], halos[1], h_back)
    h_front = call(
        functools.partial(front_kernel, cuts),
        plane2,
        (coeffs, psi, potential, t, *f0, *f1),
        scalars=1,
        scratch=[pltpu.VMEM(plane2, jnp.float32)],
        flops=40 * cells,
    )
    back0 = summed(*back0)
    back1 = add_far(*back1)
    front_a = squares(last_kernel, cut_a, face_a, h_front)
    front_b = squares(last_kernel, cut_b, face_b, h_front)
    back1 = summed(*back1)
    front_a = add_far(*front_a)
    front_c = squares(last_kernel, cut_c, face_c, h_front)
    front_b = add_far(*front_b)
    front_a = summed(*front_a)
    front_c = add_far(*front_c)
    front_b = summed(*front_b)
    places = [(2, chunk) for chunk in chunks] + [(0, cut) for cut in cuts]
    return call(
        functools.partial(join_kernel, places),
        (planes, wide, lanes),
        (back0, back1, front_a, front_b, *front_c),
    )


def solution(mesh):
    return jax.shard_map(
        shards,
        mesh=mesh,
        in_specs=(P("orb", "slab", None, None), P("slab", None, None), P()),
        out_specs=P("slab", "orb", None),
        check_vma=False,
    )
```

```python
import functools

import jax
import jax.numpy as jnp
from jax import lax
from jax.experimental import pallas as pl
from jax.experimental.pallas import tpu as pltpu
from jax.sharding import PartitionSpec as P

NEAR = -2.0 / 15.0
FAR = 1.0 / 120.0
BLOCK = 16


def own(q, odd):
    return jnp.where(odd == 1, 3 - q, q)


def parity():
    return lax.rem(lax.axis_index("slab"), 2)


def with_halo(ref, plane, start, count):
    rows = ref.shape[-2]
    before = pl.multiple_of(lax.rem(start + rows - 8, rows), 8)
    after = pl.multiple_of(lax.rem(start + count, rows), 8)
    return jnp.concatenate(
        [
            ref[plane, pl.ds(before, 8), :],
            ref[plane, pl.ds(start, count), :],
            ref[plane, pl.ds(after, 8), :],
        ],
        axis=0,
    )


def in_plane(ext):
    count, lanes = ext.shape[0] - 16, ext.shape[1]
    mid = ext[8 : 8 + count]
    near = ext[7 : 7 + count] + ext[9 : 9 + count]
    near = near + (pltpu.roll(mid, 1, 1) + pltpu.roll(mid, lanes - 1, 1))
    far = ext[6 : 6 + count] + ext[10 : 10 + count]
    far = far + (pltpu.roll(mid, 2, 1) + pltpu.roll(mid, lanes - 2, 1))
    return mid, near, far


def apply_s(ext, pot, near_z, far_z):
    mid, near, far = in_plane(ext)
    return mid, (
        mid * (0.2 * pot - 0.05) + NEAR * (near + near_z) + FAR * (far + far_z)
    )


def blocks(rows, body):
    def step(i, carry):
        body(pl.multiple_of(i * BLOCK, BLOCK))
        return carry

    lax.fori_loop(0, rows // BLOCK, step, 0)


def pack_kernel(chunk, psi, out, sem):
    lo, hi = chunk
    planes = pl.ds(2 * parity(), out.shape[0])
    copy = pltpu.make_async_copy(psi.at[planes, :, pl.ds(lo, hi - lo), :], out, sem)
    copy.start()
    copy.wait()


def start_kernel(psi, pot, g):
    odd = parity()

    def body(r):
        here = pl.ds(r, BLOCK)
        at = [own(q, odd) for q in range(4)]
        e0, e1 = with_halo(psi, at[0], r, BLOCK), with_halo(psi, at[1], r, BLOCK)
        p2, p3 = psi[at[2], here, :], psi[at[3], here, :]
        g[0, here, :] = apply_s(e0, pot[at[0], here, :], e1[8:-8], p2)[1]
        g[1, here, :] = apply_s(e1, pot[at[1], here, :], e0[8:-8] + p2, p3)[1]

    blocks(psi.shape[1], body)


def inner_kernel(c, psi, pot, psi_in, pot_in, g, t, h, row):
    odd = parity()
    at = [own(q, odd) for q in range(4)]
    base, one, two = c[0] - c[2], c[1], 2.0 * c[2]

    def first(r):
        here = pl.ds(r, BLOCK)
        e2, e3 = with_halo(psi, at[2], r, BLOCK), with_halo(psi, at[3], r, BLOCK)
        p0, p1 = psi[at[0], here, :], psi[at[1], here, :]
        p4, p5 = psi_in[at[0], here, :], psi_in[at[1], here, :]
        t[0, here, :] = apply_s(e2, pot[at[2], here, :], p1 + e3[8:-8], p0 + p4)[1]
        t[1, here, :] = apply_s(e3, pot[at[3], here, :], e2[8:-8] + p4, p1 + p5)[1]

    def second(r):
        here = pl.ds(r, BLOCK)
        e4 = with_halo(psi_in, at[0], r, BLOCK)
        e5 = with_halo(psi_in, at[1], r, BLOCK)
        p2, p3 = psi[at[2], here, :], psi[at[3], here, :]
        p6, p7 = psi_in[at[2], here, :], psi_in[at[3], here, :]
        t4 = apply_s(e4, pot_in[at[0], here, :], p3 + e5[8:-8], p2 + p6)[1]
        t5 = apply_s(e5, pot_in[at[1], here, :], e4[8:-8] + p6, p3 + p7)[1]
        g0, g1 = g[0, here, :], g[1, here, :]
        e2, e3 = with_halo(t, 0, r, BLOCK), with_halo(t, 1, r, BLOCK)
        t2, s2 = apply_s(e2, pot[at[2], here, :], g1 + e3[8:-8], g0 + t4)
        t3, s3 = apply_s(e3, pot[at[3], here, :], e2[8:-8] + t4, g1 + t5)
        h[0, here, :] = base * p2 + one * t2 + two * s2
        h[1, here, :] = base * p3 + one * t3 + two * s3

    row[...] = jnp.full(row.shape, two)
    blocks(psi.shape[1], first)
    blocks(psi.shape[1], second)


def halo_terms(halo, band, odd, rows=slice(None)):
    near, far = halo[1 - odd, band, rows, :], halo[odd, band, rows, :]
    return NEAR * near + FAR * far, FAR * near


def square(x, bands):
    return x * x * (1.0 / bands)


def face_kernel(chunk, parts, halo, g, *fs):
    odd = parity()
    lo, hi = chunk
    for (first, last), f in zip(parts, fs):
        in_halo = slice(first - lo, last - lo)
        for band in range(halo.shape[1]):
            d0, d1 = halo_terms(halo, band, odd, in_halo)
            f[0, band] = g[0, band, first:last, :] + d0
            f[1, band] = g[1, band, first:last, :] + d1


def back_kernel(chunk, row, halo, h, keep, send):
    odd = parity()
    lo, hi = chunk
    two = row[0:1, :]
    me = lax.axis_index("orb")
    bands = halo.shape[1]

    def part(band, out, slot):
        d0, d1 = halo_terms(halo, band, odd)
        v2 = h[0, band, lo:hi, :] + two * (NEAR * d1 + FAR * d0)
        v3 = h[1, band, lo:hi, :] + two * (FAR * d1)
        out[slot, 0] = square(v2, bands)
        out[slot, 1] = square(v3, bands)

    part(me ^ 1, send, 0)
    part(me ^ 2, send, 1)
    part(me, keep, 0)
    part(me ^ 3, keep, 1)


def front_kernel(chunks, c, psi, pot, t, *rest):
    fs, h, scratch = rest[:-2], rest[-2], rest[-1]
    odd = parity()
    at = [own(q, odd) for q in range(2)]
    base, one, two = c[0] - c[2], c[1], 2.0 * c[2]
    rows = psi.shape[1]
    for (lo, hi), f in zip(chunks, fs):
        bands = f.shape[1]
        for band in range(bands):
            first_row = band * (rows // bands)
            for q in range(2):
                scratch[q, first_row + lo : first_row + hi, :] = f[q, band]

    def body(r):
        here = pl.ds(r, BLOCK)
        e0, e1 = with_halo(scratch, 0, r, BLOCK), with_halo(scratch, 1, r, BLOCK)
        t2, t3 = t[0, here, :], t[1, here, :]
        f0, s0 = apply_s(e0, pot[at[0], here, :], e1[8:-8], t2)
        f1, s1 = apply_s(e1, pot[at[1], here, :], e0[8:-8] + t2, t3)
        h[0, here, :] = base * psi[at[0], here, :] + one * f0 + two * s0
        h[1, here, :] = base * psi[at[1], here, :] + one * f1 + two * s1

    blocks(rows, body)


def last_kernel(chunk, row, halo, h, keep, send):
    lo, hi = chunk
    two = row[0:1, :]
    me = lax.axis_index("orb")
    bands = halo.shape[1]

    def part(band, out, slot):
        near, far = halo[0, band], halo[1, band]
        v0 = h[0, band, lo:hi, :] + two * (NEAR * near + FAR * far)
        v1 = h[1, band, lo:hi, :] + two * (FAR * near)
        out[slot, 0] = square(v0, bands)
        out[slot, 1] = square(v1, bands)

    part(me ^ 1, send, 0)
    part(me ^ 2, send, 1)
    part(me, keep, 0)
    part(me ^ 3, keep, 1)


def add_kernel(keep, came, out):
    out[...] = keep[1] + came[1]


def sum_kernel(keep, came, far, out):
    out[...] = keep[0] + came[0] + far[...]


def join_kernel(places, *refs):
    out = refs[-1]
    odd = parity()
    for (q, (lo, hi)), ref in zip(places[:-1], refs):
        for j in range(2):
            out[own(q + j, odd), lo:hi, :] = ref[j]
    (q, (lo, hi)), (keep, came, far) = places[-1], refs[-4:-1]
    for j in range(2):
        out[own(q + j, odd), lo:hi, :] = keep[0, j] + came[0, j] + far[j]


class Line:
    def __init__(self):
        self.last = []

    def __call__(self, kernel, out, args, scalars=0, scratch=(), flops=0, hbm=False):
        vmem = pl.BlockSpec(memory_space=pltpu.VMEM)
        smem = pl.BlockSpec(memory_space=pltpu.SMEM)
        many = isinstance(out, list)
        shapes = [jax.ShapeDtypeStruct(s, jnp.float32) for s in (out if many else [out])]
        total = sum(4 * int(x.size) for x in list(args) + shapes)
        first, last = len(args), self.last

        def body(*refs):
            kernel(*refs[:first], *refs[first + len(last) :])

        result = pl.pallas_call(
            body,
            out_shape=shapes,
            in_specs=[smem] * scalars
            + [pl.BlockSpec(memory_space=pltpu.HBM) if hbm else vmem] * (first - scalars)
            + [pl.BlockSpec(memory_space=pl.ANY)] * len(last),
            out_specs=[vmem] * len(shapes),
            scratch_shapes=list(scratch),
            compiler_params=pltpu.CompilerParams(vmem_limit_bytes=40 * 2**20),
            cost_estimate=pl.CostEstimate(
                flops=flops, bytes_accessed=total, transcendentals=0
            ),
        )(*args, *last)
        self.last = [result[0]]
        return result if many else result[0]


def shards(orbitals, potential, coeffs):
    psi = orbitals[0]
    slabs, bands = lax.axis_size("slab"), lax.axis_size("orb")
    planes, rows, lanes = psi.shape
    wide = rows // bands
    half, part = wide // 2, wide // 4
    chunks = [(0, half), (half, wide)]
    cuts = [(0, half), (half, wide - part), (wide - part, wide)]
    face = [(s, (s - 1 if s % 2 == 0 else s + 1) % slabs) for s in range(slabs)]
    partner = [(s, s ^ 1) for s in range(slabs)]
    near = [(i, i ^ 1) for i in range(bands)]
    far = [(i, i ^ 3) for i in range(bands)]
    plane2 = (2, rows, lanes)
    cells = 2 * rows * lanes
    call = Line()

    def as_bands(x):
        return x.reshape(x.shape[0], bands, wide, lanes)

    def slab_shape(chunk):
        return (2, bands, chunk[1] - chunk[0], lanes)

    def pair_shape(chunk):
        return (2, 2, chunk[1] - chunk[0], lanes)

    def add_far(keep, came):
        total = call(add_kernel, keep.shape[1:], (keep, came))
        return keep, came, lax.ppermute(total, "orb", far)

    def squares(cut, halo):
        keep, send = call(
            functools.partial(last_kernel, cut),
            [pair_shape(cut)] * 2,
            (row, halo, as_bands(h_front)),
        )
        return keep, lax.ppermute(send, "orb", near)

    def back_squares(chunk, halo):
        keep, send = call(
            functools.partial(back_kernel, chunk),
            [pair_shape(chunk)] * 2,
            (row, halo, as_bands(h_back)),
        )
        return keep, lax.ppermute(send, "orb", near)

    def faces(chunk, halo, parts):
        fs = call(
            functools.partial(face_kernel, chunk, parts),
            [slab_shape(cut) for cut in parts],
            (halo, as_bands(g)),
        )
        return fs, [lax.ppermute(x, "slab", face) for x in fs]

    psi_in = lax.ppermute(psi, "slab", partner)
    pot_in = lax.ppermute(potential, "slab", partner)
    halos = []
    for chunk in chunks:
        piece = call(
            functools.partial(pack_kernel, chunk),
            slab_shape(chunk),
            (as_bands(psi),),
            scratch=[pltpu.SemaphoreType.DMA],
            hbm=True,
        )
        halos.append(lax.ppermute(piece, "slab", face))
    g = call(start_kernel, plane2, (psi, potential), flops=24 * cells)
    t, h_back, row = call(
        inner_kernel,
        [plane2, plane2, (8, lanes)],
        (coeffs, psi, potential, psi_in, pot_in, g),
        scalars=1,
        flops=80 * cells,
    )

    def summed(keep, came, from_far):
        return call(sum_kernel, from_far.shape, (keep, came, from_far))

    cut_a, cut_b, cut_c = cuts
    f0, (face_a,) = faces(chunks[0], halos[0], [cut_a])
    back0 = back_squares(chunks[0], halos[0])
    back0 = add_far(*back0)
    f1, (face_b, face_c) = faces(chunks[1], halos[1], [cut_b, cut_c])
    h_front = call(
        functools.partial(front_kernel, cuts),
        plane2,
        (coeffs, psi, potential, t, *f0, *f1),
        scalars=1,
        scratch=[pltpu.VMEM(plane2, jnp.float32)],
        flops=40 * cells,
    )
    back0 = summed(*back0)
    back1 = back_squares(chunks[1], halos[1])
    back1 = add_far(*back1)
    front_a = squares(cut_a, face_a)
    back1 = summed(*back1)
    front_b = squares(cut_b, face_b)
    front_a = add_far(*front_a)
    front_c = squares(cut_c, face_c)
    front_b = add_far(*front_b)
    front_a = summed(*front_a)
    front_c = add_far(*front_c)
    front_b = summed(*front_b)
    places = [(2, chunk) for chunk in chunks] + [(0, cut) for cut in cuts]
    return call(
        functools.partial(join_kernel, places),
        (planes, wide, lanes),
        (back0, back1, front_a, front_b, *front_c),
    )


def solution(mesh):
    return jax.shard_map(
        shards,
        mesh=mesh,
        in_specs=(P("orb", "slab", None, None), P("slab", None, None), P()),
        out_specs=P("slab", "orb", None),
        check_vma=False,
    )
```

```python
import functools

import jax
import jax.numpy as jnp
from jax import lax
from jax.experimental import pallas as pl
from jax.experimental.pallas import tpu as pltpu
from jax.sharding import PartitionSpec as P

NEAR = -2.0 / 15.0
FAR = 1.0 / 120.0
BLOCK = 16


def own(q, odd):
    return jnp.where(odd == 1, 3 - q, q)


def parity():
    return lax.rem(lax.axis_index("slab"), 2)


def with_halo(ref, plane, start, count):
    rows = ref.shape[-2]
    before = pl.multiple_of(lax.rem(start + rows - 8, rows), 8)
    after = pl.multiple_of(lax.rem(start + count, rows), 8)
    return jnp.concatenate(
        [
            ref[plane, pl.ds(before, 8), :],
            ref[plane, pl.ds(start, count), :],
            ref[plane, pl.ds(after, 8), :],
        ],
        axis=0,
    )


def in_plane(ext):
    count, lanes = ext.shape[0] - 16, ext.shape[1]
    mid = ext[8 : 8 + count]
    near = ext[7 : 7 + count] + ext[9 : 9 + count]
    near = near + (pltpu.roll(mid, 1, 1) + pltpu.roll(mid, lanes - 1, 1))
    far = ext[6 : 6 + count] + ext[10 : 10 + count]
    far = far + (pltpu.roll(mid, 2, 1) + pltpu.roll(mid, lanes - 2, 1))
    return mid, near, far


def apply_s(ext, pot, near_z, far_z):
    mid, near, far = in_plane(ext)
    return mid, (
        mid * (0.2 * pot - 0.05) + NEAR * (near + near_z) + FAR * (far + far_z)
    )


def blocks(rows, body):
    def step(i, carry):
        body(pl.multiple_of(i * BLOCK, BLOCK))
        return carry

    lax.fori_loop(0, rows // BLOCK, step, 0)


def pack_kernel(chunk, psi, out, sem):
    lo, hi = chunk
    planes = pl.ds(2 * parity(), out.shape[0])
    copy = pltpu.make_async_copy(psi.at[planes, :, pl.ds(lo, hi - lo), :], out, sem)
    copy.start()
    copy.wait()


def start_kernel(psi, pot, g):
    odd = parity()

    def body(r):
        here = pl.ds(r, BLOCK)
        at = [own(q, odd) for q in range(4)]
        e0, e1 = with_halo(psi, at[0], r, BLOCK), with_halo(psi, at[1], r, BLOCK)
        p2, p3 = psi[at[2], here, :], psi[at[3], here, :]
        g[0, here, :] = apply_s(e0, pot[at[0], here, :], e1[8:-8], p2)[1]
        g[1, here, :] = apply_s(e1, pot[at[1], here, :], e0[8:-8] + p2, p3)[1]

    blocks(psi.shape[1], body)


def inner_kernel(c, psi, pot, psi_in, pot_in, g, t, h, row):
    odd = parity()
    at = [own(q, odd) for q in range(4)]
    base, one, two = c[0] - c[2], c[1], 2.0 * c[2]

    def first(r):
        here = pl.ds(r, BLOCK)
        e2, e3 = with_halo(psi, at[2], r, BLOCK), with_halo(psi, at[3], r, BLOCK)
        p0, p1 = psi[at[0], here, :], psi[at[1], here, :]
        p4, p5 = psi_in[at[0], here, :], psi_in[at[1], here, :]
        t[0, here, :] = apply_s(e2, pot[at[2], here, :], p1 + e3[8:-8], p0 + p4)[1]
        t[1, here, :] = apply_s(e3, pot[at[3], here, :], e2[8:-8] + p4, p1 + p5)[1]

    def second(r):
        here = pl.ds(r, BLOCK)
        e4 = with_halo(psi_in, at[0], r, BLOCK)
        e5 = with_halo(psi_in, at[1], r, BLOCK)
        p2, p3 = psi[at[2], here, :], psi[at[3], here, :]
        p6, p7 = psi_in[at[2], here, :], psi_in[at[3], here, :]
        t4 = apply_s(e4, pot_in[at[0], here, :], p3 + e5[8:-8], p2 + p6)[1]
        t5 = apply_s(e5, pot_in[at[1], here, :], e4[8:-8] + p6, p3 + p7)[1]
        g0, g1 = g[0, here, :], g[1, here, :]
        e2, e3 = with_halo(t, 0, r, BLOCK), with_halo(t, 1, r, BLOCK)
        t2, s2 = apply_s(e2, pot[at[2], here, :], g1 + e3[8:-8], g0 + t4)
        t3, s3 = apply_s(e3, pot[at[3], here, :], e2[8:-8] + t4, g1 + t5)
        h[0, here, :] = base * p2 + one * t2 + two * s2
        h[1, here, :] = base * p3 + one * t3 + two * s3

    row[...] = jnp.full(row.shape, two)
    blocks(psi.shape[1], first)
    blocks(psi.shape[1], second)


def halo_terms(halo, band, odd, rows=slice(None)):
    near, far = halo[1 - odd, band, rows, :], halo[odd, band, rows, :]
    return NEAR * near + FAR * far, FAR * near


def square(x, bands):
    return x * x * (1.0 / bands)


def face_kernel(chunk, parts, halo, g, *fs):
    odd = parity()
    lo, hi = chunk
    for (first, last), f in zip(parts, fs):
        in_halo = slice(first - lo, last - lo)
        for band in range(halo.shape[1]):
            d0, d1 = halo_terms(halo, band, odd, in_halo)
            f[0, band] = g[0, band, first:last, :] + d0
            f[1, band] = g[1, band, first:last, :] + d1


def back_kernel(chunk, row, halo, h, keep, send):
    odd = parity()
    lo, hi = chunk
    two = row[0:1, :]
    me = lax.axis_index("orb")
    bands = halo.shape[1]

    def part(band, out, slot):
        d0, d1 = halo_terms(halo, band, odd)
        v2 = h[0, band, lo:hi, :] + two * (NEAR * d1 + FAR * d0)
        v3 = h[1, band, lo:hi, :] + two * (FAR * d1)
        out[slot, 0] = square(v2, bands)
        out[slot, 1] = square(v3, bands)

    part(me ^ 1, send, 0)
    part(me ^ 2, send, 1)
    part(me, keep, 0)
    part(me ^ 3, keep, 1)


def back_all_kernel(chunk, row, halo, h, out):
    odd = parity()
    lo, hi = chunk
    two = row[0:1, :]
    bands = halo.shape[1]
    for band in range(bands):
        d0, d1 = halo_terms(halo, band, odd)
        v2 = h[0, band, lo:hi, :] + two * (NEAR * d1 + FAR * d0)
        v3 = h[1, band, lo:hi, :] + two * (FAR * d1)
        out[band, 0] = square(v2, bands)
        out[band, 1] = square(v3, bands)


def sum_all_kernel(came, out):
    total = came[0]
    for band in range(1, came.shape[0]):
        total = total + came[band]
    out[...] = total


def front_kernel(chunks, c, psi, pot, t, *rest):
    fs, h, scratch = rest[:-2], rest[-2], rest[-1]
    odd = parity()
    at = [own(q, odd) for q in range(2)]
    base, one, two = c[0] - c[2], c[1], 2.0 * c[2]
    rows = psi.shape[1]
    for (lo, hi), f in zip(chunks, fs):
        bands = f.shape[1]
        for band in range(bands):
            first_row = band * (rows // bands)
            for q in range(2):
                scratch[q, first_row + lo : first_row + hi, :] = f[q, band]

    def body(r):
        here = pl.ds(r, BLOCK)
        e0, e1 = with_halo(scratch, 0, r, BLOCK), with_halo(scratch, 1, r, BLOCK)
        t2, t3 = t[0, here, :], t[1, here, :]
        f0, s0 = apply_s(e0, pot[at[0], here, :], e1[8:-8], t2)
        f1, s1 = apply_s(e1, pot[at[1], here, :], e0[8:-8] + t2, t3)
        h[0, here, :] = base * psi[at[0], here, :] + one * f0 + two * s0
        h[1, here, :] = base * psi[at[1], here, :] + one * f1 + two * s1

    blocks(rows, body)


def last_kernel(chunk, row, halo, h, keep, send):
    lo, hi = chunk
    two = row[0:1, :]
    me = lax.axis_index("orb")
    bands = halo.shape[1]

    def part(band, out, slot):
        near, far = halo[0, band], halo[1, band]
        v0 = h[0, band, lo:hi, :] + two * (NEAR * near + FAR * far)
        v1 = h[1, band, lo:hi, :] + two * (FAR * near)
        out[slot, 0] = square(v0, bands)
        out[slot, 1] = square(v1, bands)

    part(me ^ 1, send, 0)
    part(me ^ 2, send, 1)
    part(me, keep, 0)
    part(me ^ 3, keep, 1)


def add_kernel(keep, came, out):
    out[...] = keep[1] + came[1]


def sum_kernel(keep, came, far, out):
    out[...] = keep[0] + came[0] + far[...]


def join_kernel(places, *refs):
    out = refs[-1]
    odd = parity()
    for (q, (lo, hi)), ref in zip(places[:-1], refs):
        for j in range(2):
            out[own(q + j, odd), lo:hi, :] = ref[j]
    (q, (lo, hi)), (keep, came, far) = places[-1], refs[-4:-1]
    for j in range(2):
        out[own(q + j, odd), lo:hi, :] = keep[0, j] + came[0, j] + far[j]


class Line:
    def __init__(self):
        self.last = []

    def __call__(self, kernel, out, args, scalars=0, scratch=(), flops=0, hbm=False):
        vmem = pl.BlockSpec(memory_space=pltpu.VMEM)
        smem = pl.BlockSpec(memory_space=pltpu.SMEM)
        many = isinstance(out, list)
        shapes = [jax.ShapeDtypeStruct(s, jnp.float32) for s in (out if many else [out])]
        total = sum(4 * int(x.size) for x in list(args) + shapes)
        first, last = len(args), self.last

        def body(*refs):
            kernel(*refs[:first], *refs[first + len(last) :])

        result = pl.pallas_call(
            body,
            out_shape=shapes,
            in_specs=[smem] * scalars
            + [pl.BlockSpec(memory_space=pltpu.HBM) if hbm else vmem] * (first - scalars)
            + [pl.BlockSpec(memory_space=pl.ANY)] * len(last),
            out_specs=[vmem] * len(shapes),
            scratch_shapes=list(scratch),
            compiler_params=pltpu.CompilerParams(vmem_limit_bytes=40 * 2**20),
            cost_estimate=pl.CostEstimate(
                flops=flops, bytes_accessed=total, transcendentals=0
            ),
        )(*args, *last)
        self.last = [result[0]]
        return result if many else result[0]


def shards(orbitals, potential, coeffs):
    psi = orbitals[0]
    slabs, bands = lax.axis_size("slab"), lax.axis_size("orb")
    planes, rows, lanes = psi.shape
    wide = rows // bands
    half, part = wide // 2, wide // 4
    chunks = [(0, half), (half, wide)]
    cuts = [(0, half), (half, wide - part), (wide - part, wide)]
    face = [(s, (s - 1 if s % 2 == 0 else s + 1) % slabs) for s in range(slabs)]
    partner = [(s, s ^ 1) for s in range(slabs)]
    near = [(i, i ^ 1) for i in range(bands)]
    far = [(i, i ^ 3) for i in range(bands)]
    plane2 = (2, rows, lanes)
    cells = 2 * rows * lanes
    call = Line()

    def as_bands(x):
        return x.reshape(x.shape[0], bands, wide, lanes)

    def slab_shape(chunk):
        return (2, bands, chunk[1] - chunk[0], lanes)

    def pair_shape(chunk):
        return (2, 2, chunk[1] - chunk[0], lanes)

    def add_far(keep, came):
        total = call(add_kernel, keep.shape[1:], (keep, came))
        return keep, came, lax.ppermute(total, "orb", far)

    def squares(cut, halo):
        keep, send = call(
            functools.partial(last_kernel, cut),
            [pair_shape(cut)] * 2,
            (row, halo, as_bands(h_front)),
        )
        return keep, lax.ppermute(send, "orb", near)

    def back_squares(chunk, halo):
        out = call(
            functools.partial(back_all_kernel, chunk),
            (bands,) + pair_shape(chunk)[1:],
            (row, halo, as_bands(h_back)),
        )
        return lax.all_to_all(out, "orb", 0, 0, tiled=True)

    def sum_all(came):
        return call(sum_all_kernel, came.shape[1:], (came,))

    def faces(chunk, halo, parts):
        fs = call(
            functools.partial(face_kernel, chunk, parts),
            [slab_shape(cut) for cut in parts],
            (halo, as_bands(g)),
        )
        return fs, [lax.ppermute(x, "slab", face) for x in fs]

    psi_in = lax.ppermute(psi, "slab", partner)
    pot_in = lax.ppermute(potential, "slab", partner)
    halos = []
    for chunk in chunks:
        piece = call(
            functools.partial(pack_kernel, chunk),
            slab_shape(chunk),
            (as_bands(psi),),
            scratch=[pltpu.SemaphoreType.DMA],
            hbm=True,
        )
        halos.append(lax.ppermute(piece, "slab", face))
    g = call(start_kernel, plane2, (psi, potential), flops=24 * cells)
    t, h_back, row = call(
        inner_kernel,
        [plane2, plane2, (8, lanes)],
        (coeffs, psi, potential, psi_in, pot_in, g),
        scalars=1,
        flops=80 * cells,
    )

    def summed(keep, came, from_far):
        return call(sum_kernel, from_far.shape, (keep, came, from_far))

    cut_a, cut_b, cut_c = cuts
    f0, (face_a,) = faces(chunks[0], halos[0], [cut_a])
    back0 = back_squares(chunks[0], halos[0])
    f1, (face_b, face_c) = faces(chunks[1], halos[1], [cut_b, cut_c])
    back1 = back_squares(chunks[1], halos[1])
    h_front = call(
        functools.partial(front_kernel, cuts),
        plane2,
        (coeffs, psi, potential, t, *f0, *f1),
        scalars=1,
        scratch=[pltpu.VMEM(plane2, jnp.float32)],
        flops=40 * cells,
    )
    back0 = sum_all(back0)
    front_a = squares(cut_a, face_a)
    front_b = squares(cut_b, face_b)
    back1 = sum_all(back1)
    front_a = add_far(*front_a)
    front_c = squares(cut_c, face_c)
    front_b = add_far(*front_b)
    front_a = summed(*front_a)
    front_c = add_far(*front_c)
    front_b = summed(*front_b)
    places = [(2, chunk) for chunk in chunks] + [(0, cut) for cut in cuts]
    return call(
        functools.partial(join_kernel, places),
        (planes, wide, lanes),
        (back0, back1, front_a, front_b, *front_c),
    )


def solution(mesh):
    return jax.shard_map(
        shards,
        mesh=mesh,
        in_specs=(P("orb", "slab", None, None), P("slab", None, None), P()),
        out_specs=P("slab", "orb", None),
        check_vma=False,
    )
```

```python
import functools

import jax
import jax.numpy as jnp
from jax import lax
from jax.experimental import pallas as pl
from jax.experimental.pallas import tpu as pltpu
from jax.sharding import PartitionSpec as P

NEAR = -2.0 / 15.0
FAR = 1.0 / 120.0
BLOCK = 16


def own(q, odd):
    return jnp.where(odd == 1, 3 - q, q)


def parity():
    return lax.rem(lax.axis_index("slab"), 2)


def with_halo(ref, plane, start, count):
    rows = ref.shape[-2]
    before = pl.multiple_of(lax.rem(start + rows - 8, rows), 8)
    after = pl.multiple_of(lax.rem(start + count, rows), 8)
    return jnp.concatenate(
        [
            ref[plane, pl.ds(before, 8), :],
            ref[plane, pl.ds(start, count), :],
            ref[plane, pl.ds(after, 8), :],
        ],
        axis=0,
    )


def in_plane(ext):
    count, lanes = ext.shape[0] - 16, ext.shape[1]
    mid = ext[8 : 8 + count]
    near = ext[7 : 7 + count] + ext[9 : 9 + count]
    near = near + (pltpu.roll(mid, 1, 1) + pltpu.roll(mid, lanes - 1, 1))
    far = ext[6 : 6 + count] + ext[10 : 10 + count]
    far = far + (pltpu.roll(mid, 2, 1) + pltpu.roll(mid, lanes - 2, 1))
    return mid, near, far


def apply_s(ext, pot, near_z, far_z):
    mid, near, far = in_plane(ext)
    return mid, (
        mid * (0.2 * pot - 0.05) + NEAR * (near + near_z) + FAR * (far + far_z)
    )


def blocks(rows, body):
    def step(i, carry):
        body(pl.multiple_of(i * BLOCK, BLOCK))
        return carry

    lax.fori_loop(0, rows // BLOCK, step, 0)


def pack_kernel(chunk, psi, out, sem):
    lo, hi = chunk
    planes = pl.ds(2 * parity(), out.shape[0])
    copy = pltpu.make_async_copy(psi.at[planes, :, pl.ds(lo, hi - lo), :], out, sem)
    copy.start()
    copy.wait()


def start_kernel(psi, pot, g):
    odd = parity()

    def body(r):
        here = pl.ds(r, BLOCK)
        at = [own(q, odd) for q in range(4)]
        e0, e1 = with_halo(psi, at[0], r, BLOCK), with_halo(psi, at[1], r, BLOCK)
        p2, p3 = psi[at[2], here, :], psi[at[3], here, :]
        g[0, here, :] = apply_s(e0, pot[at[0], here, :], e1[8:-8], p2)[1]
        g[1, here, :] = apply_s(e1, pot[at[1], here, :], e0[8:-8] + p2, p3)[1]

    blocks(psi.shape[1], body)


def inner_kernel(c, psi, pot, psi_in, pot_in, g, t, h, row):
    odd = parity()
    at = [own(q, odd) for q in range(4)]
    base, one, two = c[0] - c[2], c[1], 2.0 * c[2]

    def first(r):
        here = pl.ds(r, BLOCK)
        e2, e3 = with_halo(psi, at[2], r, BLOCK), with_halo(psi, at[3], r, BLOCK)
        p0, p1 = psi[at[0], here, :], psi[at[1], here, :]
        p4, p5 = psi_in[at[0], here, :], psi_in[at[1], here, :]
        t[0, here, :] = apply_s(e2, pot[at[2], here, :], p1 + e3[8:-8], p0 + p4)[1]
        t[1, here, :] = apply_s(e3, pot[at[3], here, :], e2[8:-8] + p4, p1 + p5)[1]

    def second(r):
        here = pl.ds(r, BLOCK)
        e4 = with_halo(psi_in, at[0], r, BLOCK)
        e5 = with_halo(psi_in, at[1], r, BLOCK)
        p2, p3 = psi[at[2], here, :], psi[at[3], here, :]
        p6, p7 = psi_in[at[2], here, :], psi_in[at[3], here, :]
        t4 = apply_s(e4, pot_in[at[0], here, :], p3 + e5[8:-8], p2 + p6)[1]
        t5 = apply_s(e5, pot_in[at[1], here, :], e4[8:-8] + p6, p3 + p7)[1]
        g0, g1 = g[0, here, :], g[1, here, :]
        e2, e3 = with_halo(t, 0, r, BLOCK), with_halo(t, 1, r, BLOCK)
        t2, s2 = apply_s(e2, pot[at[2], here, :], g1 + e3[8:-8], g0 + t4)
        t3, s3 = apply_s(e3, pot[at[3], here, :], e2[8:-8] + t4, g1 + t5)
        h[0, here, :] = base * p2 + one * t2 + two * s2
        h[1, here, :] = base * p3 + one * t3 + two * s3

    row[...] = jnp.full(row.shape, two)
    blocks(psi.shape[1], first)
    blocks(psi.shape[1], second)


def halo_terms(halo, band, odd, rows=slice(None)):
    near, far = halo[1 - odd, band, rows, :], halo[odd, band, rows, :]
    return NEAR * near + FAR * far, FAR * near


def square(x, bands):
    return x * x * (1.0 / bands)


def face_kernel(chunk, parts, halo, g, *fs):
    odd = parity()
    lo, hi = chunk
    for (first, last), f in zip(parts, fs):
        in_halo = slice(first - lo, last - lo)
        for band in range(halo.shape[1]):
            d0, d1 = halo_terms(halo, band, odd, in_halo)
            f[0, band] = g[0, band, first:last, :] + d0
            f[1, band] = g[1, band, first:last, :] + d1


def back_kernel(chunk, row, halo, h, keep, send):
    odd = parity()
    lo, hi = chunk
    two = row[0:1, :]
    me = lax.axis_index("orb")
    bands = halo.shape[1]

    def part(band, out, slot):
        d0, d1 = halo_terms(halo, band, odd)
        v2 = h[0, band, lo:hi, :] + two * (NEAR * d1 + FAR * d0)
        v3 = h[1, band, lo:hi, :] + two * (FAR * d1)
        out[slot, 0] = square(v2, bands)
        out[slot, 1] = square(v3, bands)

    part(me ^ 1, send, 0)
    part(me ^ 2, send, 1)
    part(me, keep, 0)
    part(me ^ 3, keep, 1)


def front_kernel(chunks, c, psi, pot, t, *rest):
    fs, h, scratch = rest[:-2], rest[-2], rest[-1]
    odd = parity()
    at = [own(q, odd) for q in range(2)]
    base, one, two = c[0] - c[2], c[1], 2.0 * c[2]
    rows = psi.shape[1]
    for (lo, hi), f in zip(chunks, fs):
        bands = f.shape[1]
        for band in range(bands):
            first_row = band * (rows // bands)
            for q in range(2):
                scratch[q, first_row + lo : first_row + hi, :] = f[q, band]

    def body(r):
        here = pl.ds(r, BLOCK)
        e0, e1 = with_halo(scratch, 0, r, BLOCK), with_halo(scratch, 1, r, BLOCK)
        t2, t3 = t[0, here, :], t[1, here, :]
        f0, s0 = apply_s(e0, pot[at[0], here, :], e1[8:-8], t2)
        f1, s1 = apply_s(e1, pot[at[1], here, :], e0[8:-8] + t2, t3)
        h[0, here, :] = base * psi[at[0], here, :] + one * f0 + two * s0
        h[1, here, :] = base * psi[at[1], here, :] + one * f1 + two * s1

    blocks(rows, body)


def last_kernel(chunk, row, halo, h, keep, send):
    lo, hi = chunk
    two = row[0:1, :]
    me = lax.axis_index("orb")
    bands = halo.shape[1]

    def part(band, out, slot):
        near, far = halo[0, band], halo[1, band]
        v0 = h[0, band, lo:hi, :] + two * (NEAR * near + FAR * far)
        v1 = h[1, band, lo:hi, :] + two * (FAR * near)
        out[slot, 0] = square(v0, bands)
        out[slot, 1] = square(v1, bands)

    part(me ^ 1, send, 0)
    part(me ^ 2, send, 1)
    part(me, keep, 0)
    part(me ^ 3, keep, 1)


def add_kernel(keep, came, out):
    out[...] = keep[1] + came[1]


def sum_kernel(keep, came, far, out):
    out[...] = keep[0] + came[0] + far[...]


def join_kernel(places, *refs):
    out = refs[-1]
    odd = parity()
    for (q, (lo, hi)), ref in zip(places[:-1], refs):
        for j in range(2):
            out[own(q + j, odd), lo:hi, :] = ref[j]
    (q, (lo, hi)), (keep, came, far) = places[-1], refs[-4:-1]
    for j in range(2):
        out[own(q + j, odd), lo:hi, :] = keep[0, j] + came[0, j] + far[j]


class Line:
    def __init__(self):
        self.last = []

    def __call__(self, kernel, out, args, scalars=0, scratch=(), flops=0, hbm=False, weight=0):
        vmem = pl.BlockSpec(memory_space=pltpu.VMEM)
        smem = pl.BlockSpec(memory_space=pltpu.SMEM)
        many = isinstance(out, list)
        shapes = [jax.ShapeDtypeStruct(s, jnp.float32) for s in (out if many else [out])]
        total = sum(4 * int(x.size) for x in list(args) + shapes)
        first, last = len(args), self.last

        def body(*refs):
            kernel(*refs[:first], *refs[first + len(last) :])

        result = pl.pallas_call(
            body,
            out_shape=shapes,
            in_specs=[smem] * scalars
            + [pl.BlockSpec(memory_space=pltpu.HBM) if hbm else vmem] * (first - scalars)
            + [pl.BlockSpec(memory_space=pl.ANY)] * len(last),
            out_specs=[vmem] * len(shapes),
            scratch_shapes=list(scratch),
            compiler_params=pltpu.CompilerParams(vmem_limit_bytes=40 * 2**20),
            cost_estimate=pl.CostEstimate(
                flops=flops + weight, bytes_accessed=total, transcendentals=0
            ),
        )(*args, *last)
        self.last = [result[0]]
        return result if many else result[0]


def shards(orbitals, potential, coeffs):
    psi = orbitals[0]
    slabs, bands = lax.axis_size("slab"), lax.axis_size("orb")
    planes, rows, lanes = psi.shape
    wide = rows // bands
    half, part = wide // 2, wide // 4
    chunks = [(0, half), (half, wide)]
    cuts = [(0, half), (half, wide - part), (wide - part, wide)]
    face = [(s, (s - 1 if s % 2 == 0 else s + 1) % slabs) for s in range(slabs)]
    partner = [(s, s ^ 1) for s in range(slabs)]
    near = [(i, i ^ 1) for i in range(bands)]
    far = [(i, i ^ 3) for i in range(bands)]
    plane2 = (2, rows, lanes)
    cells = 2 * rows * lanes
    call = Line()

    def as_bands(x):
        return x.reshape(x.shape[0], bands, wide, lanes)

    def slab_shape(chunk):
        return (2, bands, chunk[1] - chunk[0], lanes)

    def pair_shape(chunk):
        return (2, 2, chunk[1] - chunk[0], lanes)

    def add_far(keep, came):
        total = call(add_kernel, keep.shape[1:], (keep, came))
        return keep, came, lax.ppermute(total, "orb", far)

    def squares(cut, halo):
        keep, send = call(
            functools.partial(last_kernel, cut),
            [pair_shape(cut)] * 2,
            (row, halo, as_bands(h_front)),
        )
        return keep, lax.ppermute(send, "orb", near)

    def back_squares(chunk, halo):
        keep, send = call(
            functools.partial(back_kernel, chunk),
            [pair_shape(chunk)] * 2,
            (row, halo, as_bands(h_back)),
        )
        return keep, lax.ppermute(send, "orb", near)

    def faces(chunk, halo, parts):
        fs = call(
            functools.partial(face_kernel, chunk, parts),
            [slab_shape(cut) for cut in parts],
            (halo, as_bands(g)),
        )
        return fs, [lax.ppermute(x, "slab", face) for x in fs]

    psi_in = lax.ppermute(psi, "slab", partner)
    pot_in = lax.ppermute(potential, "slab", partner)
    halos = []
    for chunk in chunks:
        piece = call(
            functools.partial(pack_kernel, chunk),
            slab_shape(chunk),
            (as_bands(psi),),
            scratch=[pltpu.SemaphoreType.DMA],
            hbm=True,
        )
        halos.append(lax.ppermute(piece, "slab", face))
    g = call(start_kernel, plane2, (psi, potential), flops=24 * cells)
    t, h_back, row = call(
        inner_kernel,
        [plane2, plane2, (8, lanes)],
        (coeffs, psi, potential, psi_in, pot_in, g),
        scalars=1,
        flops=80 * cells,
    )

    def summed(keep, came, from_far, weight=0):
        return call(sum_kernel, from_far.shape, (keep, came, from_far), weight=weight)

    cut_a, cut_b, cut_c = cuts
    f0, (face_a,) = faces(chunks[0], halos[0], [cut_a])
    back0 = back_squares(chunks[0], halos[0])
    back0 = add_far(*back0)
    f1, (face_b, face_c) = faces(chunks[1], halos[1], [cut_b, cut_c])
    back1 = back_squares(chunks[1], halos[1])
    back0 = summed(*back0)
    h_front = call(
        functools.partial(front_kernel, cuts),
        plane2,
        (coeffs, psi, potential, t, *f0, *f1),
        scalars=1,
        scratch=[pltpu.VMEM(plane2, jnp.float32)],
        flops=40 * cells,
        weight=3_000_000_000,
    )
    back1 = add_far(*back1)
    front_a = squares(cut_a, face_a)
    front_b = squares(cut_b, face_b)
    back1 = summed(*back1, weight=2_000_000_000)
    front_a = add_far(*front_a)
    front_c = squares(cut_c, face_c)
    front_b = add_far(*front_b)
    front_a = summed(*front_a)
    front_c = add_far(*front_c)
    front_b = summed(*front_b)
    places = [(2, chunk) for chunk in chunks] + [(0, cut) for cut in cuts]
    return call(
        functools.partial(join_kernel, places),
        (planes, wide, lanes),
        (back0, back1, front_a, front_b, *front_c),
    )


def solution(mesh):
    return jax.shard_map(
        shards,
        mesh=mesh,
        in_specs=(P("orb", "slab", None, None), P("slab", None, None), P()),
        out_specs=P("slab", "orb", None),
        check_vma=False,
    )
```

```python
import functools

import jax
import jax.numpy as jnp
from jax import lax
from jax.experimental import pallas as pl
from jax.experimental.pallas import tpu as pltpu
from jax.sharding import PartitionSpec as P

NEAR = -2.0 / 15.0
FAR = 1.0 / 120.0
BLOCK = 16


def own(q, odd):
    return jnp.where(odd == 1, 3 - q, q)


def parity():
    return lax.rem(lax.axis_index("slab"), 2)


def with_halo(ref, plane, start, count):
    rows = ref.shape[-2]
    before = pl.multiple_of(lax.rem(start + rows - 8, rows), 8)
    after = pl.multiple_of(lax.rem(start + count, rows), 8)
    return jnp.concatenate(
        [
            ref[plane, pl.ds(before, 8), :],
            ref[plane, pl.ds(start, count), :],
            ref[plane, pl.ds(after, 8), :],
        ],
        axis=0,
    )


def in_plane(ext):
    count, lanes = ext.shape[0] - 16, ext.shape[1]
    mid = ext[8 : 8 + count]
    near = ext[7 : 7 + count] + ext[9 : 9 + count]
    near = near + (pltpu.roll(mid, 1, 1) + pltpu.roll(mid, lanes - 1, 1))
    far = ext[6 : 6 + count] + ext[10 : 10 + count]
    far = far + (pltpu.roll(mid, 2, 1) + pltpu.roll(mid, lanes - 2, 1))
    return mid, near, far


def apply_s(ext, pot, near_z, far_z):
    mid, near, far = in_plane(ext)
    return mid, (
        mid * (0.2 * pot - 0.05) + NEAR * (near + near_z) + FAR * (far + far_z)
    )


def blocks(rows, body):
    def step(i, carry):
        body(pl.multiple_of(i * BLOCK, BLOCK))
        return carry

    lax.fori_loop(0, rows // BLOCK, step, 0)


def pack_kernel(chunk, psi, out, sem):
    lo, hi = chunk
    planes = pl.ds(2 * parity(), out.shape[0])
    copy = pltpu.make_async_copy(psi.at[planes, :, pl.ds(lo, hi - lo), :], out, sem)
    copy.start()
    copy.wait()


def start_kernel(psi, pot, g):
    odd = parity()

    def body(r):
        here = pl.ds(r, BLOCK)
        at = [own(q, odd) for q in range(4)]
        e0, e1 = with_halo(psi, at[0], r, BLOCK), with_halo(psi, at[1], r, BLOCK)
        p2, p3 = psi[at[2], here, :], psi[at[3], here, :]
        g[0, here, :] = apply_s(e0, pot[at[0], here, :], e1[8:-8], p2)[1]
        g[1, here, :] = apply_s(e1, pot[at[1], here, :], e0[8:-8] + p2, p3)[1]

    blocks(psi.shape[1], body)


def inner_kernel(c, psi, pot, psi_in, pot_in, g, t, h, row):
    odd = parity()
    at = [own(q, odd) for q in range(4)]
    base, one, two = c[0] - c[2], c[1], 2.0 * c[2]

    def first(r):
        here = pl.ds(r, BLOCK)
        e2, e3 = with_halo(psi, at[2], r, BLOCK), with_halo(psi, at[3], r, BLOCK)
        p0, p1 = psi[at[0], here, :], psi[at[1], here, :]
        p4, p5 = psi_in[at[0], here, :], psi_in[at[1], here, :]
        t[0, here, :] = apply_s(e2, pot[at[2], here, :], p1 + e3[8:-8], p0 + p4)[1]
        t[1, here, :] = apply_s(e3, pot[at[3], here, :], e2[8:-8] + p4, p1 + p5)[1]

    def second(r):
        here = pl.ds(r, BLOCK)
        e4 = with_halo(psi_in, at[0], r, BLOCK)
        e5 = with_halo(psi_in, at[1], r, BLOCK)
        p2, p3 = psi[at[2], here, :], psi[at[3], here, :]
        p6, p7 = psi_in[at[2], here, :], psi_in[at[3], here, :]
        t4 = apply_s(e4, pot_in[at[0], here, :], p3 + e5[8:-8], p2 + p6)[1]
        t5 = apply_s(e5, pot_in[at[1], here, :], e4[8:-8] + p6, p3 + p7)[1]
        g0, g1 = g[0, here, :], g[1, here, :]
        e2, e3 = with_halo(t, 0, r, BLOCK), with_halo(t, 1, r, BLOCK)
        t2, s2 = apply_s(e2, pot[at[2], here, :], g1 + e3[8:-8], g0 + t4)
        t3, s3 = apply_s(e3, pot[at[3], here, :], e2[8:-8] + t4, g1 + t5)
        h[0, here, :] = base * p2 + one * t2 + two * s2
        h[1, here, :] = base * p3 + one * t3 + two * s3

    row[...] = jnp.full(row.shape, two)
    blocks(psi.shape[1], first)
    blocks(psi.shape[1], second)


def halo_terms(halo, band, odd, rows=slice(None)):
    near, far = halo[1 - odd, band, rows, :], halo[odd, band, rows, :]
    return NEAR * near + FAR * far, FAR * near


def square(x, bands):
    return x * x * (1.0 / bands)


def face_kernel(chunk, parts, halo, g, *fs):
    odd = parity()
    lo, hi = chunk
    for (first, last), f in zip(parts, fs):
        in_halo = slice(first - lo, last - lo)
        for band in range(halo.shape[1]):
            d0, d1 = halo_terms(halo, band, odd, in_halo)
            f[0, band] = g[0, band, first:last, :] + d0
            f[1, band] = g[1, band, first:last, :] + d1


def offsets(bands):
    return [0, *range(bands - 1, 0, -1)]


def back_kernel(chunk, row, halo, h, *outs):
    odd = parity()
    lo, hi = chunk
    two = row[0:1, :]
    me = lax.axis_index("orb")
    bands = halo.shape[1]
    for d, out in zip(offsets(bands), outs):
        band = me ^ d
        d0, d1 = halo_terms(halo, band, odd)
        v2 = h[0, band, lo:hi, :] + two * (NEAR * d1 + FAR * d0)
        v3 = h[1, band, lo:hi, :] + two * (FAR * d1)
        out[0] = square(v2, bands)
        out[1] = square(v3, bands)


def front_kernel(chunks, c, psi, pot, t, *rest):
    fs, h, scratch = rest[:-2], rest[-2], rest[-1]
    odd = parity()
    at = [own(q, odd) for q in range(2)]
    base, one, two = c[0] - c[2], c[1], 2.0 * c[2]
    rows = psi.shape[1]
    for (lo, hi), f in zip(chunks, fs):
        bands = f.shape[1]
        for band in range(bands):
            first_row = band * (rows // bands)
            for q in range(2):
                scratch[q, first_row + lo : first_row + hi, :] = f[q, band]

    def body(r):
        here = pl.ds(r, BLOCK)
        e0, e1 = with_halo(scratch, 0, r, BLOCK), with_halo(scratch, 1, r, BLOCK)
        t2, t3 = t[0, here, :], t[1, here, :]
        f0, s0 = apply_s(e0, pot[at[0], here, :], e1[8:-8], t2)
        f1, s1 = apply_s(e1, pot[at[1], here, :], e0[8:-8] + t2, t3)
        h[0, here, :] = base * psi[at[0], here, :] + one * f0 + two * s0
        h[1, here, :] = base * psi[at[1], here, :] + one * f1 + two * s1

    blocks(rows, body)


def last_kernel(chunk, row, halo, h, keep, send):
    lo, hi = chunk
    two = row[0:1, :]
    me = lax.axis_index("orb")
    bands = halo.shape[1]

    def part(band, out, slot):
        near, far = halo[0, band], halo[1, band]
        v0 = h[0, band, lo:hi, :] + two * (NEAR * near + FAR * far)
        v1 = h[1, band, lo:hi, :] + two * (FAR * near)
        out[slot, 0] = square(v0, bands)
        out[slot, 1] = square(v1, bands)

    part(me ^ 1, send, 0)
    part(me ^ 2, send, 1)
    part(me, keep, 0)
    part(me ^ 3, keep, 1)


def add_kernel(keep, came, out):
    out[...] = keep[1] + came[1]


def sum_kernel(keep, came, far, out):
    out[...] = keep[0] + came[0] + far[...]


def sum_all_kernel(*refs):
    total = refs[0][...]
    for ref in refs[1:-1]:
        total = total + ref[...]
    refs[-1][...] = total


def join_kernel(places, *refs):
    out = refs[-1]
    odd = parity()
    for (q, (lo, hi)), ref in zip(places[:-1], refs):
        for j in range(2):
            out[own(q + j, odd), lo:hi, :] = ref[j]
    (q, (lo, hi)), (keep, came, far) = places[-1], refs[-4:-1]
    for j in range(2):
        out[own(q + j, odd), lo:hi, :] = keep[0, j] + came[0, j] + far[j]


class Line:
    def __init__(self):
        self.last = []

    def __call__(self, kernel, out, args, scalars=0, scratch=(), flops=0, hbm=False, weight=0):
        vmem = pl.BlockSpec(memory_space=pltpu.VMEM)
        smem = pl.BlockSpec(memory_space=pltpu.SMEM)
        many = isinstance(out, list)
        shapes = [jax.ShapeDtypeStruct(s, jnp.float32) for s in (out if many else [out])]
        total = sum(4 * int(x.size) for x in list(args) + shapes)
        first, last = len(args), self.last

        def body(*refs):
            kernel(*refs[:first], *refs[first + len(last) :])

        result = pl.pallas_call(
            body,
            out_shape=shapes,
            in_specs=[smem] * scalars
            + [pl.BlockSpec(memory_space=pltpu.HBM) if hbm else vmem] * (first - scalars)
            + [pl.BlockSpec(memory_space=pl.ANY)] * len(last),
            out_specs=[vmem] * len(shapes),
            scratch_shapes=list(scratch),
            compiler_params=pltpu.CompilerParams(vmem_limit_bytes=40 * 2**20),
            cost_estimate=pl.CostEstimate(
                flops=flops + weight, bytes_accessed=total, transcendentals=0
            ),
        )(*args, *last)
        self.last = [result[0]]
        return result if many else result[0]


def shards(orbitals, potential, coeffs):
    psi = orbitals[0]
    slabs, bands = lax.axis_size("slab"), lax.axis_size("orb")
    planes, rows, lanes = psi.shape
    wide = rows // bands
    half, part = wide // 2, wide // 4
    chunks = [(0, half), (half, wide)]
    cuts = [(0, half), (half, wide - part), (wide - part, wide)]
    face = [(s, (s - 1 if s % 2 == 0 else s + 1) % slabs) for s in range(slabs)]
    partner = [(s, s ^ 1) for s in range(slabs)]
    near = [(i, i ^ 1) for i in range(bands)]
    far = [(i, i ^ 3) for i in range(bands)]
    plane2 = (2, rows, lanes)
    cells = 2 * rows * lanes
    call = Line()

    def as_bands(x):
        return x.reshape(x.shape[0], bands, wide, lanes)

    def slab_shape(chunk):
        return (2, bands, chunk[1] - chunk[0], lanes)

    def pair_shape(chunk):
        return (2, 2, chunk[1] - chunk[0], lanes)

    def add_far(keep, came):
        total = call(add_kernel, keep.shape[1:], (keep, came))
        return keep, came, lax.ppermute(total, "orb", far)

    def squares(cut, halo):
        keep, send = call(
            functools.partial(last_kernel, cut),
            [pair_shape(cut)] * 2,
            (row, halo, as_bands(h_front)),
        )
        return keep, lax.ppermute(send, "orb", near)

    def back_squares(chunk, halo):
        keep, *sends = call(
            functools.partial(back_kernel, chunk),
            [pair_shape(chunk)[1:]] * bands,
            (row, halo, as_bands(h_back)),
        )
        came = [
            lax.ppermute(x, "orb", [(i, i ^ d) for i in range(bands)])
            for d, x in zip(offsets(bands)[1:], sends)
        ]
        return keep, *came

    def sum_all(keep, *came, weight=0):
        return call(sum_all_kernel, keep.shape, (keep, *came), weight=weight)

    def faces(chunk, halo, parts):
        fs = call(
            functools.partial(face_kernel, chunk, parts),
            [slab_shape(cut) for cut in parts],
            (halo, as_bands(g)),
        )
        return fs, [lax.ppermute(x, "slab", face) for x in fs]

    psi_in = lax.ppermute(psi, "slab", partner)
    pot_in = lax.ppermute(potential, "slab", partner)
    halos = []
    for chunk in chunks:
        piece = call(
            functools.partial(pack_kernel, chunk),
            slab_shape(chunk),
            (as_bands(psi),),
            scratch=[pltpu.SemaphoreType.DMA],
            hbm=True,
        )
        halos.append(lax.ppermute(piece, "slab", face))
    g = call(start_kernel, plane2, (psi, potential), flops=24 * cells)
    t, h_back, row = call(
        inner_kernel,
        [plane2, plane2, (8, lanes)],
        (coeffs, psi, potential, psi_in, pot_in, g),
        scalars=1,
        flops=80 * cells,
    )

    def summed(keep, came, from_far, weight=0):
        return call(sum_kernel, from_far.shape, (keep, came, from_far), weight=weight)

    cut_a, cut_b, cut_c = cuts
    f0, (face_a,) = faces(chunks[0], halos[0], [cut_a])
    back0 = back_squares(chunks[0], halos[0])
    f1, (face_b, face_c) = faces(chunks[1], halos[1], [cut_b, cut_c])
    back1 = back_squares(chunks[1], halos[1])
    back0 = sum_all(*back0)
    h_front = call(
        functools.partial(front_kernel, cuts),
        plane2,
        (coeffs, psi, potential, t, *f0, *f1),
        scalars=1,
        scratch=[pltpu.VMEM(plane2, jnp.float32)],
        flops=40 * cells,
        weight=3_000_000_000,
    )
    front_a = squares(cut_a, face_a)
    front_b = squares(cut_b, face_b)
    back1 = sum_all(*back1, weight=2_000_000_000)
    front_a = add_far(*front_a)
    front_c = squares(cut_c, face_c)
    front_b = add_far(*front_b)
    front_a = summed(*front_a)
    front_c = add_far(*front_c)
    front_b = summed(*front_b)
    places = [(2, chunk) for chunk in chunks] + [(0, cut) for cut in cuts]
    return call(
        functools.partial(join_kernel, places),
        (planes, wide, lanes),
        (back0, back1, front_a, front_b, *front_c),
    )


def solution(mesh):
    return jax.shard_map(
        shards,
        mesh=mesh,
        in_specs=(P("orb", "slab", None, None), P("slab", None, None), P()),
        out_specs=P("slab", "orb", None),
        check_vma=False,
    )
```

```python
import functools

import jax
import jax.numpy as jnp
from jax import lax
from jax.experimental import pallas as pl
from jax.experimental.pallas import tpu as pltpu
from jax.sharding import PartitionSpec as P

NEAR = -2.0 / 15.0
FAR = 1.0 / 120.0
BLOCK = 16


def own(q, odd):
    return jnp.where(odd == 1, 3 - q, q)


def parity():
    return lax.rem(lax.axis_index("slab"), 2)


def with_halo(ref, plane, start, count):
    rows = ref.shape[-2]
    before = pl.multiple_of(lax.rem(start + rows - 8, rows), 8)
    after = pl.multiple_of(lax.rem(start + count, rows), 8)
    return jnp.concatenate(
        [
            ref[plane, pl.ds(before, 8), :],
            ref[plane, pl.ds(start, count), :],
            ref[plane, pl.ds(after, 8), :],
        ],
        axis=0,
    )


def in_plane(ext):
    count, lanes = ext.shape[0] - 16, ext.shape[1]
    mid = ext[8 : 8 + count]
    near = ext[7 : 7 + count] + ext[9 : 9 + count]
    near = near + (pltpu.roll(mid, 1, 1) + pltpu.roll(mid, lanes - 1, 1))
    far = ext[6 : 6 + count] + ext[10 : 10 + count]
    far = far + (pltpu.roll(mid, 2, 1) + pltpu.roll(mid, lanes - 2, 1))
    return mid, near, far


def apply_s(ext, pot, near_z, far_z):
    mid, near, far = in_plane(ext)
    return mid, (
        mid * (0.2 * pot - 0.05) + NEAR * (near + near_z) + FAR * (far + far_z)
    )


def blocks(rows, body):
    def step(i, carry):
        body(pl.multiple_of(i * BLOCK, BLOCK))
        return carry

    lax.fori_loop(0, rows // BLOCK, step, 0)


def pack_kernel(chunk, psi, out, sem):
    lo, hi = chunk
    planes = pl.ds(2 * parity(), out.shape[0])
    copy = pltpu.make_async_copy(psi.at[planes, :, pl.ds(lo, hi - lo), :], out, sem)
    copy.start()
    copy.wait()


def start_kernel(psi, pot, g):
    odd = parity()

    def body(r):
        here = pl.ds(r, BLOCK)
        at = [own(q, odd) for q in range(4)]
        e0, e1 = with_halo(psi, at[0], r, BLOCK), with_halo(psi, at[1], r, BLOCK)
        p2, p3 = psi[at[2], here, :], psi[at[3], here, :]
        g[0, here, :] = apply_s(e0, pot[at[0], here, :], e1[8:-8], p2)[1]
        g[1, here, :] = apply_s(e1, pot[at[1], here, :], e0[8:-8] + p2, p3)[1]

    blocks(psi.shape[1], body)


def inner_kernel(c, psi, pot, psi_in, pot_in, g, t, h, row):
    odd = parity()
    at = [own(q, odd) for q in range(4)]
    base, one, two = c[0] - c[2], c[1], 2.0 * c[2]

    def first(r):
        here = pl.ds(r, BLOCK)
        e2, e3 = with_halo(psi, at[2], r, BLOCK), with_halo(psi, at[3], r, BLOCK)
        p0, p1 = psi[at[0], here, :], psi[at[1], here, :]
        p4, p5 = psi_in[at[0], here, :], psi_in[at[1], here, :]
        t[0, here, :] = apply_s(e2, pot[at[2], here, :], p1 + e3[8:-8], p0 + p4)[1]
        t[1, here, :] = apply_s(e3, pot[at[3], here, :], e2[8:-8] + p4, p1 + p5)[1]

    def second(r):
        here = pl.ds(r, BLOCK)
        e4 = with_halo(psi_in, at[0], r, BLOCK)
        e5 = with_halo(psi_in, at[1], r, BLOCK)
        p2, p3 = psi[at[2], here, :], psi[at[3], here, :]
        p6, p7 = psi_in[at[2], here, :], psi_in[at[3], here, :]
        t4 = apply_s(e4, pot_in[at[0], here, :], p3 + e5[8:-8], p2 + p6)[1]
        t5 = apply_s(e5, pot_in[at[1], here, :], e4[8:-8] + p6, p3 + p7)[1]
        g0, g1 = g[0, here, :], g[1, here, :]
        e2, e3 = with_halo(t, 0, r, BLOCK), with_halo(t, 1, r, BLOCK)
        t2, s2 = apply_s(e2, pot[at[2], here, :], g1 + e3[8:-8], g0 + t4)
        t3, s3 = apply_s(e3, pot[at[3], here, :], e2[8:-8] + t4, g1 + t5)
        h[0, here, :] = base * p2 + one * t2 + two * s2
        h[1, here, :] = base * p3 + one * t3 + two * s3

    row[...] = jnp.full(row.shape, two)
    blocks(psi.shape[1], first)
    blocks(psi.shape[1], second)


def halo_terms(halo, band, odd, rows=slice(None)):
    near, far = halo[1 - odd, band, rows, :], halo[odd, band, rows, :]
    return NEAR * near + FAR * far, FAR * near


def square(x, bands):
    return x * x * (1.0 / bands)


def face_kernel(chunk, parts, halo, g, *fs):
    odd = parity()
    lo, hi = chunk
    for (first, last), f in zip(parts, fs):
        in_halo = slice(first - lo, last - lo)
        for band in range(halo.shape[1]):
            d0, d1 = halo_terms(halo, band, odd, in_halo)
            f[0, band] = g[0, band, first:last, :] + d0
            f[1, band] = g[1, band, first:last, :] + d1


def offsets(bands):
    return [0, *range(bands - 1, 0, -1)]


def back_kernel(chunk, row, halo, h, *outs):
    odd = parity()
    lo, hi = chunk
    two = row[0:1, :]
    me = lax.axis_index("orb")
    bands = halo.shape[1]
    for d, out in zip(offsets(bands), outs):
        band = me ^ d
        d0, d1 = halo_terms(halo, band, odd)
        v2 = h[0, band, lo:hi, :] + two * (NEAR * d1 + FAR * d0)
        v3 = h[1, band, lo:hi, :] + two * (FAR * d1)
        out[0] = square(v2, bands)
        out[1] = square(v3, bands)


def front_kernel(chunks, c, psi, pot, t, *rest):
    fs, h, scratch = rest[:-2], rest[-2], rest[-1]
    odd = parity()
    at = [own(q, odd) for q in range(2)]
    base, one, two = c[0] - c[2], c[1], 2.0 * c[2]
    rows = psi.shape[1]
    for (lo, hi), f in zip(chunks, fs):
        bands = f.shape[1]
        for band in range(bands):
            first_row = band * (rows // bands)
            for q in range(2):
                scratch[q, first_row + lo : first_row + hi, :] = f[q, band]

    def body(r):
        here = pl.ds(r, BLOCK)
        e0, e1 = with_halo(scratch, 0, r, BLOCK), with_halo(scratch, 1, r, BLOCK)
        t2, t3 = t[0, here, :], t[1, here, :]
        f0, s0 = apply_s(e0, pot[at[0], here, :], e1[8:-8], t2)
        f1, s1 = apply_s(e1, pot[at[1], here, :], e0[8:-8] + t2, t3)
        h[0, here, :] = base * psi[at[0], here, :] + one * f0 + two * s0
        h[1, here, :] = base * psi[at[1], here, :] + one * f1 + two * s1

    blocks(rows, body)


def last_kernel(chunk, row, halo, h, keep, send):
    lo, hi = chunk
    two = row[0:1, :]
    me = lax.axis_index("orb")
    bands = halo.shape[1]

    def part(band, out, slot):
        near, far = halo[0, band], halo[1, band]
        v0 = h[0, band, lo:hi, :] + two * (NEAR * near + FAR * far)
        v1 = h[1, band, lo:hi, :] + two * (FAR * near)
        out[slot, 0] = square(v0, bands)
        out[slot, 1] = square(v1, bands)

    part(me ^ 1, send, 0)
    part(me ^ 2, send, 1)
    part(me, keep, 0)
    part(me ^ 3, keep, 1)


def add_kernel(keep, came, out):
    out[...] = keep[1] + came[1]


def sum_kernel(keep, came, far, out):
    out[...] = keep[0] + came[0] + far[...]


def sum_all_kernel(*refs):
    total = refs[0][...]
    for ref in refs[1:-1]:
        total = total + ref[...]
    refs[-1][...] = total


def join_kernel(places, *refs):
    out = refs[-1]
    odd = parity()
    for (q, (lo, hi)), ref in zip(places[:-1], refs):
        for j in range(2):
            out[own(q + j, odd), lo:hi, :] = ref[j]
    (q, (lo, hi)), (keep, came, far) = places[-1], refs[-4:-1]
    for j in range(2):
        out[own(q + j, odd), lo:hi, :] = keep[0, j] + came[0, j] + far[j]


class Line:
    def __init__(self):
        self.last = []

    def __call__(self, kernel, out, args, scalars=0, scratch=(), flops=0, hbm=False, weight=0):
        vmem = pl.BlockSpec(memory_space=pltpu.VMEM)
        smem = pl.BlockSpec(memory_space=pltpu.SMEM)
        many = isinstance(out, list)
        shapes = [jax.ShapeDtypeStruct(s, jnp.float32) for s in (out if many else [out])]
        total = sum(4 * int(x.size) for x in list(args) + shapes)
        first, last = len(args), self.last

        def body(*refs):
            kernel(*refs[:first], *refs[first + len(last) :])

        result = pl.pallas_call(
            body,
            out_shape=shapes,
            in_specs=[smem] * scalars
            + [pl.BlockSpec(memory_space=pltpu.HBM) if hbm else vmem] * (first - scalars)
            + [pl.BlockSpec(memory_space=pl.ANY)] * len(last),
            out_specs=[vmem] * len(shapes),
            scratch_shapes=list(scratch),
            compiler_params=pltpu.CompilerParams(vmem_limit_bytes=40 * 2**20),
            cost_estimate=pl.CostEstimate(
                flops=flops + weight, bytes_accessed=total, transcendentals=0
            ),
        )(*args, *last)
        self.last = [result[0]]
        return result if many else result[0]


def shards(orbitals, potential, coeffs):
    psi = orbitals[0]
    slabs, bands = lax.axis_size("slab"), lax.axis_size("orb")
    planes, rows, lanes = psi.shape
    wide = rows // bands
    half, part = wide // 2, wide // 4
    chunks = [(0, half), (half, wide)]
    cuts = [(0, half), (half, wide - part), (wide - part, wide)]
    face = [(s, (s - 1 if s % 2 == 0 else s + 1) % slabs) for s in range(slabs)]
    partner = [(s, s ^ 1) for s in range(slabs)]
    near = [(i, i ^ 1) for i in range(bands)]
    far = [(i, i ^ 3) for i in range(bands)]
    plane2 = (2, rows, lanes)
    cells = 2 * rows * lanes
    call = Line()

    def as_bands(x):
        return x.reshape(x.shape[0], bands, wide, lanes)

    def slab_shape(chunk):
        return (2, bands, chunk[1] - chunk[0], lanes)

    def pair_shape(chunk):
        return (2, 2, chunk[1] - chunk[0], lanes)

    def add_far(keep, came):
        total = call(add_kernel, keep.shape[1:], (keep, came))
        return keep, came, lax.ppermute(total, "orb", far)

    def squares(cut, halo):
        keep, send = call(
            functools.partial(last_kernel, cut),
            [pair_shape(cut)] * 2,
            (row, halo, as_bands(h_front)),
        )
        return keep, lax.ppermute(send, "orb", near)

    def back_squares(chunk, halo):
        keep, *sends = call(
            functools.partial(back_kernel, chunk),
            [pair_shape(chunk)[1:]] * bands,
            (row, halo, as_bands(h_back)),
        )
        came = [
            lax.ppermute(x, "orb", [(i, i ^ d) for i in range(bands)])
            for d, x in zip(offsets(bands)[1:], sends)
        ]
        return keep, *came

    def sum_all(keep, *came, weight=0):
        return call(sum_all_kernel, keep.shape, (keep, *came), weight=weight)

    def faces(chunk, halo, parts):
        fs = call(
            functools.partial(face_kernel, chunk, parts),
            [slab_shape(cut) for cut in parts],
            (halo, as_bands(g)),
        )
        return fs, [lax.ppermute(x, "slab", face) for x in fs]

    psi_in = lax.ppermute(psi, "slab", partner)
    pot_in = lax.ppermute(potential, "slab", partner)
    halos = []
    for chunk in chunks:
        piece = call(
            functools.partial(pack_kernel, chunk),
            slab_shape(chunk),
            (as_bands(psi),),
            scratch=[pltpu.SemaphoreType.DMA],
            hbm=True,
        )
        halos.append(lax.ppermute(piece, "slab", face))
    g = call(start_kernel, plane2, (psi, potential), flops=24 * cells)
    t, h_back, row = call(
        inner_kernel,
        [plane2, plane2, (8, lanes)],
        (coeffs, psi, potential, psi_in, pot_in, g),
        scalars=1,
        flops=80 * cells,
    )

    def summed(keep, came, from_far, weight=0):
        return call(sum_kernel, from_far.shape, (keep, came, from_far), weight=weight)

    cut_a, cut_b, cut_c = cuts
    f0, (face_a,) = faces(chunks[0], halos[0], [cut_a])
    back0 = back_squares(chunks[0], halos[0])
    f1, (face_b, face_c) = faces(chunks[1], halos[1], [cut_b, cut_c])
    back1 = back_squares(chunks[1], halos[1])
    back0 = sum_all(*back0)
    h_front = call(
        functools.partial(front_kernel, cuts),
        plane2,
        (coeffs, psi, potential, t, *f0, *f1),
        scalars=1,
        scratch=[pltpu.VMEM(plane2, jnp.float32)],
        flops=40 * cells,
        weight=3_000_000_000,
    )
    back1 = sum_all(*back1)
    front_a = squares(cut_a, face_a)
    front_b = squares(cut_b, face_b)
    front_a = add_far(*front_a)
    front_c = squares(cut_c, face_c)
    front_b = add_far(*front_b)
    front_a = summed(*front_a)
    front_c = add_far(*front_c)
    front_b = summed(*front_b)
    places = [(2, chunk) for chunk in chunks] + [(0, cut) for cut in cuts]
    return call(
        functools.partial(join_kernel, places),
        (planes, wide, lanes),
        (back0, back1, front_a, front_b, *front_c),
    )


def solution(mesh):
    return jax.shard_map(
        shards,
        mesh=mesh,
        in_specs=(P("orb", "slab", None, None), P("slab", None, None), P()),
        out_specs=P("slab", "orb", None),
        check_vma=False,
    )
```

```python
import functools

import jax
import jax.numpy as jnp
from jax import lax
from jax.experimental import pallas as pl
from jax.experimental.pallas import tpu as pltpu
from jax.sharding import PartitionSpec as P

NEAR = -2.0 / 15.0
FAR = 1.0 / 120.0
BLOCK = 16


def own(q, odd):
    return jnp.where(odd == 1, 3 - q, q)


def parity():
    return lax.rem(lax.axis_index("slab"), 2)


def with_halo(ref, plane, start, count):
    rows = ref.shape[-2]
    before = pl.multiple_of(lax.rem(start + rows - 8, rows), 8)
    after = pl.multiple_of(lax.rem(start + count, rows), 8)
    return jnp.concatenate(
        [
            ref[plane, pl.ds(before, 8), :],
            ref[plane, pl.ds(start, count), :],
            ref[plane, pl.ds(after, 8), :],
        ],
        axis=0,
    )


def in_plane(ext):
    count, lanes = ext.shape[0] - 16, ext.shape[1]
    mid = ext[8 : 8 + count]
    near = ext[7 : 7 + count] + ext[9 : 9 + count]
    near = near + (pltpu.roll(mid, 1, 1) + pltpu.roll(mid, lanes - 1, 1))
    far = ext[6 : 6 + count] + ext[10 : 10 + count]
    far = far + (pltpu.roll(mid, 2, 1) + pltpu.roll(mid, lanes - 2, 1))
    return mid, near, far


def apply_s(ext, pot, near_z, far_z):
    mid, near, far = in_plane(ext)
    return mid, (
        mid * (0.2 * pot - 0.05) + NEAR * (near + near_z) + FAR * (far + far_z)
    )


def blocks(rows, body):
    def step(i, carry):
        body(pl.multiple_of(i * BLOCK, BLOCK))
        return carry

    lax.fori_loop(0, rows // BLOCK, step, 0)


def pack_kernel(chunk, psi, out, sem):
    lo, hi = chunk
    planes = pl.ds(2 * parity(), out.shape[0])
    copy = pltpu.make_async_copy(psi.at[planes, :, pl.ds(lo, hi - lo), :], out, sem)
    copy.start()
    copy.wait()


def start_kernel(psi, pot, g):
    odd = parity()

    def body(r):
        here = pl.ds(r, BLOCK)
        at = [own(q, odd) for q in range(4)]
        e0, e1 = with_halo(psi, at[0], r, BLOCK), with_halo(psi, at[1], r, BLOCK)
        p2, p3 = psi[at[2], here, :], psi[at[3], here, :]
        g[0, here, :] = apply_s(e0, pot[at[0], here, :], e1[8:-8], p2)[1]
        g[1, here, :] = apply_s(e1, pot[at[1], here, :], e0[8:-8] + p2, p3)[1]

    blocks(psi.shape[1], body)


def inner_kernel(c, psi, pot, psi_in, pot_in, g, t, h, row):
    odd = parity()
    at = [own(q, odd) for q in range(4)]
    base, one, two = c[0] - c[2], c[1], 2.0 * c[2]

    def first(r):
        here = pl.ds(r, BLOCK)
        e2, e3 = with_halo(psi, at[2], r, BLOCK), with_halo(psi, at[3], r, BLOCK)
        p0, p1 = psi[at[0], here, :], psi[at[1], here, :]
        p4, p5 = psi_in[at[0], here, :], psi_in[at[1], here, :]
        t[0, here, :] = apply_s(e2, pot[at[2], here, :], p1 + e3[8:-8], p0 + p4)[1]
        t[1, here, :] = apply_s(e3, pot[at[3], here, :], e2[8:-8] + p4, p1 + p5)[1]

    def second(r):
        here = pl.ds(r, BLOCK)
        e4 = with_halo(psi_in, at[0], r, BLOCK)
        e5 = with_halo(psi_in, at[1], r, BLOCK)
        p2, p3 = psi[at[2], here, :], psi[at[3], here, :]
        p6, p7 = psi_in[at[2], here, :], psi_in[at[3], here, :]
        t4 = apply_s(e4, pot_in[at[0], here, :], p3 + e5[8:-8], p2 + p6)[1]
        t5 = apply_s(e5, pot_in[at[1], here, :], e4[8:-8] + p6, p3 + p7)[1]
        g0, g1 = g[0, here, :], g[1, here, :]
        e2, e3 = with_halo(t, 0, r, BLOCK), with_halo(t, 1, r, BLOCK)
        t2, s2 = apply_s(e2, pot[at[2], here, :], g1 + e3[8:-8], g0 + t4)
        t3, s3 = apply_s(e3, pot[at[3], here, :], e2[8:-8] + t4, g1 + t5)
        h[0, here, :] = base * p2 + one * t2 + two * s2
        h[1, here, :] = base * p3 + one * t3 + two * s3

    row[...] = jnp.full(row.shape, two)
    blocks(psi.shape[1], first)
    blocks(psi.shape[1], second)


def halo_terms(halo, band, odd, rows=slice(None)):
    near, far = halo[1 - odd, band, rows, :], halo[odd, band, rows, :]
    return NEAR * near + FAR * far, FAR * near


def square(x, bands):
    return x * x * (1.0 / bands)


def face_kernel(chunk, parts, halo, g, *fs):
    odd = parity()
    lo, hi = chunk
    for (first, last), f in zip(parts, fs):
        in_halo = slice(first - lo, last - lo)
        for band in range(halo.shape[1]):
            d0, d1 = halo_terms(halo, band, odd, in_halo)
            f[0, band] = g[0, band, first:last, :] + d0
            f[1, band] = g[1, band, first:last, :] + d1


def offsets(bands):
    return [0, *range(bands - 1, 0, -1)]


def back_kernel(chunk, row, halo, h, *outs):
    odd = parity()
    lo, hi = chunk
    two = row[0:1, :]
    me = lax.axis_index("orb")
    bands = halo.shape[1]
    for d, out in zip(offsets(bands), outs):
        band = me ^ d
        d0, d1 = halo_terms(halo, band, odd)
        v2 = h[0, band, lo:hi, :] + two * (NEAR * d1 + FAR * d0)
        v3 = h[1, band, lo:hi, :] + two * (FAR * d1)
        out[0] = square(v2, bands)
        out[1] = square(v3, bands)


def front_kernel(chunks, c, psi, pot, t, *rest):
    fs, h, scratch = rest[:-2], rest[-2], rest[-1]
    odd = parity()
    at = [own(q, odd) for q in range(2)]
    base, one, two = c[0] - c[2], c[1], 2.0 * c[2]
    rows = psi.shape[1]
    for (lo, hi), f in zip(chunks, fs):
        bands = f.shape[1]
        for band in range(bands):
            first_row = band * (rows // bands)
            for q in range(2):
                scratch[q, first_row + lo : first_row + hi, :] = f[q, band]

    def body(r):
        here = pl.ds(r, BLOCK)
        e0, e1 = with_halo(scratch, 0, r, BLOCK), with_halo(scratch, 1, r, BLOCK)
        t2, t3 = t[0, here, :], t[1, here, :]
        f0, s0 = apply_s(e0, pot[at[0], here, :], e1[8:-8], t2)
        f1, s1 = apply_s(e1, pot[at[1], here, :], e0[8:-8] + t2, t3)
        h[0, here, :] = base * psi[at[0], here, :] + one * f0 + two * s0
        h[1, here, :] = base * psi[at[1], here, :] + one * f1 + two * s1

    blocks(rows, body)


def last_kernel(chunk, row, halo, h, keep, send):
    lo, hi = chunk
    two = row[0:1, :]
    me = lax.axis_index("orb")
    bands = halo.shape[1]

    def part(band, out, slot):
        near, far = halo[0, band], halo[1, band]
        v0 = h[0, band, lo:hi, :] + two * (NEAR * near + FAR * far)
        v1 = h[1, band, lo:hi, :] + two * (FAR * near)
        out[slot, 0] = square(v0, bands)
        out[slot, 1] = square(v1, bands)

    part(me ^ 1, send, 0)
    part(me ^ 2, send, 1)
    part(me, keep, 0)
    part(me ^ 3, keep, 1)


def add_kernel(keep, came, out):
    out[...] = keep[1] + came[1]


def sum_kernel(keep, came, far, out):
    out[...] = keep[0] + came[0] + far[...]


def sum_all_kernel(*refs):
    total = refs[0][...]
    for ref in refs[1:-1]:
        total = total + ref[...]
    refs[-1][...] = total


def join_kernel(places, *refs):
    out = refs[-1]
    odd = parity()
    for (q, (lo, hi)), ref in zip(places[:-1], refs):
        for j in range(2):
            out[own(q + j, odd), lo:hi, :] = ref[j]
    (q, (lo, hi)), (keep, came, far) = places[-1], refs[-4:-1]
    for j in range(2):
        out[own(q + j, odd), lo:hi, :] = keep[0, j] + came[0, j] + far[j]


class Line:
    def __init__(self):
        self.last = []

    def __call__(self, kernel, out, args, scalars=0, scratch=(), flops=0, hbm=False, weight=0):
        vmem = pl.BlockSpec(memory_space=pltpu.VMEM)
        smem = pl.BlockSpec(memory_space=pltpu.SMEM)
        many = isinstance(out, list)
        shapes = [jax.ShapeDtypeStruct(s, jnp.float32) for s in (out if many else [out])]
        total = sum(4 * int(x.size) for x in list(args) + shapes)
        first, last = len(args), self.last

        def body(*refs):
            kernel(*refs[:first], *refs[first + len(last) :])

        result = pl.pallas_call(
            body,
            out_shape=shapes,
            in_specs=[smem] * scalars
            + [pl.BlockSpec(memory_space=pltpu.HBM) if hbm else vmem] * (first - scalars)
            + [pl.BlockSpec(memory_space=pl.ANY)] * len(last),
            out_specs=[vmem] * len(shapes),
            scratch_shapes=list(scratch),
            compiler_params=pltpu.CompilerParams(vmem_limit_bytes=40 * 2**20),
            cost_estimate=pl.CostEstimate(
                flops=flops + weight, bytes_accessed=total, transcendentals=0
            ),
        )(*args, *last)
        self.last = [result[0]]
        return result if many else result[0]


def shards(orbitals, potential, coeffs):
    psi = orbitals[0]
    slabs, bands = lax.axis_size("slab"), lax.axis_size("orb")
    planes, rows, lanes = psi.shape
    wide = rows // bands
    half, part = wide // 2, wide // 4
    chunks = [(0, half), (half, wide)]
    cuts = [(0, half), (half, wide - part), (wide - part, wide)]
    face = [(s, (s - 1 if s % 2 == 0 else s + 1) % slabs) for s in range(slabs)]
    partner = [(s, s ^ 1) for s in range(slabs)]
    near = [(i, i ^ 1) for i in range(bands)]
    far = [(i, i ^ 3) for i in range(bands)]
    plane2 = (2, rows, lanes)
    cells = 2 * rows * lanes
    call = Line()

    def as_bands(x):
        return x.reshape(x.shape[0], bands, wide, lanes)

    def slab_shape(chunk):
        return (2, bands, chunk[1] - chunk[0], lanes)

    def pair_shape(chunk):
        return (2, 2, chunk[1] - chunk[0], lanes)

    def add_far(keep, came):
        total = call(add_kernel, keep.shape[1:], (keep, came))
        return keep, came, lax.ppermute(total, "orb", far)

    def squares(cut, halo):
        keep, send = call(
            functools.partial(last_kernel, cut),
            [pair_shape(cut)] * 2,
            (row, halo, as_bands(h_front)),
        )
        return keep, lax.ppermute(send, "orb", near)

    def back_squares(chunk, halo):
        keep, *sends = call(
            functools.partial(back_kernel, chunk),
            [pair_shape(chunk)[1:]] * bands,
            (row, halo, as_bands(h_back)),
        )
        came = [
            lax.ppermute(x, "orb", [(i, i ^ d) for i in range(bands)])
            for d, x in zip(offsets(bands)[1:], sends)
        ]
        return keep, *came

    def sum_all(keep, *came, weight=0):
        return call(sum_all_kernel, keep.shape, (keep, *came), weight=weight)

    def faces(chunk, halo, parts):
        fs = call(
            functools.partial(face_kernel, chunk, parts),
            [slab_shape(cut) for cut in parts],
            (halo, as_bands(g)),
        )
        return fs, [lax.ppermute(x, "slab", face) for x in fs]

    psi_in = lax.ppermute(psi, "slab", partner)
    pot_in = lax.ppermute(potential, "slab", partner)
    halos = []
    for chunk in chunks:
        piece = call(
            functools.partial(pack_kernel, chunk),
            slab_shape(chunk),
            (as_bands(psi),),
            scratch=[pltpu.SemaphoreType.DMA],
            hbm=True,
        )
        halos.append(lax.ppermute(piece, "slab", face))
    g = call(start_kernel, plane2, (psi, potential), flops=24 * cells)
    t, h_back, row = call(
        inner_kernel,
        [plane2, plane2, (8, lanes)],
        (coeffs, psi, potential, psi_in, pot_in, g),
        scalars=1,
        flops=80 * cells,
    )

    def summed(keep, came, from_far, weight=0):
        return call(sum_kernel, from_far.shape, (keep, came, from_far), weight=weight)

    cut_a, cut_b, cut_c = cuts
    back0 = back_squares(chunks[0], halos[0])
    f0, (face_a,) = faces(chunks[0], halos[0], [cut_a])
    back1 = back_squares(chunks[1], halos[1])
    f1, (face_b, face_c) = faces(chunks[1], halos[1], [cut_b, cut_c])
    back0 = sum_all(*back0)
    h_front = call(
        functools.partial(front_kernel, cuts),
        plane2,
        (coeffs, psi, potential, t, *f0, *f1),
        scalars=1,
        scratch=[pltpu.VMEM(plane2, jnp.float32)],
        flops=40 * cells,
        weight=6_000_000_000,
    )
    back1 = sum_all(*back1)
    front_a = squares(cut_a, face_a)
    front_b = squares(cut_b, face_b)
    front_a = add_far(*front_a)
    front_c = squares(cut_c, face_c)
    front_b = add_far(*front_b)
    front_a = summed(*front_a)
    front_c = add_far(*front_c)
    front_b = summed(*front_b)
    places = [(2, chunk) for chunk in chunks] + [(0, cut) for cut in cuts]
    return call(
        functools.partial(join_kernel, places),
        (planes, wide, lanes),
        (back0, back1, front_a, front_b, *front_c),
    )


def solution(mesh):
    return jax.shard_map(
        shards,
        mesh=mesh,
        in_specs=(P("orb", "slab", None, None), P("slab", None, None), P()),
        out_specs=P("slab", "orb", None),
        check_vma=False,
    )
```

```python
import functools

import jax
import jax.numpy as jnp
from jax import lax
from jax.experimental import pallas as pl
from jax.experimental.pallas import tpu as pltpu
from jax.sharding import PartitionSpec as P

NEAR = -2.0 / 15.0
FAR = 1.0 / 120.0
BLOCK = 16


def own(q, odd):
    return jnp.where(odd == 1, 3 - q, q)


def parity():
    return lax.rem(lax.axis_index("slab"), 2)


def with_halo(ref, plane, start, count):
    rows = ref.shape[-2]
    before = pl.multiple_of(lax.rem(start + rows - 8, rows), 8)
    after = pl.multiple_of(lax.rem(start + count, rows), 8)
    return jnp.concatenate(
        [
            ref[plane, pl.ds(before, 8), :],
            ref[plane, pl.ds(start, count), :],
            ref[plane, pl.ds(after, 8), :],
        ],
        axis=0,
    )


def in_plane(ext):
    count, lanes = ext.shape[0] - 16, ext.shape[1]
    mid = ext[8 : 8 + count]
    near = ext[7 : 7 + count] + ext[9 : 9 + count]
    near = near + (pltpu.roll(mid, 1, 1) + pltpu.roll(mid, lanes - 1, 1))
    far = ext[6 : 6 + count] + ext[10 : 10 + count]
    far = far + (pltpu.roll(mid, 2, 1) + pltpu.roll(mid, lanes - 2, 1))
    return mid, near, far


def apply_s(ext, pot, near_z, far_z):
    mid, near, far = in_plane(ext)
    return mid, (
        mid * (0.2 * pot - 0.05) + NEAR * (near + near_z) + FAR * (far + far_z)
    )


def apply_rows(e, pot, near_z, far_z):
    count, lanes = e.shape[0] - 4, e.shape[1]
    mid = e[2 : 2 + count]
    near = e[1 : 1 + count] + e[3 : 3 + count]
    near = near + (pltpu.roll(mid, 1, 1) + pltpu.roll(mid, lanes - 1, 1))
    far = e[0:count] + e[4 : 4 + count]
    far = far + (pltpu.roll(mid, 2, 1) + pltpu.roll(mid, lanes - 2, 1))
    return mid * (0.2 * pot - 0.05) + NEAR * (near + near_z) + FAR * (far + far_z)


def blocks(rows, body):
    def step(i, carry):
        body(pl.multiple_of(i * BLOCK, BLOCK))
        return carry

    lax.fori_loop(0, rows // BLOCK, step, 0)


def pack_kernel(chunk, psi, out, sem):
    lo, hi = chunk
    planes = pl.ds(2 * parity(), out.shape[0])
    copy = pltpu.make_async_copy(psi.at[planes, :, pl.ds(lo, hi - lo), :], out, sem)
    copy.start()
    copy.wait()


def start_kernel(psi, pot, g):
    odd = parity()

    def body(r):
        here = pl.ds(r, BLOCK)
        at = [own(q, odd) for q in range(4)]
        e0, e1 = with_halo(psi, at[0], r, BLOCK), with_halo(psi, at[1], r, BLOCK)
        p2, p3 = psi[at[2], here, :], psi[at[3], here, :]
        g[0, here, :] = apply_s(e0, pot[at[0], here, :], e1[8:-8], p2)[1]
        g[1, here, :] = apply_s(e1, pot[at[1], here, :], e0[8:-8] + p2, p3)[1]

    blocks(psi.shape[1], body)


def inner_kernel(c, psi, pot, psi_in, pot_in, g, t, h, row):
    odd = parity()
    at = [own(q, odd) for q in range(4)]
    base, one, two = c[0] - c[2], c[1], 2.0 * c[2]

    def first(r):
        here = pl.ds(r, BLOCK)
        e2, e3 = with_halo(psi, at[2], r, BLOCK), with_halo(psi, at[3], r, BLOCK)
        p0, p1 = psi[at[0], here, :], psi[at[1], here, :]
        p4, p5 = psi_in[at[0], here, :], psi_in[at[1], here, :]
        t[0, here, :] = apply_s(e2, pot[at[2], here, :], p1 + e3[8:-8], p0 + p4)[1]
        t[1, here, :] = apply_s(e3, pot[at[3], here, :], e2[8:-8] + p4, p1 + p5)[1]

    def second(r):
        here = pl.ds(r, BLOCK)
        e4 = with_halo(psi_in, at[0], r, BLOCK)
        e5 = with_halo(psi_in, at[1], r, BLOCK)
        p2, p3 = psi[at[2], here, :], psi[at[3], here, :]
        p6, p7 = psi_in[at[2], here, :], psi_in[at[3], here, :]
        t4 = apply_s(e4, pot_in[at[0], here, :], p3 + e5[8:-8], p2 + p6)[1]
        t5 = apply_s(e5, pot_in[at[1], here, :], e4[8:-8] + p6, p3 + p7)[1]
        g0, g1 = g[0, here, :], g[1, here, :]
        e2, e3 = with_halo(t, 0, r, BLOCK), with_halo(t, 1, r, BLOCK)
        t2, s2 = apply_s(e2, pot[at[2], here, :], g1 + e3[8:-8], g0 + t4)
        t3, s3 = apply_s(e3, pot[at[3], here, :], e2[8:-8] + t4, g1 + t5)
        h[0, here, :] = base * p2 + one * t2 + two * s2
        h[1, here, :] = base * p3 + one * t3 + two * s3

    row[...] = jnp.full(row.shape, two)
    blocks(psi.shape[1], first)
    blocks(psi.shape[1], second)


def halo_terms(halo, band, odd, rows=slice(None)):
    near, far = halo[1 - odd, band, rows, :], halo[odd, band, rows, :]
    return NEAR * near + FAR * far, FAR * near


def square(x, bands):
    return x * x * (1.0 / bands)


def face_kernel(chunk, parts, halo, g, *fs):
    odd = parity()
    lo, hi = chunk
    for (first, last), f in zip(parts, fs):
        in_halo = slice(first - lo, last - lo)
        for band in range(halo.shape[1]):
            d0, d1 = halo_terms(halo, band, odd, in_halo)
            f[0, band] = g[0, band, first:last, :] + d0
            f[1, band] = g[1, band, first:last, :] + d1


def offsets(bands):
    return [0, *range(bands - 1, 0, -1)]


def back_kernel(chunk, part, row, halo, h, *outs):
    odd = parity()
    lo, hi = part
    in_halo = slice(lo - chunk[0], hi - chunk[0])
    two = row[0:1, :]
    me = lax.axis_index("orb")
    bands = halo.shape[1]
    for d, out in zip(offsets(bands), outs):
        band = me ^ d
        d0, d1 = halo_terms(halo, band, odd, in_halo)
        v2 = h[0, band, lo:hi, :] + two * (NEAR * d1 + FAR * d0)
        v3 = h[1, band, lo:hi, :] + two * (FAR * d1)
        out[0] = square(v2, bands)
        out[1] = square(v3, bands)


def tail_rows(ref, plane, band, start, more):
    after = lax.rem(band + 1, ref.shape[1])
    return jnp.concatenate(
        [ref[plane, band, start:, :], ref[plane, after, :more, :]], axis=0
    )


def send_rows_kernel(part, psi, *outs):
    me = lax.axis_index("orb")
    for d, out in zip(offsets(psi.shape[1]), outs):
        for plane in range(psi.shape[0]):
            out[plane] = tail_rows(psi, plane, me ^ d, part[0] - 4, 4)


def gather_kernel(*refs):
    every, halo = refs[-2:]
    odd = parity()
    count = halo.shape[0] // (2 * (len(refs) - 3))
    for k, ref in enumerate(refs[:-2]):
        every[k] = ref[...]
        for q in range(2):
            if k:
                first = (2 * (k - 1) + q) * count
                halo[first : first + count, :] = ref[own(q, odd), 2 : 2 + count, :]


def rows_kernel(part, c, x, x_in, pot, pot_in, g, t, h):
    odd = parity()
    me = lax.axis_index("orb")
    at = [own(q, odd) for q in range(4)]
    base, one, two = c[0] - c[2], c[1], 2.0 * c[2]
    v = [tail_rows(pot, at[q], me, part[0] - 2, 2) for q in range(4)]
    v += [tail_rows(pot_in, at[q], me, part[0] - 2, 2) for q in range(2)]
    n = g.shape[2]

    def step(k, carry):
        e = [x[k, at[q]] for q in range(4)] + [x_in[k, at[q]] for q in range(4)]
        m = [y[2 : 2 + n] for y in e]
        g0 = apply_rows(e[0], v[0], m[1], m[2])
        g1 = apply_rows(e[1], v[1], m[0] + m[2], m[3])
        g[k, 0], g[k, 1] = g0, g1
        full = [apply_rows(e[q], v[q], m[q - 1] + m[q + 1], m[q - 2] + m[q + 2])
                for q in range(2, 6)]
        f = [y[2 : n - 2] for y in [g0, g1, *full]]
        for j in range(2):
            t[k, j] = f[2 + j]
            q = 2 + j
            s = apply_rows(full[j], v[q][2 : n - 2], f[q - 1] + f[q + 1], f[q - 2] + f[q + 2])
            h[k, j] = base * e[q][4 : n] + one * f[q] + two * s
        return carry

    lax.fori_loop(0, x.shape[0], step, 0)


def rows_halo(part, k, halo, first, second, n):
    if k:
        at = [(2 * (k - 1) + q) * n for q in range(2)]
        near, far = [halo[a : a + n, :] for a in at]
    else:
        odd = parity()
        me = lax.axis_index("orb")
        after = lax.rem(me + 1, first.shape[1])
        near, far = [
            jnp.concatenate(
                [second[q, me, second.shape[2] - (n - 2) :, :], first[q, after, :2, :]],
                axis=0,
            )
            for q in (1 - odd, odd)
        ]
    return NEAR * near + FAR * far, FAR * near


def rows_face_kernel(part, halo, first, second, g, f, send):
    n = g.shape[2]
    for k in range(g.shape[0]):
        terms = rows_halo(part, k, halo, first, second, n)
        for q in range(2):
            value = g[k, q] + terms[q]
            f[k, q] = value
            send[k, q] = value[2 : n - 2]


def rows_front_kernel(part, c, x, pot, halo, first, second, f, t, h, back, front):
    odd = parity()
    me = lax.axis_index("orb")
    base, one, two = c[0] - c[2], c[1], 2.0 * c[2]
    n = f.shape[2]
    v = [
        tail_rows(pot, own(q, odd), me, part[0] - 2, 2)[2 : n - 2] for q in range(2)
    ]
    total = [0.0, 0.0]
    count = f.shape[0]
    for k in range(count):
        d0, d1 = [y[2 : n - 2] for y in rows_halo(part, k, halo, first, second, n)]
        v2 = h[k, 0] + two * (NEAR * d1 + FAR * d0)
        v3 = h[k, 1] + two * (FAR * d1)
        total = [total[0] + square(v2, count), total[1] + square(v3, count)]
        f0, f1 = f[k, 0], f[k, 1]
        t2, t3 = t[k, 0], t[k, 1]
        m0, m1 = f0[2 : n - 2], f1[2 : n - 2]
        s0 = apply_rows(f0, v[0], m1, t2)
        s1 = apply_rows(f1, v[1], m0 + t2, t3)
        front[k, 0] = base * x[k, own(0, odd)][4:n] + one * m0 + two * s0
        front[k, 1] = base * x[k, own(1, odd)][4:n] + one * m1 + two * s1
    back[0], back[1] = total


def front_kernel(chunks, c, psi, pot, t, *rest):
    fs, h, scratch = rest[:-2], rest[-2], rest[-1]
    odd = parity()
    at = [own(q, odd) for q in range(2)]
    base, one, two = c[0] - c[2], c[1], 2.0 * c[2]
    rows = psi.shape[1]
    for (lo, hi), f in zip(chunks, fs):
        bands = f.shape[1]
        for band in range(bands):
            first_row = band * (rows // bands)
            for q in range(2):
                scratch[q, first_row + lo : first_row + hi, :] = f[q, band]

    def body(r):
        here = pl.ds(r, BLOCK)
        e0, e1 = with_halo(scratch, 0, r, BLOCK), with_halo(scratch, 1, r, BLOCK)
        t2, t3 = t[0, here, :], t[1, here, :]
        f0, s0 = apply_s(e0, pot[at[0], here, :], e1[8:-8], t2)
        f1, s1 = apply_s(e1, pot[at[1], here, :], e0[8:-8] + t2, t3)
        h[0, here, :] = base * psi[at[0], here, :] + one * f0 + two * s0
        h[1, here, :] = base * psi[at[1], here, :] + one * f1 + two * s1

    blocks(rows, body)


def last_kernel(chunk, row, halo, h, keep, send):
    lo, hi = chunk
    two = row[0:1, :]
    me = lax.axis_index("orb")
    bands = halo.shape[1]

    def part(band, out, slot):
        near, far = halo[0, band], halo[1, band]
        v0 = h[0, band, lo:hi, :] + two * (NEAR * near + FAR * far)
        v1 = h[1, band, lo:hi, :] + two * (FAR * near)
        out[slot, 0] = square(v0, bands)
        out[slot, 1] = square(v1, bands)

    part(me ^ 1, send, 0)
    part(me ^ 2, send, 1)
    part(me, keep, 0)
    part(me ^ 3, keep, 1)


def add_kernel(keep, came, out):
    out[...] = keep[1] + came[1]


def sum_kernel(keep, came, far, out):
    out[...] = keep[0] + came[0] + far[...]


def sum_all_kernel(*refs):
    total = refs[0][...]
    for ref in refs[1:-1]:
        total = total + ref[...]
    refs[-1][...] = total


def join_kernel(places, part, *refs):
    row, halo, h, out = refs[-4:]
    odd = parity()
    for (q, (lo, hi)), ref in zip(places, refs):
        for j in range(2):
            out[own(q + j, odd), lo:hi, :] = ref[j]
    two = row[0:1, :]
    count = h.shape[0]
    total = [0.0, 0.0]
    for k in range(count):
        near, far = halo[k, 0], halo[k, 1]
        v0 = h[k, 0] + two * (NEAR * near + FAR * far)
        v1 = h[k, 1] + two * (FAR * near)
        total = [total[0] + square(v0, count), total[1] + square(v1, count)]
    for j in range(2):
        out[own(j, odd), part[0] : part[1], :] = total[j]


class Line:
    def __init__(self):
        self.last = []

    def __call__(self, kernel, out, args, scalars=0, scratch=(), flops=0, hbm=False, weight=0):
        vmem = pl.BlockSpec(memory_space=pltpu.VMEM)
        smem = pl.BlockSpec(memory_space=pltpu.SMEM)
        many = isinstance(out, list)
        shapes = [jax.ShapeDtypeStruct(s, jnp.float32) for s in (out if many else [out])]
        total = sum(4 * int(x.size) for x in list(args) + shapes)
        first, last = len(args), self.last

        def body(*refs):
            kernel(*refs[:first], *refs[first + len(last) :])

        result = pl.pallas_call(
            body,
            out_shape=shapes,
            in_specs=[smem] * scalars
            + [pl.BlockSpec(memory_space=pltpu.HBM) if hbm else vmem] * (first - scalars)
            + [pl.BlockSpec(memory_space=pl.ANY)] * len(last),
            out_specs=[vmem] * len(shapes),
            scratch_shapes=list(scratch),
            compiler_params=pltpu.CompilerParams(vmem_limit_bytes=40 * 2**20),
            cost_estimate=pl.CostEstimate(
                flops=flops + weight, bytes_accessed=total, transcendentals=0
            ),
        )(*args, *last)
        self.last = [result[0]]
        return result if many else result[0]


def shards(orbitals, potential, coeffs):
    psi = orbitals[0]
    slabs, bands = lax.axis_size("slab"), lax.axis_size("orb")
    planes, rows, lanes = psi.shape
    wide = rows // bands
    half, part = wide // 2, wide // 4
    chunks = [(0, half), (half, wide)]
    cuts = [(0, half), (half, wide - part), (wide - part, wide)]
    cut_a, cut_b, cut_c = cuts
    padded, inner = (part + 8, part + 4)
    face = [(s, (s - 1 if s % 2 == 0 else s + 1) % slabs) for s in range(slabs)]
    partner = [(s, s ^ 1) for s in range(slabs)]
    near = [(i, i ^ 1) for i in range(bands)]
    far = [(i, i ^ 3) for i in range(bands)]
    plane2 = (2, rows, lanes)
    cells = 2 * rows * lanes
    call = Line()

    def as_bands(x):
        return x.reshape(x.shape[0], bands, wide, lanes)

    def slab_shape(chunk):
        return (2, bands, chunk[1] - chunk[0], lanes)

    def pair_shape(chunk):
        return (2, 2, chunk[1] - chunk[0], lanes)

    def add_far(keep, came):
        total = call(add_kernel, keep.shape[1:], (keep, came))
        return keep, came, lax.ppermute(total, "orb", far)

    def squares(cut, halo):
        keep, send = call(
            functools.partial(last_kernel, cut),
            [pair_shape(cut)] * 2,
            (row, halo, as_bands(h_front)),
        )
        return keep, lax.ppermute(send, "orb", near)

    def over_orb(x, d):
        return lax.ppermute(x, "orb", [(i, i ^ d) for i in range(bands)])

    def back_squares(chunk, rows, halo):
        keep, *sends = call(
            functools.partial(back_kernel, chunk, rows),
            [pair_shape(rows)[1:]] * bands,
            (row, halo, as_bands(h_back)),
        )
        return keep, *[over_orb(x, d) for d, x in zip(offsets(bands)[1:], sends)]

    def sum_all(keep, *came, weight=0):
        return call(sum_all_kernel, keep.shape, (keep, *came), weight=weight)

    def faces(chunk, halo, parts):
        fs = call(
            functools.partial(face_kernel, chunk, parts),
            [slab_shape(cut) for cut in parts],
            (halo, as_bands(g)),
        )
        return fs, lax.ppermute(fs[0], "slab", face)

    psi_in = lax.ppermute(psi, "slab", partner)
    pot_in = lax.ppermute(potential, "slab", partner)
    halos = []
    for chunk in chunks:
        piece = call(
            functools.partial(pack_kernel, chunk),
            slab_shape(chunk),
            (as_bands(psi),),
            scratch=[pltpu.SemaphoreType.DMA],
            hbm=True,
        )
        halos.append(lax.ppermute(piece, "slab", face))
    keep, *sends = call(
        functools.partial(send_rows_kernel, cut_c),
        [(planes, padded, lanes)] * bands,
        (as_bands(psi),),
    )
    x_parts = [keep, *[over_orb(x, d) for d, x in zip(offsets(bands)[1:], sends)]]
    g = call(start_kernel, plane2, (psi, potential), flops=24 * cells)
    t, h_back, row = call(
        inner_kernel,
        [plane2, plane2, (8, lanes)],
        (coeffs, psi, potential, psi_in, pot_in, g),
        scalars=1,
        flops=80 * cells,
    )

    def summed(keep, came, from_far, weight=0):
        return call(sum_kernel, from_far.shape, (keep, came, from_far), weight=weight)

    back0 = back_squares(chunks[0], cut_a, halos[0])
    f0, face_a = faces(chunks[0], halos[0], [cut_a])
    x, piece = call(
        gather_kernel,
        [(bands, planes, padded, lanes), (2 * (bands - 1) * inner, lanes)],
        x_parts,
    )
    x_halo = lax.ppermute(piece, "slab", face)
    x_in = lax.ppermute(x, "slab", partner)
    back1 = back_squares(chunks[1], cut_b, halos[1])
    f1, face_b = faces(chunks[1], halos[1], [cut_b, cut_c])
    x_first, x_t, x_back = call(
        functools.partial(rows_kernel, cut_c),
        [(bands, 2, inner, lanes)] + [(bands, 2, part, lanes)] * 2,
        (coeffs, x, x_in, as_bands(potential), as_bands(pot_in)),
        scalars=1,
    )
    back0 = sum_all(*back0, weight=0)
    h_front = call(
        functools.partial(front_kernel, cuts),
        plane2,
        (coeffs, psi, potential, t, *f0, *f1),
        scalars=1,
        scratch=[pltpu.VMEM(plane2, jnp.float32)],
        flops=40 * cells,
        weight=6_000_000_000,
    )
    back1 = sum_all(*back1, weight=0)
    front_a = squares(cut_a, face_a)
    x_f, piece = call(
        functools.partial(rows_face_kernel, cut_c),
        [(bands, 2, inner, lanes), (bands, 2, part, lanes)],
        (x_halo, *halos, x_first),
    )
    x_face = lax.ppermute(piece, "slab", face)
    front_a = add_far(*front_a)
    back2, x_front = call(
        functools.partial(rows_front_kernel, cut_c),
        [(2, part, lanes), (bands, 2, part, lanes)],
        (coeffs, x, as_bands(potential), x_halo, *halos, x_f, x_t, x_back),
        scalars=1,
    )
    front_b = squares(cut_b, face_b)
    front_a = summed(*front_a)
    front_b = add_far(*front_b)
    front_b = summed(*front_b)
    places = [(2, cut) for cut in cuts] + [(0, cut_a), (0, cut_b)]
    return call(
        functools.partial(join_kernel, places, cut_c),
        (planes, wide, lanes),
        (back0, back1, back2, front_a, front_b, row, x_face, x_front),
    )


def solution(mesh):
    return jax.shard_map(
        shards,
        mesh=mesh,
        in_specs=(P("orb", "slab", None, None), P("slab", None, None), P()),
        out_specs=P("slab", "orb", None),
        check_vma=False,
    )
```

```python
import functools

import jax
import jax.numpy as jnp
from jax import lax
from jax.experimental import pallas as pl
from jax.experimental.pallas import tpu as pltpu
from jax.sharding import PartitionSpec as P

NEAR = -2.0 / 15.0
FAR = 1.0 / 120.0
BLOCK = 16


def own(q, odd):
    return jnp.where(odd == 1, 3 - q, q)


def parity():
    return lax.rem(lax.axis_index("slab"), 2)


def with_halo(ref, plane, start, count):
    rows = ref.shape[-2]
    before = pl.multiple_of(lax.rem(start + rows - 8, rows), 8)
    after = pl.multiple_of(lax.rem(start + count, rows), 8)
    return jnp.concatenate(
        [
            ref[plane, pl.ds(before, 8), :],
            ref[plane, pl.ds(start, count), :],
            ref[plane, pl.ds(after, 8), :],
        ],
        axis=0,
    )


def in_plane(ext):
    count, lanes = ext.shape[0] - 16, ext.shape[1]
    mid = ext[8 : 8 + count]
    near = ext[7 : 7 + count] + ext[9 : 9 + count]
    near = near + (pltpu.roll(mid, 1, 1) + pltpu.roll(mid, lanes - 1, 1))
    far = ext[6 : 6 + count] + ext[10 : 10 + count]
    far = far + (pltpu.roll(mid, 2, 1) + pltpu.roll(mid, lanes - 2, 1))
    return mid, near, far


def apply_s(ext, pot, near_z, far_z):
    mid, near, far = in_plane(ext)
    return mid, (
        mid * (0.2 * pot - 0.05) + NEAR * (near + near_z) + FAR * (far + far_z)
    )


def apply_rows(e, pot, near_z, far_z):
    count, lanes = e.shape[0] - 4, e.shape[1]
    mid = e[2 : 2 + count]
    near = e[1 : 1 + count] + e[3 : 3 + count]
    near = near + (pltpu.roll(mid, 1, 1) + pltpu.roll(mid, lanes - 1, 1))
    far = e[0:count] + e[4 : 4 + count]
    far = far + (pltpu.roll(mid, 2, 1) + pltpu.roll(mid, lanes - 2, 1))
    return mid * (0.2 * pot - 0.05) + NEAR * (near + near_z) + FAR * (far + far_z)


def blocks(rows, body):
    def step(i, carry):
        body(pl.multiple_of(i * BLOCK, BLOCK))
        return carry

    lax.fori_loop(0, rows // BLOCK, step, 0)


def pack_kernel(chunk, psi, out, sem):
    lo, hi = chunk
    planes = pl.ds(2 * parity(), out.shape[0])
    copy = pltpu.make_async_copy(psi.at[planes, :, pl.ds(lo, hi - lo), :], out, sem)
    copy.start()
    copy.wait()


def start_kernel(psi, pot, g):
    odd = parity()

    def body(r):
        here = pl.ds(r, BLOCK)
        at = [own(q, odd) for q in range(4)]
        e0, e1 = with_halo(psi, at[0], r, BLOCK), with_halo(psi, at[1], r, BLOCK)
        p2, p3 = psi[at[2], here, :], psi[at[3], here, :]
        g[0, here, :] = apply_s(e0, pot[at[0], here, :], e1[8:-8], p2)[1]
        g[1, here, :] = apply_s(e1, pot[at[1], here, :], e0[8:-8] + p2, p3)[1]

    blocks(psi.shape[1], body)


def inner_kernel(c, psi, pot, psi_in, pot_in, g, t, h, row):
    odd = parity()
    at = [own(q, odd) for q in range(4)]
    base, one, two = c[0] - c[2], c[1], 2.0 * c[2]

    def first(r):
        here = pl.ds(r, BLOCK)
        e2, e3 = with_halo(psi, at[2], r, BLOCK), with_halo(psi, at[3], r, BLOCK)
        p0, p1 = psi[at[0], here, :], psi[at[1], here, :]
        p4, p5 = psi_in[at[0], here, :], psi_in[at[1], here, :]
        t[0, here, :] = apply_s(e2, pot[at[2], here, :], p1 + e3[8:-8], p0 + p4)[1]
        t[1, here, :] = apply_s(e3, pot[at[3], here, :], e2[8:-8] + p4, p1 + p5)[1]

    def second(r):
        here = pl.ds(r, BLOCK)
        e4 = with_halo(psi_in, at[0], r, BLOCK)
        e5 = with_halo(psi_in, at[1], r, BLOCK)
        p2, p3 = psi[at[2], here, :], psi[at[3], here, :]
        p6, p7 = psi_in[at[2], here, :], psi_in[at[3], here, :]
        t4 = apply_s(e4, pot_in[at[0], here, :], p3 + e5[8:-8], p2 + p6)[1]
        t5 = apply_s(e5, pot_in[at[1], here, :], e4[8:-8] + p6, p3 + p7)[1]
        g0, g1 = g[0, here, :], g[1, here, :]
        e2, e3 = with_halo(t, 0, r, BLOCK), with_halo(t, 1, r, BLOCK)
        t2, s2 = apply_s(e2, pot[at[2], here, :], g1 + e3[8:-8], g0 + t4)
        t3, s3 = apply_s(e3, pot[at[3], here, :], e2[8:-8] + t4, g1 + t5)
        h[0, here, :] = base * p2 + one * t2 + two * s2
        h[1, here, :] = base * p3 + one * t3 + two * s3

    row[...] = jnp.full(row.shape, two)
    blocks(psi.shape[1], first)
    blocks(psi.shape[1], second)


def halo_terms(halo, band, odd, rows=slice(None)):
    near, far = halo[1 - odd, band, rows, :], halo[odd, band, rows, :]
    return NEAR * near + FAR * far, FAR * near


def square(x, bands):
    return x * x * (1.0 / bands)


def face_kernel(chunk, parts, halo, g, *fs):
    odd = parity()
    lo, hi = chunk
    for (first, last), f in zip(parts, fs):
        in_halo = slice(first - lo, last - lo)
        for band in range(halo.shape[1]):
            d0, d1 = halo_terms(halo, band, odd, in_halo)
            f[0, band] = g[0, band, first:last, :] + d0
            f[1, band] = g[1, band, first:last, :] + d1


def offsets(bands):
    return [0, *range(bands - 1, 0, -1)]


def back_kernel(part, row, halo, h, *outs):
    odd = parity()
    lo, hi = part
    two = row[0:1, :]
    me = lax.axis_index("orb")
    bands = halo.shape[1]
    for d, out in zip(offsets(bands), outs):
        band = me ^ d
        d0, d1 = halo_terms(halo, band, odd, slice(lo, hi))
        v2 = h[0, band, lo:hi, :] + two * (NEAR * d1 + FAR * d0)
        v3 = h[1, band, lo:hi, :] + two * (FAR * d1)
        out[0] = square(v2, bands)
        out[1] = square(v3, bands)


def tail_rows(ref, plane, band, start, more):
    after = lax.rem(band + 1, ref.shape[1])
    return jnp.concatenate(
        [ref[plane, band, start:, :], ref[plane, after, :more, :]], axis=0
    )


def send_rows_kernel(part, psi, *outs):
    me = lax.axis_index("orb")
    for d, out in zip(offsets(psi.shape[1]), outs):
        for plane in range(psi.shape[0]):
            out[plane] = tail_rows(psi, plane, me ^ d, part[0] - 4, 4)


def gather_kernel(*refs):
    every, halo = refs[-2:]
    odd = parity()
    count = halo.shape[0] // (2 * (len(refs) - 3))
    for k, ref in enumerate(refs[:-2]):
        every[k] = ref[...]
        for q in range(2):
            if k:
                first = (2 * (k - 1) + q) * count
                halo[first : first + count, :] = ref[own(q, odd), 2 : 2 + count, :]


def rows_kernel(part, c, x, x_in, pot, pot_in, g, t, h):
    odd = parity()
    me = lax.axis_index("orb")
    at = [own(q, odd) for q in range(4)]
    base, one, two = c[0] - c[2], c[1], 2.0 * c[2]
    v = [tail_rows(pot, at[q], me, part[0] - 2, 2) for q in range(4)]
    v += [tail_rows(pot_in, at[q], me, part[0] - 2, 2) for q in range(2)]
    n = g.shape[2]

    def step(k, carry):
        e = [x[k, at[q]] for q in range(4)] + [x_in[k, at[q]] for q in range(4)]
        m = [y[2 : 2 + n] for y in e]
        g0 = apply_rows(e[0], v[0], m[1], m[2])
        g1 = apply_rows(e[1], v[1], m[0] + m[2], m[3])
        g[k, 0], g[k, 1] = g0, g1
        full = [apply_rows(e[q], v[q], m[q - 1] + m[q + 1], m[q - 2] + m[q + 2])
                for q in range(2, 6)]
        f = [y[2 : n - 2] for y in [g0, g1, *full]]
        for j in range(2):
            t[k, j] = f[2 + j]
            q = 2 + j
            s = apply_rows(full[j], v[q][2 : n - 2], f[q - 1] + f[q + 1], f[q - 2] + f[q + 2])
            h[k, j] = base * e[q][4 : n] + one * f[q] + two * s
        return carry

    lax.fori_loop(0, x.shape[0], step, 0)


def rows_halo(part, k, halo, first, second, n):
    if k:
        at = [(2 * (k - 1) + q) * n for q in range(2)]
        near, far = [halo[a : a + n, :] for a in at]
    else:
        odd = parity()
        me = lax.axis_index("orb")
        after = lax.rem(me + 1, first.shape[1])
        near, far = [
            jnp.concatenate(
                [second[q, me, second.shape[2] - (n - 2) :, :], first[q, after, :2, :]],
                axis=0,
            )
            for q in (1 - odd, odd)
        ]
    return NEAR * near + FAR * far, FAR * near


def rows_face_kernel(part, halo, first, second, g, f, send):
    n = g.shape[2]
    for k in range(g.shape[0]):
        terms = rows_halo(part, k, halo, first, second, n)
        for q in range(2):
            value = g[k, q] + terms[q]
            f[k, q] = value
            send[k, q] = value[2 : n - 2]


def rows_front_kernel(part, c, x, pot, halo, first, second, f, t, h, back, front):
    odd = parity()
    me = lax.axis_index("orb")
    base, one, two = c[0] - c[2], c[1], 2.0 * c[2]
    n = f.shape[2]
    v = [
        tail_rows(pot, own(q, odd), me, part[0] - 2, 2)[2 : n - 2] for q in range(2)
    ]
    total = [0.0, 0.0]
    count = f.shape[0]
    for k in range(count):
        d0, d1 = [y[2 : n - 2] for y in rows_halo(part, k, halo, first, second, n)]
        v2 = h[k, 0] + two * (NEAR * d1 + FAR * d0)
        v3 = h[k, 1] + two * (FAR * d1)
        total = [total[0] + square(v2, count), total[1] + square(v3, count)]
        f0, f1 = f[k, 0], f[k, 1]
        t2, t3 = t[k, 0], t[k, 1]
        m0, m1 = f0[2 : n - 2], f1[2 : n - 2]
        s0 = apply_rows(f0, v[0], m1, t2)
        s1 = apply_rows(f1, v[1], m0 + t2, t3)
        front[k, 0] = base * x[k, own(0, odd)][4:n] + one * m0 + two * s0
        front[k, 1] = base * x[k, own(1, odd)][4:n] + one * m1 + two * s1
    back[0], back[1] = total


def front_kernel(chunks, c, psi, pot, t, *rest):
    fs, h, scratch = rest[:-2], rest[-2], rest[-1]
    odd = parity()
    at = [own(q, odd) for q in range(2)]
    base, one, two = c[0] - c[2], c[1], 2.0 * c[2]
    rows = psi.shape[1]
    for (lo, hi), f in zip(chunks, fs):
        bands = f.shape[1]
        for band in range(bands):
            first_row = band * (rows // bands)
            for q in range(2):
                scratch[q, first_row + lo : first_row + hi, :] = f[q, band]

    def body(r):
        here = pl.ds(r, BLOCK)
        e0, e1 = with_halo(scratch, 0, r, BLOCK), with_halo(scratch, 1, r, BLOCK)
        t2, t3 = t[0, here, :], t[1, here, :]
        f0, s0 = apply_s(e0, pot[at[0], here, :], e1[8:-8], t2)
        f1, s1 = apply_s(e1, pot[at[1], here, :], e0[8:-8] + t2, t3)
        h[0, here, :] = base * psi[at[0], here, :] + one * f0 + two * s0
        h[1, here, :] = base * psi[at[1], here, :] + one * f1 + two * s1

    blocks(rows, body)


def last_kernel(chunk, row, halo, h, keep, send):
    lo, hi = chunk
    two = row[0:1, :]
    me = lax.axis_index("orb")
    bands = halo.shape[1]

    def part(band, out, slot):
        near, far = halo[0, band], halo[1, band]
        v0 = h[0, band, lo:hi, :] + two * (NEAR * near + FAR * far)
        v1 = h[1, band, lo:hi, :] + two * (FAR * near)
        out[slot, 0] = square(v0, bands)
        out[slot, 1] = square(v1, bands)

    part(me ^ 1, send, 0)
    part(me ^ 2, send, 1)
    part(me, keep, 0)
    part(me ^ 3, keep, 1)


def add_kernel(keep, came, out):
    out[...] = keep[1] + came[1]


def sum_kernel(keep, came, far, out):
    out[...] = keep[0] + came[0] + far[...]


def sum_all_kernel(*refs):
    total = refs[0][...]
    for ref in refs[1:-1]:
        total = total + ref[...]
    refs[-1][...] = total


def join_kernel(places, part, *refs):
    row, halo, h, out = refs[-4:]
    odd = parity()
    for (q, (lo, hi)), ref in zip(places, refs):
        for j in range(2):
            out[own(q + j, odd), lo:hi, :] = ref[j]
    two = row[0:1, :]
    count = h.shape[0]
    total = [0.0, 0.0]
    for k in range(count):
        near, far = halo[k, 0], halo[k, 1]
        v0 = h[k, 0] + two * (NEAR * near + FAR * far)
        v1 = h[k, 1] + two * (FAR * near)
        total = [total[0] + square(v0, count), total[1] + square(v1, count)]
    for j in range(2):
        out[own(j, odd), part[0] : part[1], :] = total[j]


class Line:
    def __init__(self):
        self.last = []

    def __call__(self, kernel, out, args, scalars=0, scratch=(), flops=0, hbm=False, weight=0):
        vmem = pl.BlockSpec(memory_space=pltpu.VMEM)
        smem = pl.BlockSpec(memory_space=pltpu.SMEM)
        many = isinstance(out, list)
        shapes = [jax.ShapeDtypeStruct(s, jnp.float32) for s in (out if many else [out])]
        total = sum(4 * int(x.size) for x in list(args) + shapes)
        first, last = len(args), self.last

        def body(*refs):
            kernel(*refs[:first], *refs[first + len(last) :])

        result = pl.pallas_call(
            body,
            out_shape=shapes,
            in_specs=[smem] * scalars
            + [pl.BlockSpec(memory_space=pltpu.HBM) if hbm else vmem] * (first - scalars)
            + [pl.BlockSpec(memory_space=pl.ANY)] * len(last),
            out_specs=[vmem] * len(shapes),
            scratch_shapes=list(scratch),
            compiler_params=pltpu.CompilerParams(vmem_limit_bytes=40 * 2**20),
            cost_estimate=pl.CostEstimate(
                flops=flops + weight, bytes_accessed=total, transcendentals=0
            ),
        )(*args, *last)
        self.last = [result[0]]
        return result if many else result[0]


def shards(orbitals, potential, coeffs):
    psi = orbitals[0]
    slabs, bands = lax.axis_size("slab"), lax.axis_size("orb")
    planes, rows, lanes = psi.shape
    wide = rows // bands
    half, part = wide // 2, wide // 4
    chunk = (0, wide)
    cuts = [(0, half), (half, wide - part), (wide - part, wide)]
    cut_a, cut_b, cut_c = cuts
    padded, inner = (part + 8, part + 4)
    face = [(s, (s - 1 if s % 2 == 0 else s + 1) % slabs) for s in range(slabs)]
    partner = [(s, s ^ 1) for s in range(slabs)]
    near = [(i, i ^ 1) for i in range(bands)]
    far = [(i, i ^ 3) for i in range(bands)]
    plane2 = (2, rows, lanes)
    cells = 2 * rows * lanes
    call = Line()

    def as_bands(x):
        return x.reshape(x.shape[0], bands, wide, lanes)

    def slab_shape(chunk):
        return (2, bands, chunk[1] - chunk[0], lanes)

    def pair_shape(chunk):
        return (2, 2, chunk[1] - chunk[0], lanes)

    def add_far(keep, came):
        total = call(add_kernel, keep.shape[1:], (keep, came))
        return keep, came, lax.ppermute(total, "orb", far)

    def squares(cut, halo):
        keep, send = call(
            functools.partial(last_kernel, cut),
            [pair_shape(cut)] * 2,
            (row, halo, as_bands(h_front)),
        )
        return keep, lax.ppermute(send, "orb", near)

    def over_orb(x, d):
        return lax.ppermute(x, "orb", [(i, i ^ d) for i in range(bands)])

    def back_squares(rows):
        keep, *sends = call(
            functools.partial(back_kernel, rows),
            [pair_shape(rows)[1:]] * bands,
            (row, halo, as_bands(h_back)),
        )
        return keep, *[over_orb(x, d) for d, x in zip(offsets(bands)[1:], sends)]

    def sum_all(keep, *came, weight=0):
        return call(sum_all_kernel, keep.shape, (keep, *came), weight=weight)

    psi_in = lax.ppermute(psi, "slab", partner)
    pot_in = lax.ppermute(potential, "slab", partner)
    piece = call(
        functools.partial(pack_kernel, chunk),
        slab_shape(chunk),
        (as_bands(psi),),
        scratch=[pltpu.SemaphoreType.DMA],
        hbm=True,
    )
    halo = lax.ppermute(piece, "slab", face)
    keep, *sends = call(
        functools.partial(send_rows_kernel, cut_c),
        [(planes, padded, lanes)] * bands,
        (as_bands(psi),),
    )
    x_parts = [keep, *[over_orb(x, d) for d, x in zip(offsets(bands)[1:], sends)]]
    g = call(start_kernel, plane2, (psi, potential), flops=24 * cells)
    t, h_back, row = call(
        inner_kernel,
        [plane2, plane2, (8, lanes)],
        (coeffs, psi, potential, psi_in, pot_in, g),
        scalars=1,
        flops=80 * cells,
    )

    def summed(keep, came, from_far, weight=0):
        return call(sum_kernel, from_far.shape, (keep, came, from_far), weight=weight)

    x, piece = call(
        gather_kernel,
        [(bands, planes, padded, lanes), (2 * (bands - 1) * inner, lanes)],
        x_parts,
    )
    x_in = lax.ppermute(x, "slab", partner)
    x_halo = lax.ppermute(piece, "slab", face)
    x_first, x_t, x_back = call(
        functools.partial(rows_kernel, cut_c),
        [(bands, 2, inner, lanes)] + [(bands, 2, part, lanes)] * 2,
        (coeffs, x, x_in, as_bands(potential), as_bands(pot_in)),
        scalars=1,
    )
    fs = call(
        functools.partial(face_kernel, chunk, cuts),
        [slab_shape(cut) for cut in cuts],
        (halo, as_bands(g)),
    )
    face_a, face_b = [lax.ppermute(f, "slab", face) for f in fs[:2]]
    back0 = back_squares((0, wide - part))
    x_f, piece = call(
        functools.partial(rows_face_kernel, cut_c),
        [(bands, 2, inner, lanes), (bands, 2, part, lanes)],
        (x_halo, halo, halo, x_first),
    )
    x_face = lax.ppermute(piece, "slab", face)
    h_front = call(
        functools.partial(front_kernel, cuts),
        plane2,
        (coeffs, psi, potential, t, *fs),
        scalars=1,
        scratch=[pltpu.VMEM(plane2, jnp.float32)],
        flops=40 * cells,
        weight=4_000_000_000,
    )
    back2, x_front = call(
        functools.partial(rows_front_kernel, cut_c),
        [(2, part, lanes), (bands, 2, part, lanes)],
        (coeffs, x, as_bands(potential), x_halo, halo, halo, x_f, x_t, x_back),
        scalars=1,
    )
    front_a = squares(cut_a, face_a)
    back0 = sum_all(*back0, weight=1_000_000_000)
    front_b = squares(cut_b, face_b)
    front_a = add_far(*front_a)
    front_b = add_far(*front_b)
    front_a = summed(*front_a)
    front_b = summed(*front_b)
    places = [(2, (0, wide - part)), (2, cut_c), (0, cut_a), (0, cut_b)]
    return call(
        functools.partial(join_kernel, places, cut_c),
        (planes, wide, lanes),
        (back0, back2, front_a, front_b, row, x_face, x_front),
    )


def solution(mesh):
    return jax.shard_map(
        shards,
        mesh=mesh,
        in_specs=(P("orb", "slab", None, None), P("slab", None, None), P()),
        out_specs=P("slab", "orb", None),
        check_vma=False,
    )
```

```python
import functools

import jax
import jax.numpy as jnp
from jax import lax
from jax.experimental import pallas as pl
from jax.experimental.pallas import tpu as pltpu
from jax.sharding import PartitionSpec as P

NEAR = -2.0 / 15.0
FAR = 1.0 / 120.0
BLOCK = 16


def own(q, odd):
    return jnp.where(odd == 1, 3 - q, q)


def parity():
    return lax.rem(lax.axis_index("slab"), 2)


def with_halo(ref, plane, start, count):
    rows = ref.shape[-2]
    before = pl.multiple_of(lax.rem(start + rows - 8, rows), 8)
    after = pl.multiple_of(lax.rem(start + count, rows), 8)
    return jnp.concatenate(
        [
            ref[plane, pl.ds(before, 8), :],
            ref[plane, pl.ds(start, count), :],
            ref[plane, pl.ds(after, 8), :],
        ],
        axis=0,
    )


def in_plane(ext):
    count, lanes = ext.shape[0] - 16, ext.shape[1]
    mid = ext[8 : 8 + count]
    near = ext[7 : 7 + count] + ext[9 : 9 + count]
    near = near + (pltpu.roll(mid, 1, 1) + pltpu.roll(mid, lanes - 1, 1))
    far = ext[6 : 6 + count] + ext[10 : 10 + count]
    far = far + (pltpu.roll(mid, 2, 1) + pltpu.roll(mid, lanes - 2, 1))
    return mid, near, far


def apply_s(ext, pot, near_z, far_z):
    mid, near, far = in_plane(ext)
    return mid, (
        mid * (0.2 * pot - 0.05) + NEAR * (near + near_z) + FAR * (far + far_z)
    )


def apply_rows(e, pot, near_z, far_z):
    count, lanes = e.shape[0] - 4, e.shape[1]
    mid = e[2 : 2 + count]
    near = e[1 : 1 + count] + e[3 : 3 + count]
    near = near + (pltpu.roll(mid, 1, 1) + pltpu.roll(mid, lanes - 1, 1))
    far = e[0:count] + e[4 : 4 + count]
    far = far + (pltpu.roll(mid, 2, 1) + pltpu.roll(mid, lanes - 2, 1))
    return mid * (0.2 * pot - 0.05) + NEAR * (near + near_z) + FAR * (far + far_z)


def blocks(rows, body):
    def step(i, carry):
        body(pl.multiple_of(i * BLOCK, BLOCK))
        return carry

    lax.fori_loop(0, rows // BLOCK, step, 0)


def pack_kernel(chunk, psi, out, sem):
    lo, hi = chunk
    planes = pl.ds(2 * parity(), out.shape[0])
    copy = pltpu.make_async_copy(psi.at[planes, :, pl.ds(lo, hi - lo), :], out, sem)
    copy.start()
    copy.wait()


def start_kernel(psi, pot, g):
    odd = parity()

    def body(r):
        here = pl.ds(r, BLOCK)
        at = [own(q, odd) for q in range(4)]
        e0, e1 = with_halo(psi, at[0], r, BLOCK), with_halo(psi, at[1], r, BLOCK)
        p2, p3 = psi[at[2], here, :], psi[at[3], here, :]
        g[0, here, :] = apply_s(e0, pot[at[0], here, :], e1[8:-8], p2)[1]
        g[1, here, :] = apply_s(e1, pot[at[1], here, :], e0[8:-8] + p2, p3)[1]

    blocks(psi.shape[1], body)


def inner_kernel(c, psi, pot, psi_in, pot_in, g, t, h, row):
    odd = parity()
    at = [own(q, odd) for q in range(4)]
    base, one, two = c[0] - c[2], c[1], 2.0 * c[2]

    def first(r):
        here = pl.ds(r, BLOCK)
        e2, e3 = with_halo(psi, at[2], r, BLOCK), with_halo(psi, at[3], r, BLOCK)
        p0, p1 = psi[at[0], here, :], psi[at[1], here, :]
        p4, p5 = psi_in[at[0], here, :], psi_in[at[1], here, :]
        t[0, here, :] = apply_s(e2, pot[at[2], here, :], p1 + e3[8:-8], p0 + p4)[1]
        t[1, here, :] = apply_s(e3, pot[at[3], here, :], e2[8:-8] + p4, p1 + p5)[1]

    def second(r):
        here = pl.ds(r, BLOCK)
        e4 = with_halo(psi_in, at[0], r, BLOCK)
        e5 = with_halo(psi_in, at[1], r, BLOCK)
        p2, p3 = psi[at[2], here, :], psi[at[3], here, :]
        p6, p7 = psi_in[at[2], here, :], psi_in[at[3], here, :]
        t4 = apply_s(e4, pot_in[at[0], here, :], p3 + e5[8:-8], p2 + p6)[1]
        t5 = apply_s(e5, pot_in[at[1], here, :], e4[8:-8] + p6, p3 + p7)[1]
        g0, g1 = g[0, here, :], g[1, here, :]
        e2, e3 = with_halo(t, 0, r, BLOCK), with_halo(t, 1, r, BLOCK)
        t2, s2 = apply_s(e2, pot[at[2], here, :], g1 + e3[8:-8], g0 + t4)
        t3, s3 = apply_s(e3, pot[at[3], here, :], e2[8:-8] + t4, g1 + t5)
        h[0, here, :] = base * p2 + one * t2 + two * s2
        h[1, here, :] = base * p3 + one * t3 + two * s3

    row[...] = jnp.full(row.shape, two)
    blocks(psi.shape[1], first)
    blocks(psi.shape[1], second)


def halo_terms(halo, band, odd, rows=slice(None)):
    near, far = halo[1 - odd, band, rows, :], halo[odd, band, rows, :]
    return NEAR * near + FAR * far, FAR * near


def square(x, bands):
    return x * x * (1.0 / bands)


def face_kernel(chunk, parts, halo, g, *fs):
    odd = parity()
    lo, hi = chunk
    for (first, last), f in zip(parts, fs):
        in_halo = slice(first - lo, last - lo)
        for band in range(halo.shape[1]):
            d0, d1 = halo_terms(halo, band, odd, in_halo)
            f[0, band] = g[0, band, first:last, :] + d0
            f[1, band] = g[1, band, first:last, :] + d1


def offsets(bands):
    return [0, *range(bands - 1, 0, -1)]


def back_kernel(part, row, halo, h, *outs):
    odd = parity()
    lo, hi = part
    two = row[0:1, :]
    me = lax.axis_index("orb")
    bands = halo.shape[1]
    for d, out in zip(offsets(bands), outs):
        band = me ^ d
        d0, d1 = halo_terms(halo, band, odd, slice(lo, hi))
        v2 = h[0, band, lo:hi, :] + two * (NEAR * d1 + FAR * d0)
        v3 = h[1, band, lo:hi, :] + two * (FAR * d1)
        out[0] = square(v2, bands)
        out[1] = square(v3, bands)


def tail_rows(ref, plane, band, start, more):
    after = lax.rem(band + 1, ref.shape[1])
    return jnp.concatenate(
        [ref[plane, band, start:, :], ref[plane, after, :more, :]], axis=0
    )


def send_rows_kernel(part, psi, *outs):
    me = lax.axis_index("orb")
    for d, out in zip(offsets(psi.shape[1]), outs):
        for plane in range(psi.shape[0]):
            out[plane] = tail_rows(psi, plane, me ^ d, part[0] - 4, 4)


def gather_kernel(*refs):
    every, halo = refs[-2:]
    odd = parity()
    count = halo.shape[0] // (2 * (len(refs) - 3))
    for k, ref in enumerate(refs[:-2]):
        every[k] = ref[...]
        for q in range(2):
            if k:
                first = (2 * (k - 1) + q) * count
                halo[first : first + count, :] = ref[own(q, odd), 2 : 2 + count, :]


def rows_kernel(part, c, x, x_in, pot, pot_in, g, t, h):
    odd = parity()
    me = lax.axis_index("orb")
    at = [own(q, odd) for q in range(4)]
    base, one, two = c[0] - c[2], c[1], 2.0 * c[2]
    v = [tail_rows(pot, at[q], me, part[0] - 2, 2) for q in range(4)]
    v += [tail_rows(pot_in, at[q], me, part[0] - 2, 2) for q in range(2)]
    n = g.shape[2]

    def step(k, carry):
        e = [x[k, at[q]] for q in range(4)] + [x_in[k, at[q]] for q in range(4)]
        m = [y[2 : 2 + n] for y in e]
        g0 = apply_rows(e[0], v[0], m[1], m[2])
        g1 = apply_rows(e[1], v[1], m[0] + m[2], m[3])
        g[k, 0], g[k, 1] = g0, g1
        full = [apply_rows(e[q], v[q], m[q - 1] + m[q + 1], m[q - 2] + m[q + 2])
                for q in range(2, 6)]
        f = [y[2 : n - 2] for y in [g0, g1, *full]]
        for j in range(2):
            t[k, j] = f[2 + j]
            q = 2 + j
            s = apply_rows(full[j], v[q][2 : n - 2], f[q - 1] + f[q + 1], f[q - 2] + f[q + 2])
            h[k, j] = base * e[q][4 : n] + one * f[q] + two * s
        return carry

    lax.fori_loop(0, x.shape[0], step, 0)


def rows_halo(part, k, halo, first, second, n):
    if k:
        at = [(2 * (k - 1) + q) * n for q in range(2)]
        near, far = [halo[a : a + n, :] for a in at]
    else:
        odd = parity()
        me = lax.axis_index("orb")
        after = lax.rem(me + 1, first.shape[1])
        near, far = [
            jnp.concatenate(
                [second[q, me, second.shape[2] - (n - 2) :, :], first[q, after, :2, :]],
                axis=0,
            )
            for q in (1 - odd, odd)
        ]
    return NEAR * near + FAR * far, FAR * near


def rows_face_kernel(part, halo, first, second, g, f, send):
    n = g.shape[2]
    for k in range(g.shape[0]):
        terms = rows_halo(part, k, halo, first, second, n)
        for q in range(2):
            value = g[k, q] + terms[q]
            f[k, q] = value
            send[k, q] = value[2 : n - 2]


def rows_front_kernel(part, c, x, pot, halo, first, second, f, t, h, back, front):
    odd = parity()
    me = lax.axis_index("orb")
    base, one, two = c[0] - c[2], c[1], 2.0 * c[2]
    n = f.shape[2]
    v = [
        tail_rows(pot, own(q, odd), me, part[0] - 2, 2)[2 : n - 2] for q in range(2)
    ]
    total = [0.0, 0.0]
    count = f.shape[0]
    for k in range(count):
        d0, d1 = [y[2 : n - 2] for y in rows_halo(part, k, halo, first, second, n)]
        v2 = h[k, 0] + two * (NEAR * d1 + FAR * d0)
        v3 = h[k, 1] + two * (FAR * d1)
        total = [total[0] + square(v2, count), total[1] + square(v3, count)]
        f0, f1 = f[k, 0], f[k, 1]
        t2, t3 = t[k, 0], t[k, 1]
        m0, m1 = f0[2 : n - 2], f1[2 : n - 2]
        s0 = apply_rows(f0, v[0], m1, t2)
        s1 = apply_rows(f1, v[1], m0 + t2, t3)
        front[k, 0] = base * x[k, own(0, odd)][4:n] + one * m0 + two * s0
        front[k, 1] = base * x[k, own(1, odd)][4:n] + one * m1 + two * s1
    back[0], back[1] = total


def front_kernel(chunks, c, psi, pot, t, *rest):
    fs, h, scratch = rest[:-2], rest[-2], rest[-1]
    odd = parity()
    at = [own(q, odd) for q in range(2)]
    base, one, two = c[0] - c[2], c[1], 2.0 * c[2]
    rows = psi.shape[1]
    for (lo, hi), f in zip(chunks, fs):
        bands = f.shape[1]
        for band in range(bands):
            first_row = band * (rows // bands)
            for q in range(2):
                scratch[q, first_row + lo : first_row + hi, :] = f[q, band]

    def body(r):
        here = pl.ds(r, BLOCK)
        e0, e1 = with_halo(scratch, 0, r, BLOCK), with_halo(scratch, 1, r, BLOCK)
        t2, t3 = t[0, here, :], t[1, here, :]
        f0, s0 = apply_s(e0, pot[at[0], here, :], e1[8:-8], t2)
        f1, s1 = apply_s(e1, pot[at[1], here, :], e0[8:-8] + t2, t3)
        h[0, here, :] = base * psi[at[0], here, :] + one * f0 + two * s0
        h[1, here, :] = base * psi[at[1], here, :] + one * f1 + two * s1

    blocks(rows, body)


def last_kernel(chunk, row, halo, h, keep, send):
    lo, hi = chunk
    two = row[0:1, :]
    me = lax.axis_index("orb")
    bands = halo.shape[1]

    def part(band, out, slot):
        near, far = halo[0, band], halo[1, band]
        v0 = h[0, band, lo:hi, :] + two * (NEAR * near + FAR * far)
        v1 = h[1, band, lo:hi, :] + two * (FAR * near)
        out[slot, 0] = square(v0, bands)
        out[slot, 1] = square(v1, bands)

    part(me ^ 1, send, 0)
    part(me ^ 2, send, 1)
    part(me, keep, 0)
    part(me ^ 3, keep, 1)


def add_kernel(keep, came, out):
    out[...] = keep[1] + came[1]


def sum_kernel(keep, came, far, out):
    out[...] = keep[0] + came[0] + far[...]


def sum_all_kernel(*refs):
    total = refs[0][...]
    for ref in refs[1:-1]:
        total = total + ref[...]
    refs[-1][...] = total


def join_kernel(places, part, *refs):
    row, halo, h, out = refs[-4:]
    odd = parity()
    for (q, (lo, hi)), ref in zip(places, refs):
        for j in range(2):
            out[own(q + j, odd), lo:hi, :] = ref[j]
    two = row[0:1, :]
    count = h.shape[0]
    total = [0.0, 0.0]
    for k in range(count):
        near, far = halo[k, 0], halo[k, 1]
        v0 = h[k, 0] + two * (NEAR * near + FAR * far)
        v1 = h[k, 1] + two * (FAR * near)
        total = [total[0] + square(v0, count), total[1] + square(v1, count)]
    for j in range(2):
        out[own(j, odd), part[0] : part[1], :] = total[j]


class Line:
    def __init__(self):
        self.last = []

    def __call__(self, kernel, out, args, scalars=0, scratch=(), flops=0, hbm=False, weight=0):
        vmem = pl.BlockSpec(memory_space=pltpu.VMEM)
        smem = pl.BlockSpec(memory_space=pltpu.SMEM)
        many = isinstance(out, list)
        shapes = [jax.ShapeDtypeStruct(s, jnp.float32) for s in (out if many else [out])]
        total = sum(4 * int(x.size) for x in list(args) + shapes)
        first, last = len(args), self.last

        def body(*refs):
            kernel(*refs[:first], *refs[first + len(last) :])

        result = pl.pallas_call(
            body,
            out_shape=shapes,
            in_specs=[smem] * scalars
            + [pl.BlockSpec(memory_space=pltpu.HBM) if hbm else vmem] * (first - scalars)
            + [pl.BlockSpec(memory_space=pl.ANY)] * len(last),
            out_specs=[vmem] * len(shapes),
            scratch_shapes=list(scratch),
            compiler_params=pltpu.CompilerParams(vmem_limit_bytes=40 * 2**20),
            cost_estimate=pl.CostEstimate(
                flops=flops + weight, bytes_accessed=total, transcendentals=0
            ),
        )(*args, *last)
        self.last = [result[0]]
        return result if many else result[0]


def shards(orbitals, potential, coeffs):
    psi = orbitals[0]
    slabs, bands = lax.axis_size("slab"), lax.axis_size("orb")
    planes, rows, lanes = psi.shape
    wide = rows // bands
    half, part = wide // 2, wide // 4
    chunk = (0, wide)
    cuts = [(0, half), (half, wide - part), (wide - part, wide)]
    cut_a, cut_b, cut_c = cuts
    padded, inner = (part + 8, part + 4)
    face = [(s, (s - 1 if s % 2 == 0 else s + 1) % slabs) for s in range(slabs)]
    partner = [(s, s ^ 1) for s in range(slabs)]
    near = [(i, i ^ 1) for i in range(bands)]
    far = [(i, i ^ 3) for i in range(bands)]
    plane2 = (2, rows, lanes)
    cells = 2 * rows * lanes
    call = Line()

    def as_bands(x):
        return x.reshape(x.shape[0], bands, wide, lanes)

    def slab_shape(chunk):
        return (2, bands, chunk[1] - chunk[0], lanes)

    def pair_shape(chunk):
        return (2, 2, chunk[1] - chunk[0], lanes)

    def add_far(keep, came):
        total = call(add_kernel, keep.shape[1:], (keep, came))
        return keep, came, lax.ppermute(total, "orb", far)

    def squares(cut, halo):
        keep, send = call(
            functools.partial(last_kernel, cut),
            [pair_shape(cut)] * 2,
            (row, halo, as_bands(h_front)),
        )
        return keep, lax.ppermute(send, "orb", near)

    def over_orb(x, d):
        return lax.ppermute(x, "orb", [(i, i ^ d) for i in range(bands)])

    def back_squares(rows):
        keep, *sends = call(
            functools.partial(back_kernel, rows),
            [pair_shape(rows)[1:]] * bands,
            (row, halo, as_bands(h_back)),
        )
        return keep, *[over_orb(x, d) for d, x in zip(offsets(bands)[1:], sends)]

    def sum_all(keep, *came, weight=0):
        return call(sum_all_kernel, keep.shape, (keep, *came), weight=weight)

    psi_in = lax.ppermute(psi, "slab", partner)
    pot_in = lax.ppermute(potential, "slab", partner)
    piece = call(
        functools.partial(pack_kernel, chunk),
        slab_shape(chunk),
        (as_bands(psi),),
        scratch=[pltpu.SemaphoreType.DMA],
        hbm=True,
    )
    halo = lax.ppermute(piece, "slab", face)
    keep, *sends = call(
        functools.partial(send_rows_kernel, cut_c),
        [(planes, padded, lanes)] * bands,
        (as_bands(psi),),
    )
    x_parts = [keep, *[over_orb(x, d) for d, x in zip(offsets(bands)[1:], sends)]]
    g = call(start_kernel, plane2, (psi, potential), flops=24 * cells)
    t, h_back, row = call(
        inner_kernel,
        [plane2, plane2, (8, lanes)],
        (coeffs, psi, potential, psi_in, pot_in, g),
        scalars=1,
        flops=80 * cells,
    )

    def summed(keep, came, from_far, weight=0):
        return call(sum_kernel, from_far.shape, (keep, came, from_far), weight=weight)

    x, piece = call(
        gather_kernel,
        [(bands, planes, padded, lanes), (2 * (bands - 1) * inner, lanes)],
        x_parts,
    )
    x_in = lax.ppermute(x, "slab", partner)
    x_halo = lax.ppermute(piece, "slab", face)
    fs = call(
        functools.partial(face_kernel, chunk, cuts),
        [slab_shape(cut) for cut in cuts],
        (halo, as_bands(g)),
    )
    face_a, face_b = [lax.ppermute(f, "slab", face) for f in fs[:2]]
    back0 = back_squares((0, wide - part))
    x_first, x_t, x_back = call(
        functools.partial(rows_kernel, cut_c),
        [(bands, 2, inner, lanes)] + [(bands, 2, part, lanes)] * 2,
        (coeffs, x, x_in, as_bands(potential), as_bands(pot_in)),
        scalars=1,
    )
    x_f, piece = call(
        functools.partial(rows_face_kernel, cut_c),
        [(bands, 2, inner, lanes), (bands, 2, part, lanes)],
        (x_halo, halo, halo, x_first),
    )
    x_face = lax.ppermute(piece, "slab", face)
    h_front = call(
        functools.partial(front_kernel, cuts),
        plane2,
        (coeffs, psi, potential, t, *fs),
        scalars=1,
        scratch=[pltpu.VMEM(plane2, jnp.float32)],
        flops=40 * cells,
        weight=4_000_000_000,
    )
    back2, x_front = call(
        functools.partial(rows_front_kernel, cut_c),
        [(2, part, lanes), (bands, 2, part, lanes)],
        (coeffs, x, as_bands(potential), x_halo, halo, halo, x_f, x_t, x_back),
        scalars=1,
    )
    front_a = squares(cut_a, face_a)
    back0 = sum_all(*back0, weight=1_000_000_000)
    front_b = squares(cut_b, face_b)
    front_a = add_far(*front_a)
    front_b = add_far(*front_b)
    front_a = summed(*front_a)
    front_b = summed(*front_b)
    places = [(2, (0, wide - part)), (2, cut_c), (0, cut_a), (0, cut_b)]
    return call(
        functools.partial(join_kernel, places, cut_c),
        (planes, wide, lanes),
        (back0, back2, front_a, front_b, row, x_face, x_front),
    )


def solution(mesh):
    return jax.shard_map(
        shards,
        mesh=mesh,
        in_specs=(P("orb", "slab", None, None), P("slab", None, None), P()),
        out_specs=P("slab", "orb", None),
        check_vma=False,
    )
```

```python
import functools

import jax
import jax.numpy as jnp
from jax import lax
from jax.experimental import pallas as pl
from jax.experimental.pallas import tpu as pltpu
from jax.sharding import PartitionSpec as P

NEAR = -2.0 / 15.0
FAR = 1.0 / 120.0
BLOCK = 16


def own(q, odd):
    return jnp.where(odd == 1, 3 - q, q)


def parity():
    return lax.rem(lax.axis_index("slab"), 2)


def with_halo(ref, plane, start, count):
    rows = ref.shape[-2]
    before = pl.multiple_of(lax.rem(start + rows - 8, rows), 8)
    after = pl.multiple_of(lax.rem(start + count, rows), 8)
    return jnp.concatenate(
        [
            ref[plane, pl.ds(before, 8), :],
            ref[plane, pl.ds(start, count), :],
            ref[plane, pl.ds(after, 8), :],
        ],
        axis=0,
    )


def in_plane(ext):
    count, lanes = ext.shape[0] - 16, ext.shape[1]
    mid = ext[8 : 8 + count]
    near = ext[7 : 7 + count] + ext[9 : 9 + count]
    near = near + (pltpu.roll(mid, 1, 1) + pltpu.roll(mid, lanes - 1, 1))
    far = ext[6 : 6 + count] + ext[10 : 10 + count]
    far = far + (pltpu.roll(mid, 2, 1) + pltpu.roll(mid, lanes - 2, 1))
    return mid, near, far


def apply_s(ext, pot, near_z, far_z):
    mid, near, far = in_plane(ext)
    return mid, (
        mid * (0.2 * pot - 0.05) + NEAR * (near + near_z) + FAR * (far + far_z)
    )


def apply_rows(e, pot, near_z, far_z):
    count, lanes = e.shape[0] - 4, e.shape[1]
    mid = e[2 : 2 + count]
    near = e[1 : 1 + count] + e[3 : 3 + count]
    near = near + (pltpu.roll(mid, 1, 1) + pltpu.roll(mid, lanes - 1, 1))
    far = e[0:count] + e[4 : 4 + count]
    far = far + (pltpu.roll(mid, 2, 1) + pltpu.roll(mid, lanes - 2, 1))
    return mid * (0.2 * pot - 0.05) + NEAR * (near + near_z) + FAR * (far + far_z)


def blocks(rows, body):
    def step(i, carry):
        body(pl.multiple_of(i * BLOCK, BLOCK))
        return carry

    lax.fori_loop(0, rows // BLOCK, step, 0)


def pack_kernel(chunk, psi, out, sem):
    lo, hi = chunk
    planes = pl.ds(2 * parity(), out.shape[0])
    copy = pltpu.make_async_copy(psi.at[planes, :, pl.ds(lo, hi - lo), :], out, sem)
    copy.start()
    copy.wait()


def start_kernel(psi, pot, g):
    odd = parity()

    def body(r):
        here = pl.ds(r, BLOCK)
        at = [own(q, odd) for q in range(4)]
        e0, e1 = with_halo(psi, at[0], r, BLOCK), with_halo(psi, at[1], r, BLOCK)
        p2, p3 = psi[at[2], here, :], psi[at[3], here, :]
        g[0, here, :] = apply_s(e0, pot[at[0], here, :], e1[8:-8], p2)[1]
        g[1, here, :] = apply_s(e1, pot[at[1], here, :], e0[8:-8] + p2, p3)[1]

    blocks(psi.shape[1], body)


def inner_kernel(c, psi, pot, psi_in, pot_in, g, t, h, row):
    odd = parity()
    at = [own(q, odd) for q in range(4)]
    base, one, two = c[0] - c[2], c[1], 2.0 * c[2]

    def first(r):
        here = pl.ds(r, BLOCK)
        e2, e3 = with_halo(psi, at[2], r, BLOCK), with_halo(psi, at[3], r, BLOCK)
        p0, p1 = psi[at[0], here, :], psi[at[1], here, :]
        p4, p5 = psi_in[at[0], here, :], psi_in[at[1], here, :]
        t[0, here, :] = apply_s(e2, pot[at[2], here, :], p1 + e3[8:-8], p0 + p4)[1]
        t[1, here, :] = apply_s(e3, pot[at[3], here, :], e2[8:-8] + p4, p1 + p5)[1]

    def second(r):
        here = pl.ds(r, BLOCK)
        e4 = with_halo(psi_in, at[0], r, BLOCK)
        e5 = with_halo(psi_in, at[1], r, BLOCK)
        p2, p3 = psi[at[2], here, :], psi[at[3], here, :]
        p6, p7 = psi_in[at[2], here, :], psi_in[at[3], here, :]
        t4 = apply_s(e4, pot_in[at[0], here, :], p3 + e5[8:-8], p2 + p6)[1]
        t5 = apply_s(e5, pot_in[at[1], here, :], e4[8:-8] + p6, p3 + p7)[1]
        g0, g1 = g[0, here, :], g[1, here, :]
        e2, e3 = with_halo(t, 0, r, BLOCK), with_halo(t, 1, r, BLOCK)
        t2, s2 = apply_s(e2, pot[at[2], here, :], g1 + e3[8:-8], g0 + t4)
        t3, s3 = apply_s(e3, pot[at[3], here, :], e2[8:-8] + t4, g1 + t5)
        h[0, here, :] = base * p2 + one * t2 + two * s2
        h[1, here, :] = base * p3 + one * t3 + two * s3

    row[...] = jnp.full(row.shape, two)
    blocks(psi.shape[1], first)
    blocks(psi.shape[1], second)


def halo_terms(halo, band, odd, rows=slice(None)):
    near, far = halo[1 - odd, band, rows, :], halo[odd, band, rows, :]
    return NEAR * near + FAR * far, FAR * near


def square(x, bands):
    return x * x * (1.0 / bands)


def face_kernel(chunk, parts, halo, g, *fs):
    odd = parity()
    lo, hi = chunk
    for (first, last), f in zip(parts, fs):
        in_halo = slice(first - lo, last - lo)
        for band in range(halo.shape[1]):
            d0, d1 = halo_terms(halo, band, odd, in_halo)
            f[0, band] = g[0, band, first:last, :] + d0
            f[1, band] = g[1, band, first:last, :] + d1


def offsets(bands):
    return [0, *range(bands - 1, 0, -1)]


def back_kernel(part, row, halo, h, *outs):
    odd = parity()
    lo, hi = part
    two = row[0:1, :]
    me = lax.axis_index("orb")
    bands = halo.shape[1]
    for d, out in zip(offsets(bands), outs):
        band = me ^ d
        d0, d1 = halo_terms(halo, band, odd, slice(lo, hi))
        v2 = h[0, band, lo:hi, :] + two * (NEAR * d1 + FAR * d0)
        v3 = h[1, band, lo:hi, :] + two * (FAR * d1)
        out[0] = square(v2, bands)
        out[1] = square(v3, bands)


def tail_rows(ref, plane, band, start, more):
    after = lax.rem(band + 1, ref.shape[1])
    return jnp.concatenate(
        [ref[plane, band, start:, :], ref[plane, after, :more, :]], axis=0
    )


def send_rows_kernel(part, psi, *outs):
    me = lax.axis_index("orb")
    for d, out in zip(offsets(psi.shape[1]), outs):
        for plane in range(psi.shape[0]):
            out[plane] = tail_rows(psi, plane, me ^ d, part[0] - 4, 4)


def gather_kernel(*refs):
    every, halo = refs[-2:]
    odd = parity()
    count = halo.shape[0] // (2 * (len(refs) - 3))
    for k, ref in enumerate(refs[:-2]):
        every[k] = ref[...]
        for q in range(2):
            if k:
                first = (2 * (k - 1) + q) * count
                halo[first : first + count, :] = ref[own(q, odd), 2 : 2 + count, :]


def rows_kernel(part, c, x, x_in, pot, pot_in, g, t, h):
    odd = parity()
    me = lax.axis_index("orb")
    at = [own(q, odd) for q in range(4)]
    base, one, two = c[0] - c[2], c[1], 2.0 * c[2]
    v = [tail_rows(pot, at[q], me, part[0] - 2, 2) for q in range(4)]
    v += [tail_rows(pot_in, at[q], me, part[0] - 2, 2) for q in range(2)]
    n = g.shape[2]

    def step(k, carry):
        e = [x[k, at[q]] for q in range(4)] + [x_in[k, at[q]] for q in range(4)]
        m = [y[2 : 2 + n] for y in e]
        g0 = apply_rows(e[0], v[0], m[1], m[2])
        g1 = apply_rows(e[1], v[1], m[0] + m[2], m[3])
        g[k, 0], g[k, 1] = g0, g1
        full = [apply_rows(e[q], v[q], m[q - 1] + m[q + 1], m[q - 2] + m[q + 2])
                for q in range(2, 6)]
        f = [y[2 : n - 2] for y in [g0, g1, *full]]
        for j in range(2):
            t[k, j] = f[2 + j]
            q = 2 + j
            s = apply_rows(full[j], v[q][2 : n - 2], f[q - 1] + f[q + 1], f[q - 2] + f[q + 2])
            h[k, j] = base * e[q][4 : n] + one * f[q] + two * s
        return carry

    lax.fori_loop(0, x.shape[0], step, 0)


def rows_halo(part, k, halo, first, second, n):
    if k:
        at = [(2 * (k - 1) + q) * n for q in range(2)]
        near, far = [halo[a : a + n, :] for a in at]
    else:
        odd = parity()
        me = lax.axis_index("orb")
        after = lax.rem(me + 1, first.shape[1])
        near, far = [
            jnp.concatenate(
                [second[q, me, second.shape[2] - (n - 2) :, :], first[q, after, :2, :]],
                axis=0,
            )
            for q in (1 - odd, odd)
        ]
    return NEAR * near + FAR * far, FAR * near


def rows_face_kernel(part, halo, first, second, g, f, send):
    n = g.shape[2]
    for k in range(g.shape[0]):
        terms = rows_halo(part, k, halo, first, second, n)
        for q in range(2):
            value = g[k, q] + terms[q]
            f[k, q] = value
            send[k, q] = value[2 : n - 2]


def rows_front_kernel(part, c, x, pot, halo, first, second, f, t, h, back, front):
    odd = parity()
    me = lax.axis_index("orb")
    base, one, two = c[0] - c[2], c[1], 2.0 * c[2]
    n = f.shape[2]
    v = [
        tail_rows(pot, own(q, odd), me, part[0] - 2, 2)[2 : n - 2] for q in range(2)
    ]
    total = [0.0, 0.0]
    count = f.shape[0]
    for k in range(count):
        d0, d1 = [y[2 : n - 2] for y in rows_halo(part, k, halo, first, second, n)]
        v2 = h[k, 0] + two * (NEAR * d1 + FAR * d0)
        v3 = h[k, 1] + two * (FAR * d1)
        total = [total[0] + square(v2, count), total[1] + square(v3, count)]
        f0, f1 = f[k, 0], f[k, 1]
        t2, t3 = t[k, 0], t[k, 1]
        m0, m1 = f0[2 : n - 2], f1[2 : n - 2]
        s0 = apply_rows(f0, v[0], m1, t2)
        s1 = apply_rows(f1, v[1], m0 + t2, t3)
        front[k, 0] = base * x[k, own(0, odd)][4:n] + one * m0 + two * s0
        front[k, 1] = base * x[k, own(1, odd)][4:n] + one * m1 + two * s1
    back[0], back[1] = total


def front_kernel(chunks, c, psi, pot, t, *rest):
    fs, h, scratch = rest[:-2], rest[-2], rest[-1]
    odd = parity()
    at = [own(q, odd) for q in range(2)]
    base, one, two = c[0] - c[2], c[1], 2.0 * c[2]
    rows = psi.shape[1]
    for (lo, hi), f in zip(chunks, fs):
        bands = f.shape[1]
        for band in range(bands):
            first_row = band * (rows // bands)
            for q in range(2):
                scratch[q, first_row + lo : first_row + hi, :] = f[q, band]

    def body(r):
        here = pl.ds(r, BLOCK)
        e0, e1 = with_halo(scratch, 0, r, BLOCK), with_halo(scratch, 1, r, BLOCK)
        t2, t3 = t[0, here, :], t[1, here, :]
        f0, s0 = apply_s(e0, pot[at[0], here, :], e1[8:-8], t2)
        f1, s1 = apply_s(e1, pot[at[1], here, :], e0[8:-8] + t2, t3)
        h[0, here, :] = base * psi[at[0], here, :] + one * f0 + two * s0
        h[1, here, :] = base * psi[at[1], here, :] + one * f1 + two * s1

    blocks(rows, body)


def last_kernel(chunk, row, halo, h, keep, send):
    lo, hi = chunk
    two = row[0:1, :]
    me = lax.axis_index("orb")
    bands = halo.shape[1]

    def part(band, out, slot):
        near, far = halo[0, band], halo[1, band]
        v0 = h[0, band, lo:hi, :] + two * (NEAR * near + FAR * far)
        v1 = h[1, band, lo:hi, :] + two * (FAR * near)
        out[slot, 0] = square(v0, bands)
        out[slot, 1] = square(v1, bands)

    part(me ^ 1, send, 0)
    part(me ^ 2, send, 1)
    part(me, keep, 0)
    part(me ^ 3, keep, 1)


def add_kernel(keep, came, out):
    out[...] = keep[1] + came[1]


def sum_kernel(keep, came, far, out):
    out[...] = keep[0] + came[0] + far[...]


def sum_all_kernel(*refs):
    total = refs[0][...]
    for ref in refs[1:-1]:
        total = total + ref[...]
    refs[-1][...] = total


def join_kernel(places, part, *refs):
    row, halo, h, out = refs[-4:]
    odd = parity()
    for (q, (lo, hi)), ref in zip(places, refs):
        for j in range(2):
            out[own(q + j, odd), lo:hi, :] = ref[j]
    two = row[0:1, :]
    count = h.shape[0]
    total = [0.0, 0.0]
    for k in range(count):
        near, far = halo[k, 0], halo[k, 1]
        v0 = h[k, 0] + two * (NEAR * near + FAR * far)
        v1 = h[k, 1] + two * (FAR * near)
        total = [total[0] + square(v0, count), total[1] + square(v1, count)]
    for j in range(2):
        out[own(j, odd), part[0] : part[1], :] = total[j]


class Line:
    def __init__(self):
        self.last = []

    def __call__(self, kernel, out, args, scalars=0, scratch=(), flops=0, hbm=False, weight=0):
        vmem = pl.BlockSpec(memory_space=pltpu.VMEM)
        smem = pl.BlockSpec(memory_space=pltpu.SMEM)
        many = isinstance(out, list)
        shapes = [jax.ShapeDtypeStruct(s, jnp.float32) for s in (out if many else [out])]
        total = sum(4 * int(x.size) for x in list(args) + shapes)
        first, last = len(args), self.last

        def body(*refs):
            kernel(*refs[:first], *refs[first + len(last) :])

        result = pl.pallas_call(
            body,
            out_shape=shapes,
            in_specs=[smem] * scalars
            + [pl.BlockSpec(memory_space=pltpu.HBM) if hbm else vmem] * (first - scalars)
            + [pl.BlockSpec(memory_space=pl.ANY)] * len(last),
            out_specs=[vmem] * len(shapes),
            scratch_shapes=list(scratch),
            compiler_params=pltpu.CompilerParams(vmem_limit_bytes=40 * 2**20),
            cost_estimate=pl.CostEstimate(
                flops=flops + weight, bytes_accessed=total, transcendentals=0
            ),
        )(*args, *last)
        self.last = [result[0]]
        return result if many else result[0]


def shards(orbitals, potential, coeffs):
    psi = orbitals[0]
    slabs, bands = lax.axis_size("slab"), lax.axis_size("orb")
    planes, rows, lanes = psi.shape
    wide = rows // bands
    half, part = wide // 2, wide // 4
    chunk = (0, wide)
    cuts = [(0, half), (half, wide - part), (wide - part, wide)]
    cut_a, cut_b, cut_c = cuts
    padded, inner = (part + 8, part + 4)
    face = [(s, (s - 1 if s % 2 == 0 else s + 1) % slabs) for s in range(slabs)]
    partner = [(s, s ^ 1) for s in range(slabs)]
    near = [(i, i ^ 1) for i in range(bands)]
    far = [(i, i ^ 3) for i in range(bands)]
    plane2 = (2, rows, lanes)
    cells = 2 * rows * lanes
    call = Line()

    def as_bands(x):
        return x.reshape(x.shape[0], bands, wide, lanes)

    def slab_shape(chunk):
        return (2, bands, chunk[1] - chunk[0], lanes)

    def pair_shape(chunk):
        return (2, 2, chunk[1] - chunk[0], lanes)

    def add_far(keep, came):
        total = call(add_kernel, keep.shape[1:], (keep, came))
        return keep, came, lax.ppermute(total, "orb", far)

    def squares(cut, halo):
        keep, send = call(
            functools.partial(last_kernel, cut),
            [pair_shape(cut)] * 2,
            (row, halo, as_bands(h_front)),
        )
        return keep, lax.ppermute(send, "orb", near)

    def over_orb(x, d):
        return lax.ppermute(x, "orb", [(i, i ^ d) for i in range(bands)])

    def back_squares(rows):
        keep, *sends = call(
            functools.partial(back_kernel, rows),
            [pair_shape(rows)[1:]] * bands,
            (row, halo, as_bands(h_back)),
        )
        return keep, *[over_orb(x, d) for d, x in zip(offsets(bands)[1:], sends)]

    def sum_all(keep, *came, weight=0):
        return call(sum_all_kernel, keep.shape, (keep, *came), weight=weight)

    psi_in = lax.ppermute(psi, "slab", partner)
    pot_in = lax.ppermute(potential, "slab", partner)
    piece = call(
        functools.partial(pack_kernel, chunk),
        slab_shape(chunk),
        (as_bands(psi),),
        scratch=[pltpu.SemaphoreType.DMA],
        hbm=True,
    )
    halo = lax.ppermute(piece, "slab", face)
    keep, *sends = call(
        functools.partial(send_rows_kernel, cut_c),
        [(planes, padded, lanes)] * bands,
        (as_bands(psi),),
    )
    x_parts = [keep, *[over_orb(x, d) for d, x in zip(offsets(bands)[1:], sends)]]
    g = call(start_kernel, plane2, (psi, potential), flops=24 * cells)
    t, h_back, row = call(
        inner_kernel,
        [plane2, plane2, (8, lanes)],
        (coeffs, psi, potential, psi_in, pot_in, g),
        scalars=1,
        flops=80 * cells,
    )

    def summed(keep, came, from_far, weight=0):
        return call(sum_kernel, from_far.shape, (keep, came, from_far), weight=weight)

    x, piece = call(
        gather_kernel,
        [(bands, planes, padded, lanes), (2 * (bands - 1) * inner, lanes)],
        x_parts,
    )
    x_in = lax.ppermute(x, "slab", partner)
    x_halo = lax.ppermute(piece, "slab", face)
    back0 = back_squares((0, wide - part))
    fs = call(
        functools.partial(face_kernel, chunk, cuts),
        [slab_shape(cut) for cut in cuts],
        (halo, as_bands(g)),
    )
    face_a, face_b = [lax.ppermute(f, "slab", face) for f in fs[:2]]
    x_first, x_t, x_back = call(
        functools.partial(rows_kernel, cut_c),
        [(bands, 2, inner, lanes)] + [(bands, 2, part, lanes)] * 2,
        (coeffs, x, x_in, as_bands(potential), as_bands(pot_in)),
        scalars=1,
    )
    x_f, piece = call(
        functools.partial(rows_face_kernel, cut_c),
        [(bands, 2, inner, lanes), (bands, 2, part, lanes)],
        (x_halo, halo, halo, x_first),
    )
    x_face = lax.ppermute(piece, "slab", face)
    h_front = call(
        functools.partial(front_kernel, cuts),
        plane2,
        (coeffs, psi, potential, t, *fs),
        scalars=1,
        scratch=[pltpu.VMEM(plane2, jnp.float32)],
        flops=40 * cells,
        weight=4_000_000_000,
    )
    back2, x_front = call(
        functools.partial(rows_front_kernel, cut_c),
        [(2, part, lanes), (bands, 2, part, lanes)],
        (coeffs, x, as_bands(potential), x_halo, halo, halo, x_f, x_t, x_back),
        scalars=1,
    )
    back0 = sum_all(*back0, weight=3_000_000_000)
    front_a = squares(cut_a, face_a)
    front_b = squares(cut_b, face_b)
    front_a = add_far(*front_a)
    front_b = add_far(*front_b)
    front_a = summed(*front_a)
    front_b = summed(*front_b)
    places = [(2, (0, wide - part)), (2, cut_c), (0, cut_a), (0, cut_b)]
    return call(
        functools.partial(join_kernel, places, cut_c),
        (planes, wide, lanes),
        (back0, back2, front_a, front_b, row, x_face, x_front),
    )


def solution(mesh):
    return jax.shard_map(
        shards,
        mesh=mesh,
        in_specs=(P("orb", "slab", None, None), P("slab", None, None), P()),
        out_specs=P("slab", "orb", None),
        check_vma=False,
    )
```

```python
import functools

import jax
import jax.numpy as jnp
from jax import lax
from jax.experimental import pallas as pl
from jax.experimental.pallas import tpu as pltpu
from jax.sharding import PartitionSpec as P

NEAR = -2.0 / 15.0
FAR = 1.0 / 120.0
BLOCK = 16


def own(q, odd):
    return jnp.where(odd == 1, 3 - q, q)


def parity():
    return lax.rem(lax.axis_index("slab"), 2)


def with_halo(ref, plane, start, count):
    rows = ref.shape[-2]
    before = pl.multiple_of(lax.rem(start + rows - 8, rows), 8)
    after = pl.multiple_of(lax.rem(start + count, rows), 8)
    return jnp.concatenate(
        [
            ref[plane, pl.ds(before, 8), :],
            ref[plane, pl.ds(start, count), :],
            ref[plane, pl.ds(after, 8), :],
        ],
        axis=0,
    )


def in_plane(ext):
    count, lanes = ext.shape[0] - 16, ext.shape[1]
    mid = ext[8 : 8 + count]
    near = ext[7 : 7 + count] + ext[9 : 9 + count]
    near = near + (pltpu.roll(mid, 1, 1) + pltpu.roll(mid, lanes - 1, 1))
    far = ext[6 : 6 + count] + ext[10 : 10 + count]
    far = far + (pltpu.roll(mid, 2, 1) + pltpu.roll(mid, lanes - 2, 1))
    return mid, near, far


def apply_s(ext, pot, near_z, far_z):
    mid, near, far = in_plane(ext)
    return mid, (
        mid * (0.2 * pot - 0.05) + NEAR * (near + near_z) + FAR * (far + far_z)
    )


def apply_rows(e, pot, near_z, far_z):
    count, lanes = e.shape[0] - 4, e.shape[1]
    mid = e[2 : 2 + count]
    near = e[1 : 1 + count] + e[3 : 3 + count]
    near = near + (pltpu.roll(mid, 1, 1) + pltpu.roll(mid, lanes - 1, 1))
    far = e[0:count] + e[4 : 4 + count]
    far = far + (pltpu.roll(mid, 2, 1) + pltpu.roll(mid, lanes - 2, 1))
    return mid * (0.2 * pot - 0.05) + NEAR * (near + near_z) + FAR * (far + far_z)


def blocks(rows, body):
    def step(i, carry):
        body(pl.multiple_of(i * BLOCK, BLOCK))
        return carry

    lax.fori_loop(0, rows // BLOCK, step, 0)


def pack_kernel(chunk, psi, out, sem):
    lo, hi = chunk
    planes = pl.ds(2 * parity(), out.shape[0])
    copy = pltpu.make_async_copy(psi.at[planes, :, pl.ds(lo, hi - lo), :], out, sem)
    copy.start()
    copy.wait()


def start_kernel(psi, pot, g):
    odd = parity()

    def body(r):
        here = pl.ds(r, BLOCK)
        at = [own(q, odd) for q in range(4)]
        e0, e1 = with_halo(psi, at[0], r, BLOCK), with_halo(psi, at[1], r, BLOCK)
        p2, p3 = psi[at[2], here, :], psi[at[3], here, :]
        g[0, here, :] = apply_s(e0, pot[at[0], here, :], e1[8:-8], p2)[1]
        g[1, here, :] = apply_s(e1, pot[at[1], here, :], e0[8:-8] + p2, p3)[1]

    blocks(psi.shape[1], body)


def inner_kernel(c, psi, pot, psi_in, pot_in, g, t, h, row):
    odd = parity()
    at = [own(q, odd) for q in range(4)]
    base, one, two = c[0] - c[2], c[1], 2.0 * c[2]

    def first(r):
        here = pl.ds(r, BLOCK)
        e2, e3 = with_halo(psi, at[2], r, BLOCK), with_halo(psi, at[3], r, BLOCK)
        p0, p1 = psi[at[0], here, :], psi[at[1], here, :]
        p4, p5 = psi_in[at[0], here, :], psi_in[at[1], here, :]
        t[0, here, :] = apply_s(e2, pot[at[2], here, :], p1 + e3[8:-8], p0 + p4)[1]
        t[1, here, :] = apply_s(e3, pot[at[3], here, :], e2[8:-8] + p4, p1 + p5)[1]

    def second(r):
        here = pl.ds(r, BLOCK)
        e4 = with_halo(psi_in, at[0], r, BLOCK)
        e5 = with_halo(psi_in, at[1], r, BLOCK)
        p2, p3 = psi[at[2], here, :], psi[at[3], here, :]
        p6, p7 = psi_in[at[2], here, :], psi_in[at[3], here, :]
        t4 = apply_s(e4, pot_in[at[0], here, :], p3 + e5[8:-8], p2 + p6)[1]
        t5 = apply_s(e5, pot_in[at[1], here, :], e4[8:-8] + p6, p3 + p7)[1]
        g0, g1 = g[0, here, :], g[1, here, :]
        e2, e3 = with_halo(t, 0, r, BLOCK), with_halo(t, 1, r, BLOCK)
        t2, s2 = apply_s(e2, pot[at[2], here, :], g1 + e3[8:-8], g0 + t4)
        t3, s3 = apply_s(e3, pot[at[3], here, :], e2[8:-8] + t4, g1 + t5)
        h[0, here, :] = base * p2 + one * t2 + two * s2
        h[1, here, :] = base * p3 + one * t3 + two * s3

    row[...] = jnp.full(row.shape, two)
    blocks(psi.shape[1], first)
    blocks(psi.shape[1], second)


def halo_terms(halo, band, odd, rows=slice(None)):
    near, far = halo[1 - odd, band, rows, :], halo[odd, band, rows, :]
    return NEAR * near + FAR * far, FAR * near


def square(x, bands):
    return x * x * (1.0 / bands)


def face_kernel(chunk, parts, halo, g, *fs):
    odd = parity()
    lo, hi = chunk
    for (first, last), f in zip(parts, fs):
        in_halo = slice(first - lo, last - lo)
        for band in range(halo.shape[1]):
            d0, d1 = halo_terms(halo, band, odd, in_halo)
            f[0, band] = g[0, band, first:last, :] + d0
            f[1, band] = g[1, band, first:last, :] + d1


def offsets(bands):
    return [0, *range(bands - 1, 0, -1)]


def back_kernel(chunk, part, row, halo, h, keep, send):
    odd = parity()
    lo, hi = part
    in_halo = slice(lo - chunk[0], hi - chunk[0])
    two = row[0:1, :]
    me = lax.axis_index("orb")
    bands = halo.shape[1]

    def put(band, out, slot):
        d0, d1 = halo_terms(halo, band, odd, in_halo)
        v2 = h[0, band, lo:hi, :] + two * (NEAR * d1 + FAR * d0)
        v3 = h[1, band, lo:hi, :] + two * (FAR * d1)
        out[slot, 0] = square(v2, bands)
        out[slot, 1] = square(v3, bands)

    put(me ^ 1, send, 0)
    put(me ^ 2, send, 1)
    put(me, keep, 0)
    put(me ^ 3, keep, 1)


def tail_rows(ref, plane, band, start, more):
    after = lax.rem(band + 1, ref.shape[1])
    return jnp.concatenate(
        [ref[plane, band, start:, :], ref[plane, after, :more, :]], axis=0
    )


def send_rows_kernel(part, psi, *outs):
    me = lax.axis_index("orb")
    for d, out in zip(offsets(psi.shape[1]), outs):
        for plane in range(psi.shape[0]):
            out[plane] = tail_rows(psi, plane, me ^ d, part[0] - 4, 4)


def gather_kernel(*refs):
    every, halo = refs[-2:]
    odd = parity()
    count = halo.shape[0] // (2 * (len(refs) - 3))
    for k, ref in enumerate(refs[:-2]):
        every[k] = ref[...]
        for q in range(2):
            if k:
                first = (2 * (k - 1) + q) * count
                halo[first : first + count, :] = ref[own(q, odd), 2 : 2 + count, :]


def rows_kernel(part, c, x, x_in, pot, pot_in, g, t, h):
    odd = parity()
    me = lax.axis_index("orb")
    at = [own(q, odd) for q in range(4)]
    base, one, two = c[0] - c[2], c[1], 2.0 * c[2]
    v = [tail_rows(pot, at[q], me, part[0] - 2, 2) for q in range(4)]
    v += [tail_rows(pot_in, at[q], me, part[0] - 2, 2) for q in range(2)]
    n = g.shape[2]

    def step(k, carry):
        e = [x[k, at[q]] for q in range(4)] + [x_in[k, at[q]] for q in range(4)]
        m = [y[2 : 2 + n] for y in e]
        g0 = apply_rows(e[0], v[0], m[1], m[2])
        g1 = apply_rows(e[1], v[1], m[0] + m[2], m[3])
        g[k, 0], g[k, 1] = g0, g1
        full = [apply_rows(e[q], v[q], m[q - 1] + m[q + 1], m[q - 2] + m[q + 2])
                for q in range(2, 6)]
        f = [y[2 : n - 2] for y in [g0, g1, *full]]
        for j in range(2):
            t[k, j] = f[2 + j]
            q = 2 + j
            s = apply_rows(full[j], v[q][2 : n - 2], f[q - 1] + f[q + 1], f[q - 2] + f[q + 2])
            h[k, j] = base * e[q][4 : n] + one * f[q] + two * s
        return carry

    lax.fori_loop(0, x.shape[0], step, 0)


def rows_halo(part, k, halo, first, second, n):
    if k:
        at = [(2 * (k - 1) + q) * n for q in range(2)]
        near, far = [halo[a : a + n, :] for a in at]
    else:
        odd = parity()
        me = lax.axis_index("orb")
        after = lax.rem(me + 1, first.shape[1])
        near, far = [
            jnp.concatenate(
                [second[q, me, second.shape[2] - (n - 2) :, :], first[q, after, :2, :]],
                axis=0,
            )
            for q in (1 - odd, odd)
        ]
    return NEAR * near + FAR * far, FAR * near


def rows_face_kernel(part, halo, first, second, g, f, send):
    n = g.shape[2]
    for k in range(g.shape[0]):
        terms = rows_halo(part, k, halo, first, second, n)
        for q in range(2):
            value = g[k, q] + terms[q]
            f[k, q] = value
            send[k, q] = value[2 : n - 2]


def rows_front_kernel(part, c, x, pot, halo, first, second, f, t, h, back, front):
    odd = parity()
    me = lax.axis_index("orb")
    base, one, two = c[0] - c[2], c[1], 2.0 * c[2]
    n = f.shape[2]
    v = [
        tail_rows(pot, own(q, odd), me, part[0] - 2, 2)[2 : n - 2] for q in range(2)
    ]
    total = [0.0, 0.0]
    count = f.shape[0]
    for k in range(count):
        d0, d1 = [y[2 : n - 2] for y in rows_halo(part, k, halo, first, second, n)]
        v2 = h[k, 0] + two * (NEAR * d1 + FAR * d0)
        v3 = h[k, 1] + two * (FAR * d1)
        total = [total[0] + square(v2, count), total[1] + square(v3, count)]
        f0, f1 = f[k, 0], f[k, 1]
        t2, t3 = t[k, 0], t[k, 1]
        m0, m1 = f0[2 : n - 2], f1[2 : n - 2]
        s0 = apply_rows(f0, v[0], m1, t2)
        s1 = apply_rows(f1, v[1], m0 + t2, t3)
        front[k, 0] = base * x[k, own(0, odd)][4:n] + one * m0 + two * s0
        front[k, 1] = base * x[k, own(1, odd)][4:n] + one * m1 + two * s1
    back[0], back[1] = total


def front_kernel(chunks, c, psi, pot, t, *rest):
    fs, h, scratch = rest[:-2], rest[-2], rest[-1]
    odd = parity()
    at = [own(q, odd) for q in range(2)]
    base, one, two = c[0] - c[2], c[1], 2.0 * c[2]
    rows = psi.shape[1]
    for (lo, hi), f in zip(chunks, fs):
        bands = f.shape[1]
        for band in range(bands):
            first_row = band * (rows // bands)
            for q in range(2):
                scratch[q, first_row + lo : first_row + hi, :] = f[q, band]

    def body(r):
        here = pl.ds(r, BLOCK)
        e0, e1 = with_halo(scratch, 0, r, BLOCK), with_halo(scratch, 1, r, BLOCK)
        t2, t3 = t[0, here, :], t[1, here, :]
        f0, s0 = apply_s(e0, pot[at[0], here, :], e1[8:-8], t2)
        f1, s1 = apply_s(e1, pot[at[1], here, :], e0[8:-8] + t2, t3)
        h[0, here, :] = base * psi[at[0], here, :] + one * f0 + two * s0
        h[1, here, :] = base * psi[at[1], here, :] + one * f1 + two * s1

    blocks(rows, body)


def last_kernel(chunk, row, halo, h, keep, send):
    lo, hi = chunk
    two = row[0:1, :]
    me = lax.axis_index("orb")
    bands = halo.shape[1]

    def part(band, out, slot):
        near, far = halo[0, band], halo[1, band]
        v0 = h[0, band, lo:hi, :] + two * (NEAR * near + FAR * far)
        v1 = h[1, band, lo:hi, :] + two * (FAR * near)
        out[slot, 0] = square(v0, bands)
        out[slot, 1] = square(v1, bands)

    part(me ^ 1, send, 0)
    part(me ^ 2, send, 1)
    part(me, keep, 0)
    part(me ^ 3, keep, 1)


def add_kernel(keep, came, out):
    out[...] = keep[1] + came[1]


def sum_kernel(keep, came, far, out):
    out[...] = keep[0] + came[0] + far[...]


def join_kernel(places, part, *refs):
    row, halo, h, out = refs[-4:]
    odd = parity()
    for (q, (lo, hi)), ref in zip(places, refs):
        for j in range(2):
            out[own(q + j, odd), lo:hi, :] = ref[j]
    two = row[0:1, :]
    count = h.shape[0]
    total = [0.0, 0.0]
    for k in range(count):
        near, far = halo[k, 0], halo[k, 1]
        v0 = h[k, 0] + two * (NEAR * near + FAR * far)
        v1 = h[k, 1] + two * (FAR * near)
        total = [total[0] + square(v0, count), total[1] + square(v1, count)]
    for j in range(2):
        out[own(j, odd), part[0] : part[1], :] = total[j]


class Line:
    def __init__(self):
        self.last = []

    def __call__(self, kernel, out, args, scalars=0, scratch=(), flops=0, hbm=False, weight=0):
        vmem = pl.BlockSpec(memory_space=pltpu.VMEM)
        smem = pl.BlockSpec(memory_space=pltpu.SMEM)
        many = isinstance(out, list)
        shapes = [jax.ShapeDtypeStruct(s, jnp.float32) for s in (out if many else [out])]
        total = sum(4 * int(x.size) for x in list(args) + shapes)
        first, last = len(args), self.last

        def body(*refs):
            kernel(*refs[:first], *refs[first + len(last) :])

        result = pl.pallas_call(
            body,
            out_shape=shapes,
            in_specs=[smem] * scalars
            + [pl.BlockSpec(memory_space=pltpu.HBM) if hbm else vmem] * (first - scalars)
            + [pl.BlockSpec(memory_space=pl.ANY)] * len(last),
            out_specs=[vmem] * len(shapes),
            scratch_shapes=list(scratch),
            compiler_params=pltpu.CompilerParams(vmem_limit_bytes=40 * 2**20),
            cost_estimate=pl.CostEstimate(
                flops=flops + weight, bytes_accessed=total, transcendentals=0
            ),
        )(*args, *last)
        self.last = [result[0]]
        return result if many else result[0]


def shards(orbitals, potential, coeffs):
    psi = orbitals[0]
    slabs, bands = lax.axis_size("slab"), lax.axis_size("orb")
    planes, rows, lanes = psi.shape
    wide = rows // bands
    half, part = wide // 2, wide // 4
    chunks = [(0, half), (half, wide)]
    cuts = [(0, half), (half, wide - part), (wide - part, wide)]
    cut_a, cut_b, cut_c = cuts
    padded, inner = (part + 8, part + 4)
    face = [(s, (s - 1 if s % 2 == 0 else s + 1) % slabs) for s in range(slabs)]
    partner = [(s, s ^ 1) for s in range(slabs)]
    near = [(i, i ^ 1) for i in range(bands)]
    far = [(i, i ^ 3) for i in range(bands)]
    plane2 = (2, rows, lanes)
    cells = 2 * rows * lanes
    call = Line()

    def as_bands(x):
        return x.reshape(x.shape[0], bands, wide, lanes)

    def slab_shape(chunk):
        return (2, bands, chunk[1] - chunk[0], lanes)

    def pair_shape(chunk):
        return (2, 2, chunk[1] - chunk[0], lanes)

    def add_far(keep, came):
        total = call(add_kernel, keep.shape[1:], (keep, came))
        return keep, came, lax.ppermute(total, "orb", far)

    def squares(cut, halo):
        keep, send = call(
            functools.partial(last_kernel, cut),
            [pair_shape(cut)] * 2,
            (row, halo, as_bands(h_front)),
        )
        return keep, lax.ppermute(send, "orb", near)

    def over_orb(x, d):
        return lax.ppermute(x, "orb", [(i, i ^ d) for i in range(bands)])

    def back_squares(chunk, rows, halo, weight=0):
        keep, send = call(
            functools.partial(back_kernel, chunk, rows),
            [pair_shape(rows)] * 2,
            (row, halo, as_bands(h_back)),
            weight=weight,
        )
        return keep, lax.ppermute(send, "orb", near)

    def faces(chunk, halo, parts):
        fs = call(
            functools.partial(face_kernel, chunk, parts),
            [slab_shape(cut) for cut in parts],
            (halo, as_bands(g)),
        )
        return fs, lax.ppermute(fs[0], "slab", face)

    psi_in = lax.ppermute(psi, "slab", partner)
    pot_in = lax.ppermute(potential, "slab", partner)
    halos = []
    for chunk in chunks:
        piece = call(
            functools.partial(pack_kernel, chunk),
            slab_shape(chunk),
            (as_bands(psi),),
            scratch=[pltpu.SemaphoreType.DMA],
            hbm=True,
        )
        halos.append(lax.ppermute(piece, "slab", face))
    keep, *sends = call(
        functools.partial(send_rows_kernel, cut_c),
        [(planes, padded, lanes)] * bands,
        (as_bands(psi),),
    )
    x_parts = [keep, *[over_orb(x, d) for d, x in zip(offsets(bands)[1:], sends)]]
    g = call(start_kernel, plane2, (psi, potential), flops=24 * cells)
    t, h_back, row = call(
        inner_kernel,
        [plane2, plane2, (8, lanes)],
        (coeffs, psi, potential, psi_in, pot_in, g),
        scalars=1,
        flops=80 * cells,
    )

    def summed(keep, came, from_far, weight=0):
        return call(sum_kernel, from_far.shape, (keep, came, from_far), weight=weight)

    x, piece = call(
        gather_kernel,
        [(bands, planes, padded, lanes), (2 * (bands - 1) * inner, lanes)],
        x_parts,
    )
    x_in = lax.ppermute(x, "slab", partner)
    x_halo = lax.ppermute(piece, "slab", face)
    back0 = back_squares(chunks[0], cut_a, halos[0])
    f0, face_a = faces(chunks[0], halos[0], [cut_a])
    f1, face_b = faces(chunks[1], halos[1], [cut_b, cut_c])
    back1 = back_squares(chunks[1], cut_b, halos[1], weight=8_000_000_000)
    x_first, x_t, x_back = call(
        functools.partial(rows_kernel, cut_c),
        [(bands, 2, inner, lanes)] + [(bands, 2, part, lanes)] * 2,
        (coeffs, x, x_in, as_bands(potential), as_bands(pot_in)),
        scalars=1,
    )
    back0 = add_far(*back0)
    h_front = call(
        functools.partial(front_kernel, cuts),
        plane2,
        (coeffs, psi, potential, t, *f0, *f1),
        scalars=1,
        scratch=[pltpu.VMEM(plane2, jnp.float32)],
        flops=40 * cells,
    )
    back1 = add_far(*back1)
    front_a = squares(cut_a, face_a)
    back0 = summed(*back0)
    back1 = summed(*back1)
    x_f, piece = call(
        functools.partial(rows_face_kernel, cut_c),
        [(bands, 2, inner, lanes), (bands, 2, part, lanes)],
        (x_halo, *halos, x_first),
    )
    x_face = lax.ppermute(piece, "slab", face)
    back2, x_front = call(
        functools.partial(rows_front_kernel, cut_c),
        [(2, part, lanes), (bands, 2, part, lanes)],
        (coeffs, x, as_bands(potential), x_halo, *halos, x_f, x_t, x_back),
        scalars=1,
    )
    front_b = squares(cut_b, face_b)
    front_a = add_far(*front_a)
    front_b = add_far(*front_b)
    front_a = summed(*front_a)
    front_b = summed(*front_b)
    places = [(2, cut) for cut in cuts] + [(0, cut_a), (0, cut_b)]
    return call(
        functools.partial(join_kernel, places, cut_c),
        (planes, wide, lanes),
        (back0, back1, back2, front_a, front_b, row, x_face, x_front),
    )


def solution(mesh):
    return jax.shard_map(
        shards,
        mesh=mesh,
        in_specs=(P("orb", "slab", None, None), P("slab", None, None), P()),
        out_specs=P("slab", "orb", None),
        check_vma=False,
    )
```

```python
import functools

import jax
import jax.numpy as jnp
from jax import lax
from jax.experimental import pallas as pl
from jax.experimental.pallas import tpu as pltpu
from jax.sharding import PartitionSpec as P

NEAR = -2.0 / 15.0
FAR = 1.0 / 120.0
BLOCK = 16


def own(q, odd):
    return jnp.where(odd == 1, 3 - q, q)


def parity():
    return lax.rem(lax.axis_index("slab"), 2)


def with_halo(ref, plane, start, count):
    rows = ref.shape[-2]
    before = pl.multiple_of(lax.rem(start + rows - 8, rows), 8)
    after = pl.multiple_of(lax.rem(start + count, rows), 8)
    return jnp.concatenate(
        [
            ref[plane, pl.ds(before, 8), :],
            ref[plane, pl.ds(start, count), :],
            ref[plane, pl.ds(after, 8), :],
        ],
        axis=0,
    )


def in_plane(ext):
    count, lanes = ext.shape[0] - 16, ext.shape[1]
    mid = ext[8 : 8 + count]
    near = ext[7 : 7 + count] + ext[9 : 9 + count]
    near = near + (pltpu.roll(mid, 1, 1) + pltpu.roll(mid, lanes - 1, 1))
    far = ext[6 : 6 + count] + ext[10 : 10 + count]
    far = far + (pltpu.roll(mid, 2, 1) + pltpu.roll(mid, lanes - 2, 1))
    return mid, near, far


def apply_s(ext, pot, near_z, far_z):
    mid, near, far = in_plane(ext)
    return mid, (
        mid * (0.2 * pot - 0.05) + NEAR * (near + near_z) + FAR * (far + far_z)
    )


def apply_rows(e, pot, near_z, far_z):
    count, lanes = e.shape[0] - 4, e.shape[1]
    mid = e[2 : 2 + count]
    near = e[1 : 1 + count] + e[3 : 3 + count]
    near = near + (pltpu.roll(mid, 1, 1) + pltpu.roll(mid, lanes - 1, 1))
    far = e[0:count] + e[4 : 4 + count]
    far = far + (pltpu.roll(mid, 2, 1) + pltpu.roll(mid, lanes - 2, 1))
    return mid * (0.2 * pot - 0.05) + NEAR * (near + near_z) + FAR * (far + far_z)


def blocks(rows, body):
    def step(i, carry):
        body(pl.multiple_of(i * BLOCK, BLOCK))
        return carry

    lax.fori_loop(0, rows // BLOCK, step, 0)


def pack_kernel(chunk, psi, out, sem):
    lo, hi = chunk
    planes = pl.ds(2 * parity(), out.shape[0])
    copy = pltpu.make_async_copy(psi.at[planes, :, pl.ds(lo, hi - lo), :], out, sem)
    copy.start()
    copy.wait()


def start_kernel(psi, pot, g):
    odd = parity()

    def body(r):
        here = pl.ds(r, BLOCK)
        at = [own(q, odd) for q in range(4)]
        e0, e1 = with_halo(psi, at[0], r, BLOCK), with_halo(psi, at[1], r, BLOCK)
        p2, p3 = psi[at[2], here, :], psi[at[3], here, :]
        g[0, here, :] = apply_s(e0, pot[at[0], here, :], e1[8:-8], p2)[1]
        g[1, here, :] = apply_s(e1, pot[at[1], here, :], e0[8:-8] + p2, p3)[1]

    blocks(psi.shape[1], body)


def inner_kernel(c, psi, pot, psi_in, pot_in, g, t, h, row):
    odd = parity()
    at = [own(q, odd) for q in range(4)]
    base, one, two = c[0] - c[2], c[1], 2.0 * c[2]

    def first(r):
        here = pl.ds(r, BLOCK)
        e2, e3 = with_halo(psi, at[2], r, BLOCK), with_halo(psi, at[3], r, BLOCK)
        p0, p1 = psi[at[0], here, :], psi[at[1], here, :]
        p4, p5 = psi_in[at[0], here, :], psi_in[at[1], here, :]
        t[0, here, :] = apply_s(e2, pot[at[2], here, :], p1 + e3[8:-8], p0 + p4)[1]
        t[1, here, :] = apply_s(e3, pot[at[3], here, :], e2[8:-8] + p4, p1 + p5)[1]

    def second(r):
        here = pl.ds(r, BLOCK)
        e4 = with_halo(psi_in, at[0], r, BLOCK)
        e5 = with_halo(psi_in, at[1], r, BLOCK)
        p2, p3 = psi[at[2], here, :], psi[at[3], here, :]
        p6, p7 = psi_in[at[2], here, :], psi_in[at[3], here, :]
        t4 = apply_s(e4, pot_in[at[0], here, :], p3 + e5[8:-8], p2 + p6)[1]
        t5 = apply_s(e5, pot_in[at[1], here, :], e4[8:-8] + p6, p3 + p7)[1]
        g0, g1 = g[0, here, :], g[1, here, :]
        e2, e3 = with_halo(t, 0, r, BLOCK), with_halo(t, 1, r, BLOCK)
        t2, s2 = apply_s(e2, pot[at[2], here, :], g1 + e3[8:-8], g0 + t4)
        t3, s3 = apply_s(e3, pot[at[3], here, :], e2[8:-8] + t4, g1 + t5)
        h[0, here, :] = base * p2 + one * t2 + two * s2
        h[1, here, :] = base * p3 + one * t3 + two * s3

    row[...] = jnp.full(row.shape, two)
    blocks(psi.shape[1], first)
    blocks(psi.shape[1], second)


def halo_terms(halo, band, odd, rows=slice(None)):
    near, far = halo[1 - odd, band, rows, :], halo[odd, band, rows, :]
    return NEAR * near + FAR * far, FAR * near


def square(x, bands):
    return x * x * (1.0 / bands)


def face_kernel(chunk, parts, halo, g, *fs):
    odd = parity()
    lo, hi = chunk
    for (first, last), f in zip(parts, fs):
        in_halo = slice(first - lo, last - lo)
        for band in range(halo.shape[1]):
            d0, d1 = halo_terms(halo, band, odd, in_halo)
            f[0, band] = g[0, band, first:last, :] + d0
            f[1, band] = g[1, band, first:last, :] + d1


def offsets(bands):
    return [0, *range(bands - 1, 0, -1)]


def back_kernel(chunk, part, row, halo, h, keep, send):
    odd = parity()
    lo, hi = part
    in_halo = slice(lo - chunk[0], hi - chunk[0])
    two = row[0:1, :]
    me = lax.axis_index("orb")
    bands = halo.shape[1]

    def put(band, out, slot):
        d0, d1 = halo_terms(halo, band, odd, in_halo)
        v2 = h[0, band, lo:hi, :] + two * (NEAR * d1 + FAR * d0)
        v3 = h[1, band, lo:hi, :] + two * (FAR * d1)
        out[slot, 0] = square(v2, bands)
        out[slot, 1] = square(v3, bands)

    put(me ^ 1, send, 0)
    put(me ^ 2, send, 1)
    put(me, keep, 0)
    put(me ^ 3, keep, 1)


def tail_rows(ref, plane, band, start, more):
    after = lax.rem(band + 1, ref.shape[1])
    return jnp.concatenate(
        [ref[plane, band, start:, :], ref[plane, after, :more, :]], axis=0
    )


def send_rows_kernel(part, psi, *outs):
    me = lax.axis_index("orb")
    for d, out in zip(offsets(psi.shape[1]), outs):
        for plane in range(psi.shape[0]):
            out[plane] = tail_rows(psi, plane, me ^ d, part[0] - 4, 4)


def gather_kernel(*refs):
    every, halo = refs[-2:]
    odd = parity()
    count = halo.shape[0] // (2 * (len(refs) - 3))
    for k, ref in enumerate(refs[:-2]):
        every[k] = ref[...]
        for q in range(2):
            if k:
                first = (2 * (k - 1) + q) * count
                halo[first : first + count, :] = ref[own(q, odd), 2 : 2 + count, :]


def rows_kernel(part, c, x, x_in, pot, pot_in, g, t, h):
    odd = parity()
    me = lax.axis_index("orb")
    at = [own(q, odd) for q in range(4)]
    base, one, two = c[0] - c[2], c[1], 2.0 * c[2]
    v = [tail_rows(pot, at[q], me, part[0] - 2, 2) for q in range(4)]
    v += [tail_rows(pot_in, at[q], me, part[0] - 2, 2) for q in range(2)]
    n = g.shape[2]

    def step(k, carry):
        e = [x[k, at[q]] for q in range(4)] + [x_in[k, at[q]] for q in range(4)]
        m = [y[2 : 2 + n] for y in e]
        g0 = apply_rows(e[0], v[0], m[1], m[2])
        g1 = apply_rows(e[1], v[1], m[0] + m[2], m[3])
        g[k, 0], g[k, 1] = g0, g1
        full = [apply_rows(e[q], v[q], m[q - 1] + m[q + 1], m[q - 2] + m[q + 2])
                for q in range(2, 6)]
        f = [y[2 : n - 2] for y in [g0, g1, *full]]
        for j in range(2):
            t[k, j] = f[2 + j]
            q = 2 + j
            s = apply_rows(full[j], v[q][2 : n - 2], f[q - 1] + f[q + 1], f[q - 2] + f[q + 2])
            h[k, j] = base * e[q][4 : n] + one * f[q] + two * s
        return carry

    lax.fori_loop(0, x.shape[0], step, 0)


def rows_halo(part, k, halo, first, second, n):
    if k:
        at = [(2 * (k - 1) + q) * n for q in range(2)]
        near, far = [halo[a : a + n, :] for a in at]
    else:
        odd = parity()
        me = lax.axis_index("orb")
        after = lax.rem(me + 1, first.shape[1])
        near, far = [
            jnp.concatenate(
                [second[q, me, second.shape[2] - (n - 2) :, :], first[q, after, :2, :]],
                axis=0,
            )
            for q in (1 - odd, odd)
        ]
    return NEAR * near + FAR * far, FAR * near


def rows_face_kernel(part, halo, first, second, g, f, send):
    n = g.shape[2]
    for k in range(g.shape[0]):
        terms = rows_halo(part, k, halo, first, second, n)
        for q in range(2):
            value = g[k, q] + terms[q]
            f[k, q] = value
            send[k, q] = value[2 : n - 2]


def rows_front_kernel(part, c, x, pot, halo, first, second, f, t, h, back, front):
    odd = parity()
    me = lax.axis_index("orb")
    base, one, two = c[0] - c[2], c[1], 2.0 * c[2]
    n = f.shape[2]
    v = [
        tail_rows(pot, own(q, odd), me, part[0] - 2, 2)[2 : n - 2] for q in range(2)
    ]
    total = [0.0, 0.0]
    count = f.shape[0]
    for k in range(count):
        d0, d1 = [y[2 : n - 2] for y in rows_halo(part, k, halo, first, second, n)]
        v2 = h[k, 0] + two * (NEAR * d1 + FAR * d0)
        v3 = h[k, 1] + two * (FAR * d1)
        total = [total[0] + square(v2, count), total[1] + square(v3, count)]
        f0, f1 = f[k, 0], f[k, 1]
        t2, t3 = t[k, 0], t[k, 1]
        m0, m1 = f0[2 : n - 2], f1[2 : n - 2]
        s0 = apply_rows(f0, v[0], m1, t2)
        s1 = apply_rows(f1, v[1], m0 + t2, t3)
        front[k, 0] = base * x[k, own(0, odd)][4:n] + one * m0 + two * s0
        front[k, 1] = base * x[k, own(1, odd)][4:n] + one * m1 + two * s1
    back[0], back[1] = total


def front_kernel(chunks, c, psi, pot, t, *rest):
    fs, h, scratch = rest[:-2], rest[-2], rest[-1]
    odd = parity()
    at = [own(q, odd) for q in range(2)]
    base, one, two = c[0] - c[2], c[1], 2.0 * c[2]
    rows = psi.shape[1]
    for (lo, hi), f in zip(chunks, fs):
        bands = f.shape[1]
        for band in range(bands):
            first_row = band * (rows // bands)
            for q in range(2):
                scratch[q, first_row + lo : first_row + hi, :] = f[q, band]

    def body(r):
        here = pl.ds(r, BLOCK)
        e0, e1 = with_halo(scratch, 0, r, BLOCK), with_halo(scratch, 1, r, BLOCK)
        t2, t3 = t[0, here, :], t[1, here, :]
        f0, s0 = apply_s(e0, pot[at[0], here, :], e1[8:-8], t2)
        f1, s1 = apply_s(e1, pot[at[1], here, :], e0[8:-8] + t2, t3)
        h[0, here, :] = base * psi[at[0], here, :] + one * f0 + two * s0
        h[1, here, :] = base * psi[at[1], here, :] + one * f1 + two * s1

    blocks(rows, body)


def last_kernel(chunk, row, halo, h, keep, send):
    lo, hi = chunk
    two = row[0:1, :]
    me = lax.axis_index("orb")
    bands = halo.shape[1]

    def part(band, out, slot):
        near, far = halo[0, band], halo[1, band]
        v0 = h[0, band, lo:hi, :] + two * (NEAR * near + FAR * far)
        v1 = h[1, band, lo:hi, :] + two * (FAR * near)
        out[slot, 0] = square(v0, bands)
        out[slot, 1] = square(v1, bands)

    part(me ^ 1, send, 0)
    part(me ^ 2, send, 1)
    part(me, keep, 0)
    part(me ^ 3, keep, 1)


def add_kernel(keep, came, out):
    out[...] = keep[1] + came[1]


def sum_kernel(keep, came, far, out):
    out[...] = keep[0] + came[0] + far[...]


def join_kernel(places, part, *refs):
    row, halo, h, out = refs[-4:]
    odd = parity()
    for (q, (lo, hi)), ref in zip(places, refs):
        for j in range(2):
            out[own(q + j, odd), lo:hi, :] = ref[j]
    two = row[0:1, :]
    count = h.shape[0]
    total = [0.0, 0.0]
    for k in range(count):
        near, far = halo[k, 0], halo[k, 1]
        v0 = h[k, 0] + two * (NEAR * near + FAR * far)
        v1 = h[k, 1] + two * (FAR * near)
        total = [total[0] + square(v0, count), total[1] + square(v1, count)]
    for j in range(2):
        out[own(j, odd), part[0] : part[1], :] = total[j]


class Line:
    def __init__(self):
        self.last = []

    def __call__(self, kernel, out, args, scalars=0, scratch=(), flops=0, hbm=False, weight=0):
        vmem = pl.BlockSpec(memory_space=pltpu.VMEM)
        smem = pl.BlockSpec(memory_space=pltpu.SMEM)
        many = isinstance(out, list)
        shapes = [jax.ShapeDtypeStruct(s, jnp.float32) for s in (out if many else [out])]
        total = sum(4 * int(x.size) for x in list(args) + shapes)
        first, last = len(args), self.last

        def body(*refs):
            kernel(*refs[:first], *refs[first + len(last) :])

        result = pl.pallas_call(
            body,
            out_shape=shapes,
            in_specs=[smem] * scalars
            + [pl.BlockSpec(memory_space=pltpu.HBM) if hbm else vmem] * (first - scalars)
            + [pl.BlockSpec(memory_space=pl.ANY)] * len(last),
            out_specs=[vmem] * len(shapes),
            scratch_shapes=list(scratch),
            compiler_params=pltpu.CompilerParams(vmem_limit_bytes=40 * 2**20),
            cost_estimate=pl.CostEstimate(
                flops=flops + weight, bytes_accessed=total, transcendentals=0
            ),
        )(*args, *last)
        self.last = [result[0]]
        return result if many else result[0]


def shards(orbitals, potential, coeffs):
    psi = orbitals[0]
    slabs, bands = lax.axis_size("slab"), lax.axis_size("orb")
    planes, rows, lanes = psi.shape
    wide = rows // bands
    half, part = wide // 2, wide // 4
    chunks = [(0, half), (half, wide)]
    cuts = [(0, half), (half, wide - part), (wide - part, wide)]
    cut_a, cut_b, cut_c = cuts
    padded, inner = (part + 8, part + 4)
    face = [(s, (s - 1 if s % 2 == 0 else s + 1) % slabs) for s in range(slabs)]
    partner = [(s, s ^ 1) for s in range(slabs)]
    near = [(i, i ^ 1) for i in range(bands)]
    far = [(i, i ^ 3) for i in range(bands)]
    plane2 = (2, rows, lanes)
    cells = 2 * rows * lanes
    call = Line()

    def as_bands(x):
        return x.reshape(x.shape[0], bands, wide, lanes)

    def slab_shape(chunk):
        return (2, bands, chunk[1] - chunk[0], lanes)

    def pair_shape(chunk):
        return (2, 2, chunk[1] - chunk[0], lanes)

    def add_far(keep, came):
        total = call(add_kernel, keep.shape[1:], (keep, came))
        return keep, came, lax.ppermute(total, "orb", far)

    def squares(cut, halo):
        keep, send = call(
            functools.partial(last_kernel, cut),
            [pair_shape(cut)] * 2,
            (row, halo, as_bands(h_front)),
        )
        return keep, lax.ppermute(send, "orb", near)

    def over_orb(x, d):
        return lax.ppermute(x, "orb", [(i, i ^ d) for i in range(bands)])

    def back_squares(chunk, rows, halo, weight=0):
        keep, send = call(
            functools.partial(back_kernel, chunk, rows),
            [pair_shape(rows)] * 2,
            (row, halo, as_bands(h_back)),
            weight=weight,
        )
        return keep, lax.ppermute(send, "orb", near)

    def faces(chunk, halo, parts):
        fs = call(
            functools.partial(face_kernel, chunk, parts),
            [slab_shape(cut) for cut in parts],
            (halo, as_bands(g)),
        )
        return fs, lax.ppermute(fs[0], "slab", face)

    psi_in = lax.ppermute(psi, "slab", partner)
    pot_in = lax.ppermute(potential, "slab", partner)
    halos = []
    for chunk in chunks:
        piece = call(
            functools.partial(pack_kernel, chunk),
            slab_shape(chunk),
            (as_bands(psi),),
            scratch=[pltpu.SemaphoreType.DMA],
            hbm=True,
        )
        halos.append(lax.ppermute(piece, "slab", face))
    keep, *sends = call(
        functools.partial(send_rows_kernel, cut_c),
        [(planes, padded, lanes)] * bands,
        (as_bands(psi),),
    )
    x_parts = [keep, *[over_orb(x, d) for d, x in zip(offsets(bands)[1:], sends)]]
    g = call(start_kernel, plane2, (psi, potential), flops=24 * cells)
    t, h_back, row = call(
        inner_kernel,
        [plane2, plane2, (8, lanes)],
        (coeffs, psi, potential, psi_in, pot_in, g),
        scalars=1,
        flops=80 * cells,
    )

    def summed(keep, came, from_far, weight=0):
        return call(sum_kernel, from_far.shape, (keep, came, from_far), weight=weight)

    x, piece = call(
        gather_kernel,
        [(bands, planes, padded, lanes), (2 * (bands - 1) * inner, lanes)],
        x_parts,
    )
    x_in = lax.ppermute(x, "slab", partner)
    x_halo = lax.ppermute(piece, "slab", face)
    back0 = back_squares(chunks[0], cut_a, halos[0])
    f0, face_a = faces(chunks[0], halos[0], [cut_a])
    f1, face_b = faces(chunks[1], halos[1], [cut_b, cut_c])
    back1 = back_squares(chunks[1], cut_b, halos[1], weight=8_000_000_000)
    back0 = add_far(*back0)
    h_front = call(
        functools.partial(front_kernel, cuts),
        plane2,
        (coeffs, psi, potential, t, *f0, *f1),
        scalars=1,
        scratch=[pltpu.VMEM(plane2, jnp.float32)],
        flops=40 * cells,
    )
    back1 = add_far(*back1)
    front_a = squares(cut_a, face_a)
    x_first, x_t, x_back = call(
        functools.partial(rows_kernel, cut_c),
        [(bands, 2, inner, lanes)] + [(bands, 2, part, lanes)] * 2,
        (coeffs, x, x_in, as_bands(potential), as_bands(pot_in)),
        scalars=1,
    )
    back0 = summed(*back0)
    front_b = squares(cut_b, face_b)
    back1 = summed(*back1, weight=4_000_000_000)
    front_a = add_far(*front_a)
    x_f, piece = call(
        functools.partial(rows_face_kernel, cut_c),
        [(bands, 2, inner, lanes), (bands, 2, part, lanes)],
        (x_halo, *halos, x_first),
    )
    x_face = lax.ppermute(piece, "slab", face)
    back2, x_front = call(
        functools.partial(rows_front_kernel, cut_c),
        [(2, part, lanes), (bands, 2, part, lanes)],
        (coeffs, x, as_bands(potential), x_halo, *halos, x_f, x_t, x_back),
        scalars=1,
    )
    front_b = add_far(*front_b)
    front_a = summed(*front_a)
    front_b = summed(*front_b, weight=2_000_000_000)
    places = [(2, cut) for cut in cuts] + [(0, cut_a), (0, cut_b)]
    return call(
        functools.partial(join_kernel, places, cut_c),
        (planes, wide, lanes),
        (back0, back1, back2, front_a, front_b, row, x_face, x_front),
    )


def solution(mesh):
    return jax.shard_map(
        shards,
        mesh=mesh,
        in_specs=(P("orb", "slab", None, None), P("slab", None, None), P()),
        out_specs=P("slab", "orb", None),
        check_vma=False,
    )
```

```python
import functools

import jax
import jax.numpy as jnp
from jax import lax
from jax.experimental import pallas as pl
from jax.experimental.pallas import tpu as pltpu
from jax.sharding import PartitionSpec as P

NEAR = -2.0 / 15.0
FAR = 1.0 / 120.0
BLOCK = 16


def own(q, odd):
    return jnp.where(odd == 1, 3 - q, q)


def parity():
    return lax.rem(lax.axis_index("slab"), 2)


def with_halo(ref, plane, start, count):
    rows = ref.shape[-2]
    before = pl.multiple_of(lax.rem(start + rows - 8, rows), 8)
    after = pl.multiple_of(lax.rem(start + count, rows), 8)
    return jnp.concatenate(
        [
            ref[plane, pl.ds(before, 8), :],
            ref[plane, pl.ds(start, count), :],
            ref[plane, pl.ds(after, 8), :],
        ],
        axis=0,
    )


def in_plane(ext):
    count, lanes = ext.shape[0] - 16, ext.shape[1]
    mid = ext[8 : 8 + count]
    near = ext[7 : 7 + count] + ext[9 : 9 + count]
    near = near + (pltpu.roll(mid, 1, 1) + pltpu.roll(mid, lanes - 1, 1))
    far = ext[6 : 6 + count] + ext[10 : 10 + count]
    far = far + (pltpu.roll(mid, 2, 1) + pltpu.roll(mid, lanes - 2, 1))
    return mid, near, far


def apply_s(ext, pot, near_z, far_z):
    mid, near, far = in_plane(ext)
    return mid, (
        mid * (0.2 * pot - 0.05) + NEAR * (near + near_z) + FAR * (far + far_z)
    )


def apply_rows(e, pot, near_z, far_z):
    count, lanes = e.shape[0] - 4, e.shape[1]
    mid = e[2 : 2 + count]
    near = e[1 : 1 + count] + e[3 : 3 + count]
    near = near + (pltpu.roll(mid, 1, 1) + pltpu.roll(mid, lanes - 1, 1))
    far = e[0:count] + e[4 : 4 + count]
    far = far + (pltpu.roll(mid, 2, 1) + pltpu.roll(mid, lanes - 2, 1))
    return mid * (0.2 * pot - 0.05) + NEAR * (near + near_z) + FAR * (far + far_z)


def blocks(rows, body):
    def step(i, carry):
        body(pl.multiple_of(i * BLOCK, BLOCK))
        return carry

    lax.fori_loop(0, rows // BLOCK, step, 0)


def pack_kernel(chunk, psi, out, sem):
    lo, hi = chunk
    planes = pl.ds(2 * parity(), out.shape[0])
    copy = pltpu.make_async_copy(psi.at[planes, :, pl.ds(lo, hi - lo), :], out, sem)
    copy.start()
    copy.wait()


def start_kernel(psi, pot, g):
    odd = parity()

    def body(r):
        here = pl.ds(r, BLOCK)
        at = [own(q, odd) for q in range(4)]
        e0, e1 = with_halo(psi, at[0], r, BLOCK), with_halo(psi, at[1], r, BLOCK)
        p2, p3 = psi[at[2], here, :], psi[at[3], here, :]
        g[0, here, :] = apply_s(e0, pot[at[0], here, :], e1[8:-8], p2)[1]
        g[1, here, :] = apply_s(e1, pot[at[1], here, :], e0[8:-8] + p2, p3)[1]

    blocks(psi.shape[1], body)


def inner_kernel(c, psi, pot, psi_in, pot_in, g, t, h, row):
    odd = parity()
    at = [own(q, odd) for q in range(4)]
    base, one, two = c[0] - c[2], c[1], 2.0 * c[2]

    def first(r):
        here = pl.ds(r, BLOCK)
        e2, e3 = with_halo(psi, at[2], r, BLOCK), with_halo(psi, at[3], r, BLOCK)
        p0, p1 = psi[at[0], here, :], psi[at[1], here, :]
        p4, p5 = psi_in[at[0], here, :], psi_in[at[1], here, :]
        t[0, here, :] = apply_s(e2, pot[at[2], here, :], p1 + e3[8:-8], p0 + p4)[1]
        t[1, here, :] = apply_s(e3, pot[at[3], here, :], e2[8:-8] + p4, p1 + p5)[1]

    def second(r):
        here = pl.ds(r, BLOCK)
        e4 = with_halo(psi_in, at[0], r, BLOCK)
        e5 = with_halo(psi_in, at[1], r, BLOCK)
        p2, p3 = psi[at[2], here, :], psi[at[3], here, :]
        p6, p7 = psi_in[at[2], here, :], psi_in[at[3], here, :]
        t4 = apply_s(e4, pot_in[at[0], here, :], p3 + e5[8:-8], p2 + p6)[1]
        t5 = apply_s(e5, pot_in[at[1], here, :], e4[8:-8] + p6, p3 + p7)[1]
        g0, g1 = g[0, here, :], g[1, here, :]
        e2, e3 = with_halo(t, 0, r, BLOCK), with_halo(t, 1, r, BLOCK)
        t2, s2 = apply_s(e2, pot[at[2], here, :], g1 + e3[8:-8], g0 + t4)
        t3, s3 = apply_s(e3, pot[at[3], here, :], e2[8:-8] + t4, g1 + t5)
        h[0, here, :] = base * p2 + one * t2 + two * s2
        h[1, here, :] = base * p3 + one * t3 + two * s3

    row[...] = jnp.full(row.shape, two)
    blocks(psi.shape[1], first)
    blocks(psi.shape[1], second)


def halo_terms(halo, band, odd, rows=slice(None)):
    near, far = halo[1 - odd, band, rows, :], halo[odd, band, rows, :]
    return NEAR * near + FAR * far, FAR * near


def square(x, bands):
    return x * x * (1.0 / bands)


def face_kernel(chunk, parts, halo, g, *fs):
    odd = parity()
    lo, hi = chunk
    for (first, last), f in zip(parts, fs):
        in_halo = slice(first - lo, last - lo)
        for band in range(halo.shape[1]):
            d0, d1 = halo_terms(halo, band, odd, in_halo)
            f[0, band] = g[0, band, first:last, :] + d0
            f[1, band] = g[1, band, first:last, :] + d1


def offsets(bands):
    return [0, *range(bands - 1, 0, -1)]


def back_kernel(chunk, part, row, halo, h, keep, send):
    odd = parity()
    lo, hi = part
    in_halo = slice(lo - chunk[0], hi - chunk[0])
    two = row[0:1, :]
    me = lax.axis_index("orb")
    bands = halo.shape[1]

    def put(band, out, slot):
        d0, d1 = halo_terms(halo, band, odd, in_halo)
        v2 = h[0, band, lo:hi, :] + two * (NEAR * d1 + FAR * d0)
        v3 = h[1, band, lo:hi, :] + two * (FAR * d1)
        out[slot, 0] = square(v2, bands)
        out[slot, 1] = square(v3, bands)

    put(me ^ 1, send, 0)
    put(me ^ 2, send, 1)
    put(me, keep, 0)
    put(me ^ 3, keep, 1)


def tail_rows(ref, plane, band, start, more):
    after = lax.rem(band + 1, ref.shape[1])
    return jnp.concatenate(
        [ref[plane, band, start:, :], ref[plane, after, :more, :]], axis=0
    )


def send_rows_kernel(part, psi, *outs):
    me = lax.axis_index("orb")
    for d, out in zip(offsets(psi.shape[1]), outs):
        for plane in range(psi.shape[0]):
            out[plane] = tail_rows(psi, plane, me ^ d, part[0] - 4, 4)


def gather_kernel(*refs):
    every, halo = refs[-2:]
    odd = parity()
    count = halo.shape[0] // (2 * (len(refs) - 3))
    for k, ref in enumerate(refs[:-2]):
        every[k] = ref[...]
        for q in range(2):
            if k:
                first = (2 * (k - 1) + q) * count
                halo[first : first + count, :] = ref[own(q, odd), 2 : 2 + count, :]


def rows_kernel(part, c, x, x_in, pot, pot_in, g, t, h):
    odd = parity()
    me = lax.axis_index("orb")
    at = [own(q, odd) for q in range(4)]
    base, one, two = c[0] - c[2], c[1], 2.0 * c[2]
    v = [tail_rows(pot, at[q], me, part[0] - 2, 2) for q in range(4)]
    v += [tail_rows(pot_in, at[q], me, part[0] - 2, 2) for q in range(2)]
    n = g.shape[2]

    def step(k, carry):
        e = [x[k, at[q]] for q in range(4)] + [x_in[k, at[q]] for q in range(4)]
        m = [y[2 : 2 + n] for y in e]
        g0 = apply_rows(e[0], v[0], m[1], m[2])
        g1 = apply_rows(e[1], v[1], m[0] + m[2], m[3])
        g[k, 0], g[k, 1] = g0, g1
        full = [apply_rows(e[q], v[q], m[q - 1] + m[q + 1], m[q - 2] + m[q + 2])
                for q in range(2, 6)]
        f = [y[2 : n - 2] for y in [g0, g1, *full]]
        for j in range(2):
            t[k, j] = f[2 + j]
            q = 2 + j
            s = apply_rows(full[j], v[q][2 : n - 2], f[q - 1] + f[q + 1], f[q - 2] + f[q + 2])
            h[k, j] = base * e[q][4 : n] + one * f[q] + two * s
        return carry

    lax.fori_loop(0, x.shape[0], step, 0)


def rows_halo(part, k, halo, first, second, n):
    if k:
        at = [(2 * (k - 1) + q) * n for q in range(2)]
        near, far = [halo[a : a + n, :] for a in at]
    else:
        odd = parity()
        me = lax.axis_index("orb")
        after = lax.rem(me + 1, first.shape[1])
        near, far = [
            jnp.concatenate(
                [second[q, me, second.shape[2] - (n - 2) :, :], first[q, after, :2, :]],
                axis=0,
            )
            for q in (1 - odd, odd)
        ]
    return NEAR * near + FAR * far, FAR * near


def rows_face_kernel(part, halo, first, second, g, f, send):
    n = g.shape[2]
    for k in range(g.shape[0]):
        terms = rows_halo(part, k, halo, first, second, n)
        for q in range(2):
            value = g[k, q] + terms[q]
            f[k, q] = value
            send[k, q] = value[2 : n - 2]


def rows_front_kernel(part, c, x, pot, halo, first, second, f, t, h, back, front):
    odd = parity()
    me = lax.axis_index("orb")
    base, one, two = c[0] - c[2], c[1], 2.0 * c[2]
    n = f.shape[2]
    v = [
        tail_rows(pot, own(q, odd), me, part[0] - 2, 2)[2 : n - 2] for q in range(2)
    ]
    total = [0.0, 0.0]
    count = f.shape[0]
    for k in range(count):
        d0, d1 = [y[2 : n - 2] for y in rows_halo(part, k, halo, first, second, n)]
        v2 = h[k, 0] + two * (NEAR * d1 + FAR * d0)
        v3 = h[k, 1] + two * (FAR * d1)
        total = [total[0] + square(v2, count), total[1] + square(v3, count)]
        f0, f1 = f[k, 0], f[k, 1]
        t2, t3 = t[k, 0], t[k, 1]
        m0, m1 = f0[2 : n - 2], f1[2 : n - 2]
        s0 = apply_rows(f0, v[0], m1, t2)
        s1 = apply_rows(f1, v[1], m0 + t2, t3)
        front[k, 0] = base * x[k, own(0, odd)][4:n] + one * m0 + two * s0
        front[k, 1] = base * x[k, own(1, odd)][4:n] + one * m1 + two * s1
    back[0], back[1] = total


def front_kernel(chunks, c, psi, pot, t, *rest):
    fs, h, scratch = rest[:-2], rest[-2], rest[-1]
    odd = parity()
    at = [own(q, odd) for q in range(2)]
    base, one, two = c[0] - c[2], c[1], 2.0 * c[2]
    rows = psi.shape[1]
    for (lo, hi), f in zip(chunks, fs):
        bands = f.shape[1]
        for band in range(bands):
            first_row = band * (rows // bands)
            for q in range(2):
                scratch[q, first_row + lo : first_row + hi, :] = f[q, band]

    def body(r):
        here = pl.ds(r, BLOCK)
        e0, e1 = with_halo(scratch, 0, r, BLOCK), with_halo(scratch, 1, r, BLOCK)
        t2, t3 = t[0, here, :], t[1, here, :]
        f0, s0 = apply_s(e0, pot[at[0], here, :], e1[8:-8], t2)
        f1, s1 = apply_s(e1, pot[at[1], here, :], e0[8:-8] + t2, t3)
        h[0, here, :] = base * psi[at[0], here, :] + one * f0 + two * s0
        h[1, here, :] = base * psi[at[1], here, :] + one * f1 + two * s1

    blocks(rows, body)


def last_kernel(chunk, row, halo, h, keep, send):
    lo, hi = chunk
    two = row[0:1, :]
    me = lax.axis_index("orb")
    bands = halo.shape[1]

    def part(band, out, slot):
        near, far = halo[0, band], halo[1, band]
        v0 = h[0, band, lo:hi, :] + two * (NEAR * near + FAR * far)
        v1 = h[1, band, lo:hi, :] + two * (FAR * near)
        out[slot, 0] = square(v0, bands)
        out[slot, 1] = square(v1, bands)

    part(me ^ 1, send, 0)
    part(me ^ 2, send, 1)
    part(me, keep, 0)
    part(me ^ 3, keep, 1)


def add_kernel(keep, came, out):
    out[...] = keep[1] + came[1]


def sum_kernel(keep, came, far, out):
    out[...] = keep[0] + came[0] + far[...]


def join_kernel(places, part, *refs):
    row, halo, h, out = refs[-4:]
    odd = parity()
    for (q, (lo, hi)), ref in zip(places, refs):
        for j in range(2):
            out[own(q + j, odd), lo:hi, :] = ref[j]
    two = row[0:1, :]
    count = h.shape[0]
    total = [0.0, 0.0]
    for k in range(count):
        near, far = halo[k, 0], halo[k, 1]
        v0 = h[k, 0] + two * (NEAR * near + FAR * far)
        v1 = h[k, 1] + two * (FAR * near)
        total = [total[0] + square(v0, count), total[1] + square(v1, count)]
    for j in range(2):
        out[own(j, odd), part[0] : part[1], :] = total[j]


class Line:
    def __init__(self):
        self.last = []

    def __call__(self, kernel, out, args, scalars=0, scratch=(), flops=0, hbm=False, weight=0):
        vmem = pl.BlockSpec(memory_space=pltpu.VMEM)
        smem = pl.BlockSpec(memory_space=pltpu.SMEM)
        many = isinstance(out, list)
        shapes = [jax.ShapeDtypeStruct(s, jnp.float32) for s in (out if many else [out])]
        total = sum(4 * int(x.size) for x in list(args) + shapes)
        first, last = len(args), self.last

        def body(*refs):
            kernel(*refs[:first], *refs[first + len(last) :])

        result = pl.pallas_call(
            body,
            out_shape=shapes,
            in_specs=[smem] * scalars
            + [pl.BlockSpec(memory_space=pltpu.HBM) if hbm else vmem] * (first - scalars)
            + [pl.BlockSpec(memory_space=pl.ANY)] * len(last),
            out_specs=[vmem] * len(shapes),
            scratch_shapes=list(scratch),
            compiler_params=pltpu.CompilerParams(vmem_limit_bytes=40 * 2**20),
            cost_estimate=pl.CostEstimate(
                flops=flops + weight, bytes_accessed=total, transcendentals=0
            ),
        )(*args, *last)
        self.last = [result[0]]
        return result if many else result[0]


def shards(orbitals, potential, coeffs):
    psi = orbitals[0]
    slabs, bands = lax.axis_size("slab"), lax.axis_size("orb")
    planes, rows, lanes = psi.shape
    wide = rows // bands
    half, part = wide // 2, wide // 4
    chunks = [(0, half), (half, wide)]
    cuts = [(0, half), (half, wide - part), (wide - part, wide)]
    cut_a, cut_b, cut_c = cuts
    padded, inner = (part + 8, part + 4)
    face = [(s, (s - 1 if s % 2 == 0 else s + 1) % slabs) for s in range(slabs)]
    partner = [(s, s ^ 1) for s in range(slabs)]
    near = [(i, i ^ 1) for i in range(bands)]
    far = [(i, i ^ 3) for i in range(bands)]
    plane2 = (2, rows, lanes)
    cells = 2 * rows * lanes
    call = Line()

    def as_bands(x):
        return x.reshape(x.shape[0], bands, wide, lanes)

    def slab_shape(chunk):
        return (2, bands, chunk[1] - chunk[0], lanes)

    def pair_shape(chunk):
        return (2, 2, chunk[1] - chunk[0], lanes)

    def add_far(keep, came):
        total = call(add_kernel, keep.shape[1:], (keep, came))
        return keep, came, lax.ppermute(total, "orb", far)

    def squares(cut, halo):
        keep, send = call(
            functools.partial(last_kernel, cut),
            [pair_shape(cut)] * 2,
            (row, halo, as_bands(h_front)),
        )
        return keep, lax.ppermute(send, "orb", near)

    def over_orb(x, d):
        return lax.ppermute(x, "orb", [(i, i ^ d) for i in range(bands)])

    def back_squares(chunk, rows, halo, weight=0):
        keep, send = call(
            functools.partial(back_kernel, chunk, rows),
            [pair_shape(rows)] * 2,
            (row, halo, as_bands(h_back)),
            weight=weight,
        )
        return keep, lax.ppermute(send, "orb", near)

    def faces(chunk, halo, parts):
        fs = call(
            functools.partial(face_kernel, chunk, parts),
            [slab_shape(cut) for cut in parts],
            (halo, as_bands(g)),
        )
        return fs, lax.ppermute(fs[0], "slab", face)

    psi_in = lax.ppermute(psi, "slab", partner)
    pot_in = lax.ppermute(potential, "slab", partner)
    halos = []
    for chunk in chunks:
        piece = call(
            functools.partial(pack_kernel, chunk),
            slab_shape(chunk),
            (as_bands(psi),),
            scratch=[pltpu.SemaphoreType.DMA],
            hbm=True,
        )
        halos.append(lax.ppermute(piece, "slab", face))
    keep, *sends = call(
        functools.partial(send_rows_kernel, cut_c),
        [(planes, padded, lanes)] * bands,
        (as_bands(psi),),
    )
    x_parts = [keep, *[over_orb(x, d) for d, x in zip(offsets(bands)[1:], sends)]]
    g = call(start_kernel, plane2, (psi, potential), flops=24 * cells)
    t, h_back, row = call(
        inner_kernel,
        [plane2, plane2, (8, lanes)],
        (coeffs, psi, potential, psi_in, pot_in, g),
        scalars=1,
        flops=80 * cells,
    )

    def summed(keep, came, from_far, weight=0):
        return call(sum_kernel, from_far.shape, (keep, came, from_far), weight=weight)

    f0, face_a = faces(chunks[0], halos[0], [cut_a])
    x, piece = call(
        gather_kernel,
        [(bands, planes, padded, lanes), (2 * (bands - 1) * inner, lanes)],
        x_parts,
    )
    x_in = lax.ppermute(x, "slab", partner)
    x_halo = lax.ppermute(piece, "slab", face)
    back0 = back_squares(chunks[0], cut_a, halos[0])
    f1, face_b = faces(chunks[1], halos[1], [cut_b, cut_c])
    back1 = back_squares(chunks[1], cut_b, halos[1], weight=8_000_000_000)
    x_first, x_t, x_back = call(
        functools.partial(rows_kernel, cut_c),
        [(bands, 2, inner, lanes)] + [(bands, 2, part, lanes)] * 2,
        (coeffs, x, x_in, as_bands(potential), as_bands(pot_in)),
        scalars=1,
    )
    back0 = add_far(*back0)
    h_front = call(
        functools.partial(front_kernel, cuts),
        plane2,
        (coeffs, psi, potential, t, *f0, *f1),
        scalars=1,
        scratch=[pltpu.VMEM(plane2, jnp.float32)],
        flops=40 * cells,
    )
    back1 = add_far(*back1)
    front_a = squares(cut_a, face_a)
    back0 = summed(*back0)
    front_b = squares(cut_b, face_b)
    back1 = summed(*back1, weight=4_000_000_000)
    x_f, piece = call(
        functools.partial(rows_face_kernel, cut_c),
        [(bands, 2, inner, lanes), (bands, 2, part, lanes)],
        (x_halo, *halos, x_first),
    )
    x_face = lax.ppermute(piece, "slab", face)
    back2, x_front = call(
        functools.partial(rows_front_kernel, cut_c),
        [(2, part, lanes), (bands, 2, part, lanes)],
        (coeffs, x, as_bands(potential), x_halo, *halos, x_f, x_t, x_back),
        scalars=1,
    )
    front_a = add_far(*front_a)
    front_b = add_far(*front_b)
    front_a = summed(*front_a)
    front_b = summed(*front_b, weight=1_000_000_000)
    places = [(2, cut) for cut in cuts] + [(0, cut_a), (0, cut_b)]
    return call(
        functools.partial(join_kernel, places, cut_c),
        (planes, wide, lanes),
        (back0, back1, back2, front_a, front_b, row, x_face, x_front),
    )


def solution(mesh):
    return jax.shard_map(
        shards,
        mesh=mesh,
        in_specs=(P("orb", "slab", None, None), P("slab", None, None), P()),
        out_specs=P("slab", "orb", None),
        check_vma=False,
    )
```

```python
import functools

import jax
import jax.numpy as jnp
from jax import lax
from jax.experimental import pallas as pl
from jax.experimental.pallas import tpu as pltpu
from jax.sharding import PartitionSpec as P

NEAR = -2.0 / 15.0
FAR = 1.0 / 120.0
BLOCK = 16


def own(q, odd):
    return jnp.where(odd == 1, 3 - q, q)


def parity():
    return lax.rem(lax.axis_index("slab"), 2)


def with_halo(ref, plane, start, count):
    rows = ref.shape[-2]
    before = pl.multiple_of(lax.rem(start + rows - 8, rows), 8)
    after = pl.multiple_of(lax.rem(start + count, rows), 8)
    return jnp.concatenate(
        [
            ref[plane, pl.ds(before, 8), :],
            ref[plane, pl.ds(start, count), :],
            ref[plane, pl.ds(after, 8), :],
        ],
        axis=0,
    )


def in_plane(ext):
    count, lanes = ext.shape[0] - 16, ext.shape[1]
    mid = ext[8 : 8 + count]
    near = ext[7 : 7 + count] + ext[9 : 9 + count]
    near = near + (pltpu.roll(mid, 1, 1) + pltpu.roll(mid, lanes - 1, 1))
    far = ext[6 : 6 + count] + ext[10 : 10 + count]
    far = far + (pltpu.roll(mid, 2, 1) + pltpu.roll(mid, lanes - 2, 1))
    return mid, near, far


def apply_s(ext, pot, near_z, far_z):
    mid, near, far = in_plane(ext)
    return mid, (
        mid * (0.2 * pot - 0.05) + NEAR * (near + near_z) + FAR * (far + far_z)
    )


def apply_rows(e, pot, near_z, far_z):
    count, lanes = e.shape[0] - 4, e.shape[1]
    mid = e[2 : 2 + count]
    near = e[1 : 1 + count] + e[3 : 3 + count]
    near = near + (pltpu.roll(mid, 1, 1) + pltpu.roll(mid, lanes - 1, 1))
    far = e[0:count] + e[4 : 4 + count]
    far = far + (pltpu.roll(mid, 2, 1) + pltpu.roll(mid, lanes - 2, 1))
    return mid * (0.2 * pot - 0.05) + NEAR * (near + near_z) + FAR * (far + far_z)


def blocks(rows, body):
    def step(i, carry):
        body(pl.multiple_of(i * BLOCK, BLOCK))
        return carry

    lax.fori_loop(0, rows // BLOCK, step, 0, unroll=4)


def pack_kernel(chunk, psi, out, sem):
    lo, hi = chunk
    planes = pl.ds(2 * parity(), out.shape[0])
    copy = pltpu.make_async_copy(psi.at[planes, :, pl.ds(lo, hi - lo), :], out, sem)
    copy.start()
    copy.wait()


def start_kernel(psi, pot, g):
    odd = parity()

    def body(r):
        here = pl.ds(r, BLOCK)
        at = [own(q, odd) for q in range(4)]
        e0, e1 = with_halo(psi, at[0], r, BLOCK), with_halo(psi, at[1], r, BLOCK)
        p2, p3 = psi[at[2], here, :], psi[at[3], here, :]
        g[0, here, :] = apply_s(e0, pot[at[0], here, :], e1[8:-8], p2)[1]
        g[1, here, :] = apply_s(e1, pot[at[1], here, :], e0[8:-8] + p2, p3)[1]

    blocks(psi.shape[1], body)


def inner_kernel(c, psi, pot, psi_in, pot_in, g, t, h, row):
    odd = parity()
    at = [own(q, odd) for q in range(4)]
    base, one, two = c[0] - c[2], c[1], 2.0 * c[2]

    def first(r):
        here = pl.ds(r, BLOCK)
        e2, e3 = with_halo(psi, at[2], r, BLOCK), with_halo(psi, at[3], r, BLOCK)
        p0, p1 = psi[at[0], here, :], psi[at[1], here, :]
        p4, p5 = psi_in[at[0], here, :], psi_in[at[1], here, :]
        t[0, here, :] = apply_s(e2, pot[at[2], here, :], p1 + e3[8:-8], p0 + p4)[1]
        t[1, here, :] = apply_s(e3, pot[at[3], here, :], e2[8:-8] + p4, p1 + p5)[1]

    def second(r):
        here = pl.ds(r, BLOCK)
        e4 = with_halo(psi_in, at[0], r, BLOCK)
        e5 = with_halo(psi_in, at[1], r, BLOCK)
        p2, p3 = psi[at[2], here, :], psi[at[3], here, :]
        p6, p7 = psi_in[at[2], here, :], psi_in[at[3], here, :]
        t4 = apply_s(e4, pot_in[at[0], here, :], p3 + e5[8:-8], p2 + p6)[1]
        t5 = apply_s(e5, pot_in[at[1], here, :], e4[8:-8] + p6, p3 + p7)[1]
        g0, g1 = g[0, here, :], g[1, here, :]
        e2, e3 = with_halo(t, 0, r, BLOCK), with_halo(t, 1, r, BLOCK)
        t2, s2 = apply_s(e2, pot[at[2], here, :], g1 + e3[8:-8], g0 + t4)
        t3, s3 = apply_s(e3, pot[at[3], here, :], e2[8:-8] + t4, g1 + t5)
        h[0, here, :] = base * p2 + one * t2 + two * s2
        h[1, here, :] = base * p3 + one * t3 + two * s3

    row[...] = jnp.full(row.shape, two)
    blocks(psi.shape[1], first)
    blocks(psi.shape[1], second)


def halo_terms(halo, band, odd, rows=slice(None)):
    near, far = halo[1 - odd, band, rows, :], halo[odd, band, rows, :]
    return NEAR * near + FAR * far, FAR * near


def square(x, bands):
    return x * x * (1.0 / bands)


def face_kernel(chunk, parts, halo, g, *fs):
    odd = parity()
    lo, hi = chunk
    for (first, last), f in zip(parts, fs):
        in_halo = slice(first - lo, last - lo)
        for band in range(halo.shape[1]):
            d0, d1 = halo_terms(halo, band, odd, in_halo)
            f[0, band] = g[0, band, first:last, :] + d0
            f[1, band] = g[1, band, first:last, :] + d1


def offsets(bands):
    return [0, *range(bands - 1, 0, -1)]


def back_kernel(chunk, part, row, halo, h, keep, send):
    odd = parity()
    lo, hi = part
    in_halo = slice(lo - chunk[0], hi - chunk[0])
    two = row[0:1, :]
    me = lax.axis_index("orb")
    bands = halo.shape[1]

    def put(band, out, slot):
        d0, d1 = halo_terms(halo, band, odd, in_halo)
        v2 = h[0, band, lo:hi, :] + two * (NEAR * d1 + FAR * d0)
        v3 = h[1, band, lo:hi, :] + two * (FAR * d1)
        out[slot, 0] = square(v2, bands)
        out[slot, 1] = square(v3, bands)

    put(me ^ 1, send, 0)
    put(me ^ 2, send, 1)
    put(me, keep, 0)
    put(me ^ 3, keep, 1)


def tail_rows(ref, plane, band, start, more):
    after = lax.rem(band + 1, ref.shape[1])
    return jnp.concatenate(
        [ref[plane, band, start:, :], ref[plane, after, :more, :]], axis=0
    )


def send_rows_kernel(part, psi, *outs):
    me = lax.axis_index("orb")
    for d, out in zip(offsets(psi.shape[1]), outs):
        for plane in range(psi.shape[0]):
            out[plane] = tail_rows(psi, plane, me ^ d, part[0] - 4, 4)


def gather_kernel(*refs):
    every, halo = refs[-2:]
    odd = parity()
    count = halo.shape[0] // (2 * (len(refs) - 3))
    for k, ref in enumerate(refs[:-2]):
        every[k] = ref[...]
        for q in range(2):
            if k:
                first = (2 * (k - 1) + q) * count
                halo[first : first + count, :] = ref[own(q, odd), 2 : 2 + count, :]


def rows_kernel(part, c, x, x_in, pot, pot_in, g, t, h):
    odd = parity()
    me = lax.axis_index("orb")
    at = [own(q, odd) for q in range(4)]
    base, one, two = c[0] - c[2], c[1], 2.0 * c[2]
    v = [tail_rows(pot, at[q], me, part[0] - 2, 2) for q in range(4)]
    v += [tail_rows(pot_in, at[q], me, part[0] - 2, 2) for q in range(2)]
    n = g.shape[2]

    def step(k, carry):
        e = [x[k, at[q]] for q in range(4)] + [x_in[k, at[q]] for q in range(4)]
        m = [y[2 : 2 + n] for y in e]
        g0 = apply_rows(e[0], v[0], m[1], m[2])
        g1 = apply_rows(e[1], v[1], m[0] + m[2], m[3])
        g[k, 0], g[k, 1] = g0, g1
        full = [apply_rows(e[q], v[q], m[q - 1] + m[q + 1], m[q - 2] + m[q + 2])
                for q in range(2, 6)]
        f = [y[2 : n - 2] for y in [g0, g1, *full]]
        for j in range(2):
            t[k, j] = f[2 + j]
            q = 2 + j
            s = apply_rows(full[j], v[q][2 : n - 2], f[q - 1] + f[q + 1], f[q - 2] + f[q + 2])
            h[k, j] = base * e[q][4 : n] + one * f[q] + two * s
        return carry

    lax.fori_loop(0, x.shape[0], step, 0, unroll=True)


def rows_halo(part, k, halo, first, second, n):
    if k:
        at = [(2 * (k - 1) + q) * n for q in range(2)]
        near, far = [halo[a : a + n, :] for a in at]
    else:
        odd = parity()
        me = lax.axis_index("orb")
        after = lax.rem(me + 1, first.shape[1])
        near, far = [
            jnp.concatenate(
                [second[q, me, second.shape[2] - (n - 2) :, :], first[q, after, :2, :]],
                axis=0,
            )
            for q in (1 - odd, odd)
        ]
    return NEAR * near + FAR * far, FAR * near


def rows_face_kernel(part, halo, first, second, g, f, send):
    n = g.shape[2]
    for k in range(g.shape[0]):
        terms = rows_halo(part, k, halo, first, second, n)
        for q in range(2):
            value = g[k, q] + terms[q]
            f[k, q] = value
            send[k, q] = value[2 : n - 2]


def rows_front_kernel(part, c, x, pot, halo, first, second, f, t, h, back, front):
    odd = parity()
    me = lax.axis_index("orb")
    base, one, two = c[0] - c[2], c[1], 2.0 * c[2]
    n = f.shape[2]
    v = [
        tail_rows(pot, own(q, odd), me, part[0] - 2, 2)[2 : n - 2] for q in range(2)
    ]
    total = [0.0, 0.0]
    count = f.shape[0]
    for k in range(count):
        d0, d1 = [y[2 : n - 2] for y in rows_halo(part, k, halo, first, second, n)]
        v2 = h[k, 0] + two * (NEAR * d1 + FAR * d0)
        v3 = h[k, 1] + two * (FAR * d1)
        total = [total[0] + square(v2, count), total[1] + square(v3, count)]
        f0, f1 = f[k, 0], f[k, 1]
        t2, t3 = t[k, 0], t[k, 1]
        m0, m1 = f0[2 : n - 2], f1[2 : n - 2]
        s0 = apply_rows(f0, v[0], m1, t2)
        s1 = apply_rows(f1, v[1], m0 + t2, t3)
        front[k, 0] = base * x[k, own(0, odd)][4:n] + one * m0 + two * s0
        front[k, 1] = base * x[k, own(1, odd)][4:n] + one * m1 + two * s1
    back[0], back[1] = total


def front_kernel(chunks, c, psi, pot, t, *rest):
    fs, h, scratch = rest[:-2], rest[-2], rest[-1]
    odd = parity()
    at = [own(q, odd) for q in range(2)]
    base, one, two = c[0] - c[2], c[1], 2.0 * c[2]
    rows = psi.shape[1]
    for (lo, hi), f in zip(chunks, fs):
        bands = f.shape[1]
        for band in range(bands):
            first_row = band * (rows // bands)
            for q in range(2):
                scratch[q, first_row + lo : first_row + hi, :] = f[q, band]

    def body(r):
        here = pl.ds(r, BLOCK)
        e0, e1 = with_halo(scratch, 0, r, BLOCK), with_halo(scratch, 1, r, BLOCK)
        t2, t3 = t[0, here, :], t[1, here, :]
        f0, s0 = apply_s(e0, pot[at[0], here, :], e1[8:-8], t2)
        f1, s1 = apply_s(e1, pot[at[1], here, :], e0[8:-8] + t2, t3)
        h[0, here, :] = base * psi[at[0], here, :] + one * f0 + two * s0
        h[1, here, :] = base * psi[at[1], here, :] + one * f1 + two * s1

    blocks(rows, body)


def last_kernel(chunk, row, halo, h, keep, send):
    lo, hi = chunk
    two = row[0:1, :]
    me = lax.axis_index("orb")
    bands = halo.shape[1]

    def part(band, out, slot):
        near, far = halo[0, band], halo[1, band]
        v0 = h[0, band, lo:hi, :] + two * (NEAR * near + FAR * far)
        v1 = h[1, band, lo:hi, :] + two * (FAR * near)
        out[slot, 0] = square(v0, bands)
        out[slot, 1] = square(v1, bands)

    part(me ^ 1, send, 0)
    part(me ^ 2, send, 1)
    part(me, keep, 0)
    part(me ^ 3, keep, 1)


def add_kernel(keep, came, out):
    out[...] = keep[1] + came[1]


def sum_kernel(keep, came, far, out):
    out[...] = keep[0] + came[0] + far[...]


def join_kernel(places, part, *refs):
    row, halo, h, out = refs[-4:]
    odd = parity()
    for (q, (lo, hi)), ref in zip(places, refs):
        for j in range(2):
            out[own(q + j, odd), lo:hi, :] = ref[j]
    two = row[0:1, :]
    count = h.shape[0]
    total = [0.0, 0.0]
    for k in range(count):
        near, far = halo[k, 0], halo[k, 1]
        v0 = h[k, 0] + two * (NEAR * near + FAR * far)
        v1 = h[k, 1] + two * (FAR * near)
        total = [total[0] + square(v0, count), total[1] + square(v1, count)]
    for j in range(2):
        out[own(j, odd), part[0] : part[1], :] = total[j]


class Line:
    def __init__(self):
        self.last = []

    def __call__(self, kernel, out, args, scalars=0, scratch=(), flops=0, hbm=False, weight=0):
        vmem = pl.BlockSpec(memory_space=pltpu.VMEM)
        smem = pl.BlockSpec(memory_space=pltpu.SMEM)
        many = isinstance(out, list)
        shapes = [jax.ShapeDtypeStruct(s, jnp.float32) for s in (out if many else [out])]
        total = sum(4 * int(x.size) for x in list(args) + shapes)
        first, last = len(args), self.last

        def body(*refs):
            kernel(*refs[:first], *refs[first + len(last) :])

        result = pl.pallas_call(
            body,
            out_shape=shapes,
            in_specs=[smem] * scalars
            + [pl.BlockSpec(memory_space=pltpu.HBM) if hbm else vmem] * (first - scalars)
            + [pl.BlockSpec(memory_space=pl.ANY)] * len(last),
            out_specs=[vmem] * len(shapes),
            scratch_shapes=list(scratch),
            compiler_params=pltpu.CompilerParams(vmem_limit_bytes=40 * 2**20),
            cost_estimate=pl.CostEstimate(
                flops=flops + weight, bytes_accessed=total, transcendentals=0
            ),
        )(*args, *last)
        self.last = [result[0]]
        return result if many else result[0]


def shards(orbitals, potential, coeffs):
    psi = orbitals[0]
    slabs, bands = lax.axis_size("slab"), lax.axis_size("orb")
    planes, rows, lanes = psi.shape
    wide = rows // bands
    half, part = wide // 2, wide // 4
    chunks = [(0, half), (half, wide)]
    cuts = [(0, half), (half, wide - part), (wide - part, wide)]
    cut_a, cut_b, cut_c = cuts
    padded, inner = (part + 8, part + 4)
    face = [(s, (s - 1 if s % 2 == 0 else s + 1) % slabs) for s in range(slabs)]
    partner = [(s, s ^ 1) for s in range(slabs)]
    near = [(i, i ^ 1) for i in range(bands)]
    far = [(i, i ^ 3) for i in range(bands)]
    plane2 = (2, rows, lanes)
    cells = 2 * rows * lanes
    call = Line()

    def as_bands(x):
        return x.reshape(x.shape[0], bands, wide, lanes)

    def slab_shape(chunk):
        return (2, bands, chunk[1] - chunk[0], lanes)

    def pair_shape(chunk):
        return (2, 2, chunk[1] - chunk[0], lanes)

    def add_far(keep, came):
        total = call(add_kernel, keep.shape[1:], (keep, came))
        return keep, came, lax.ppermute(total, "orb", far)

    def squares(cut, halo):
        keep, send = call(
            functools.partial(last_kernel, cut),
            [pair_shape(cut)] * 2,
            (row, halo, as_bands(h_front)),
        )
        return keep, lax.ppermute(send, "orb", near)

    def over_orb(x, d):
        return lax.ppermute(x, "orb", [(i, i ^ d) for i in range(bands)])

    def back_squares(chunk, rows, halo, weight=0):
        keep, send = call(
            functools.partial(back_kernel, chunk, rows),
            [pair_shape(rows)] * 2,
            (row, halo, as_bands(h_back)),
            weight=weight,
        )
        return keep, lax.ppermute(send, "orb", near)

    def faces(chunk, halo, parts):
        fs = call(
            functools.partial(face_kernel, chunk, parts),
            [slab_shape(cut) for cut in parts],
            (halo, as_bands(g)),
        )
        return fs, lax.ppermute(fs[0], "slab", face)

    psi_in = lax.ppermute(psi, "slab", partner)
    pot_in = lax.ppermute(potential, "slab", partner)
    halos = []
    for chunk in chunks:
        piece = call(
            functools.partial(pack_kernel, chunk),
            slab_shape(chunk),
            (as_bands(psi),),
            scratch=[pltpu.SemaphoreType.DMA],
            hbm=True,
        )
        halos.append(lax.ppermute(piece, "slab", face))
    keep, *sends = call(
        functools.partial(send_rows_kernel, cut_c),
        [(planes, padded, lanes)] * bands,
        (as_bands(psi),),
    )
    x_parts = [keep, *[over_orb(x, d) for d, x in zip(offsets(bands)[1:], sends)]]
    g = call(start_kernel, plane2, (psi, potential), flops=24 * cells)
    t, h_back, row = call(
        inner_kernel,
        [plane2, plane2, (8, lanes)],
        (coeffs, psi, potential, psi_in, pot_in, g),
        scalars=1,
        flops=80 * cells,
    )

    def summed(keep, came, from_far, weight=0):
        return call(sum_kernel, from_far.shape, (keep, came, from_far), weight=weight)

    f0, face_a = faces(chunks[0], halos[0], [cut_a])
    x, piece = call(
        gather_kernel,
        [(bands, planes, padded, lanes), (2 * (bands - 1) * inner, lanes)],
        x_parts,
    )
    x_in = lax.ppermute(x, "slab", partner)
    x_halo = lax.ppermute(piece, "slab", face)
    back0 = back_squares(chunks[0], cut_a, halos[0])
    f1, face_b = faces(chunks[1], halos[1], [cut_b, cut_c])
    back1 = back_squares(chunks[1], cut_b, halos[1], weight=8_000_000_000)
    x_first, x_t, x_back = call(
        functools.partial(rows_kernel, cut_c),
        [(bands, 2, inner, lanes)] + [(bands, 2, part, lanes)] * 2,
        (coeffs, x, x_in, as_bands(potential), as_bands(pot_in)),
        scalars=1,
    )
    back0 = add_far(*back0)
    h_front = call(
        functools.partial(front_kernel, cuts),
        plane2,
        (coeffs, psi, potential, t, *f0, *f1),
        scalars=1,
        scratch=[pltpu.VMEM(plane2, jnp.float32)],
        flops=40 * cells,
    )
    back1 = add_far(*back1)
    front_a = squares(cut_a, face_a)
    back0 = summed(*back0)
    front_b = squares(cut_b, face_b)
    back1 = summed(*back1, weight=4_000_000_000)
    front_a = add_far(*front_a)
    x_f, piece = call(
        functools.partial(rows_face_kernel, cut_c),
        [(bands, 2, inner, lanes), (bands, 2, part, lanes)],
        (x_halo, *halos, x_first),
    )
    x_face = lax.ppermute(piece, "slab", face)
    front_b = add_far(*front_b)
    back2, x_front = call(
        functools.partial(rows_front_kernel, cut_c),
        [(2, part, lanes), (bands, 2, part, lanes)],
        (coeffs, x, as_bands(potential), x_halo, *halos, x_f, x_t, x_back),
        scalars=1,
    )
    front_a = summed(*front_a)
    front_b = summed(*front_b, weight=2_000_000_000)
    places = [(2, cut) for cut in cuts] + [(0, cut_a), (0, cut_b)]
    return call(
        functools.partial(join_kernel, places, cut_c),
        (planes, wide, lanes),
        (back0, back1, back2, front_a, front_b, row, x_face, x_front),
    )


def solution(mesh):
    return jax.shard_map(
        shards,
        mesh=mesh,
        in_specs=(P("orb", "slab", None, None), P("slab", None, None), P()),
        out_specs=P("slab", "orb", None),
        check_vma=False,
    )
```

```python
import functools

import jax
import jax.numpy as jnp
from jax import lax
from jax.experimental import pallas as pl
from jax.experimental.pallas import tpu as pltpu
from jax.sharding import PartitionSpec as P

NEAR = -2.0 / 15.0
FAR = 1.0 / 120.0
BLOCK = 16


def own(q, odd):
    return jnp.where(odd == 1, 3 - q, q)


def parity():
    return lax.rem(lax.axis_index("slab"), 2)


def with_halo(ref, plane, start, count):
    rows = ref.shape[-2]
    before = pl.multiple_of(lax.rem(start + rows - 8, rows), 8)
    after = pl.multiple_of(lax.rem(start + count, rows), 8)
    return jnp.concatenate(
        [
            ref[plane, pl.ds(before, 8), :],
            ref[plane, pl.ds(start, count), :],
            ref[plane, pl.ds(after, 8), :],
        ],
        axis=0,
    )


def in_plane(ext):
    count, lanes = ext.shape[0] - 16, ext.shape[1]
    mid = ext[8 : 8 + count]
    near = ext[7 : 7 + count] + ext[9 : 9 + count]
    near = near + (pltpu.roll(mid, 1, 1) + pltpu.roll(mid, lanes - 1, 1))
    far = ext[6 : 6 + count] + ext[10 : 10 + count]
    far = far + (pltpu.roll(mid, 2, 1) + pltpu.roll(mid, lanes - 2, 1))
    return mid, near, far


def apply_s(ext, pot, near_z, far_z):
    mid, near, far = in_plane(ext)
    return mid, (
        mid * (0.2 * pot - 0.05) + NEAR * (near + near_z) + FAR * (far + far_z)
    )


def apply_rows(e, pot, near_z, far_z):
    count, lanes = e.shape[0] - 4, e.shape[1]
    mid = e[2 : 2 + count]
    near = e[1 : 1 + count] + e[3 : 3 + count]
    near = near + (pltpu.roll(mid, 1, 1) + pltpu.roll(mid, lanes - 1, 1))
    far = e[0:count] + e[4 : 4 + count]
    far = far + (pltpu.roll(mid, 2, 1) + pltpu.roll(mid, lanes - 2, 1))
    return mid * (0.2 * pot - 0.05) + NEAR * (near + near_z) + FAR * (far + far_z)


def blocks(rows, body):
    def step(i, carry):
        body(pl.multiple_of(i * BLOCK, BLOCK))
        return carry

    lax.fori_loop(0, rows // BLOCK, step, 0, unroll=4)


def pack_kernel(chunk, psi, out, sem):
    lo, hi = chunk
    planes = pl.ds(2 * parity(), out.shape[0])
    copy = pltpu.make_async_copy(psi.at[planes, :, pl.ds(lo, hi - lo), :], out, sem)
    copy.start()
    copy.wait()


def start_kernel(psi, pot, g):
    odd = parity()

    def body(r):
        here = pl.ds(r, BLOCK)
        at = [own(q, odd) for q in range(4)]
        e0, e1 = with_halo(psi, at[0], r, BLOCK), with_halo(psi, at[1], r, BLOCK)
        p2, p3 = psi[at[2], here, :], psi[at[3], here, :]
        g[0, here, :] = apply_s(e0, pot[at[0], here, :], e1[8:-8], p2)[1]
        g[1, here, :] = apply_s(e1, pot[at[1], here, :], e0[8:-8] + p2, p3)[1]

    blocks(psi.shape[1], body)


def inner_kernel(c, psi, pot, psi_in, pot_in, g, t, h, row):
    odd = parity()
    at = [own(q, odd) for q in range(4)]
    base, one, two = c[0] - c[2], c[1], 2.0 * c[2]

    def first(r):
        here = pl.ds(r, BLOCK)
        e2, e3 = with_halo(psi, at[2], r, BLOCK), with_halo(psi, at[3], r, BLOCK)
        p0, p1 = psi[at[0], here, :], psi[at[1], here, :]
        p4, p5 = psi_in[at[0], here, :], psi_in[at[1], here, :]
        t[0, here, :] = apply_s(e2, pot[at[2], here, :], p1 + e3[8:-8], p0 + p4)[1]
        t[1, here, :] = apply_s(e3, pot[at[3], here, :], e2[8:-8] + p4, p1 + p5)[1]

    def second(r):
        here = pl.ds(r, BLOCK)
        e4 = with_halo(psi_in, at[0], r, BLOCK)
        e5 = with_halo(psi_in, at[1], r, BLOCK)
        p2, p3 = psi[at[2], here, :], psi[at[3], here, :]
        p6, p7 = psi_in[at[2], here, :], psi_in[at[3], here, :]
        t4 = apply_s(e4, pot_in[at[0], here, :], p3 + e5[8:-8], p2 + p6)[1]
        t5 = apply_s(e5, pot_in[at[1], here, :], e4[8:-8] + p6, p3 + p7)[1]
        g0, g1 = g[0, here, :], g[1, here, :]
        e2, e3 = with_halo(t, 0, r, BLOCK), with_halo(t, 1, r, BLOCK)
        t2, s2 = apply_s(e2, pot[at[2], here, :], g1 + e3[8:-8], g0 + t4)
        t3, s3 = apply_s(e3, pot[at[3], here, :], e2[8:-8] + t4, g1 + t5)
        h[0, here, :] = base * p2 + one * t2 + two * s2
        h[1, here, :] = base * p3 + one * t3 + two * s3

    row[...] = jnp.full(row.shape, two)
    blocks(psi.shape[1], first)
    blocks(psi.shape[1], second)


def halo_terms(halo, band, odd, rows=slice(None)):
    near, far = halo[1 - odd, band, rows, :], halo[odd, band, rows, :]
    return NEAR * near + FAR * far, FAR * near


def square(x, bands):
    return x * x * (1.0 / bands)


def face_kernel(chunk, parts, halo, g, *fs):
    odd = parity()
    lo, hi = chunk
    for (first, last), f in zip(parts, fs):
        in_halo = slice(first - lo, last - lo)
        for band in range(halo.shape[1]):
            d0, d1 = halo_terms(halo, band, odd, in_halo)
            f[0, band] = g[0, band, first:last, :] + d0
            f[1, band] = g[1, band, first:last, :] + d1


def offsets(bands):
    return [0, *range(bands - 1, 0, -1)]


def back_kernel(chunk, part, row, halo, h, keep, send):
    odd = parity()
    lo, hi = part
    in_halo = slice(lo - chunk[0], hi - chunk[0])
    two = row[0:1, :]
    me = lax.axis_index("orb")
    bands = halo.shape[1]

    def put(band, out, slot):
        d0, d1 = halo_terms(halo, band, odd, in_halo)
        v2 = h[0, band, lo:hi, :] + two * (NEAR * d1 + FAR * d0)
        v3 = h[1, band, lo:hi, :] + two * (FAR * d1)
        out[slot, 0] = square(v2, bands)
        out[slot, 1] = square(v3, bands)

    put(me ^ 1, send, 0)
    put(me ^ 2, send, 1)
    put(me, keep, 0)
    put(me ^ 3, keep, 1)


def tail_rows(ref, plane, band, start, more):
    after = lax.rem(band + 1, ref.shape[1])
    return jnp.concatenate(
        [ref[plane, band, start:, :], ref[plane, after, :more, :]], axis=0
    )


def send_rows_kernel(part, psi, *outs):
    me = lax.axis_index("orb")
    for d, out in zip(offsets(psi.shape[1]), outs):
        for plane in range(psi.shape[0]):
            out[plane] = tail_rows(psi, plane, me ^ d, part[0] - 4, 4)


def gather_kernel(*refs):
    every, halo = refs[-2:]
    odd = parity()
    count = halo.shape[0] // (2 * (len(refs) - 3))
    for k, ref in enumerate(refs[:-2]):
        every[k] = ref[...]
        for q in range(2):
            if k:
                first = (2 * (k - 1) + q) * count
                halo[first : first + count, :] = ref[own(q, odd), 2 : 2 + count, :]


def rows_kernel(part, c, x, x_in, pot, pot_in, g, t, h):
    odd = parity()
    me = lax.axis_index("orb")
    at = [own(q, odd) for q in range(4)]
    base, one, two = c[0] - c[2], c[1], 2.0 * c[2]
    v = [tail_rows(pot, at[q], me, part[0] - 2, 2) for q in range(4)]
    v += [tail_rows(pot_in, at[q], me, part[0] - 2, 2) for q in range(2)]
    n = g.shape[2]

    def step(k, carry):
        e = [x[k, at[q]] for q in range(4)] + [x_in[k, at[q]] for q in range(4)]
        m = [y[2 : 2 + n] for y in e]
        g0 = apply_rows(e[0], v[0], m[1], m[2])
        g1 = apply_rows(e[1], v[1], m[0] + m[2], m[3])
        g[k, 0], g[k, 1] = g0, g1
        full = [apply_rows(e[q], v[q], m[q - 1] + m[q + 1], m[q - 2] + m[q + 2])
                for q in range(2, 6)]
        f = [y[2 : n - 2] for y in [g0, g1, *full]]
        for j in range(2):
            t[k, j] = f[2 + j]
            q = 2 + j
            s = apply_rows(full[j], v[q][2 : n - 2], f[q - 1] + f[q + 1], f[q - 2] + f[q + 2])
            h[k, j] = base * e[q][4 : n] + one * f[q] + two * s
        return carry

    lax.fori_loop(0, x.shape[0], step, 0, unroll=True)


def rows_halo(part, k, halo, first, second, n):
    if k:
        at = [(2 * (k - 1) + q) * n for q in range(2)]
        near, far = [halo[a : a + n, :] for a in at]
    else:
        odd = parity()
        me = lax.axis_index("orb")
        after = lax.rem(me + 1, first.shape[1])
        near, far = [
            jnp.concatenate(
                [second[q, me, second.shape[2] - (n - 2) :, :], first[q, after, :2, :]],
                axis=0,
            )
            for q in (1 - odd, odd)
        ]
    return NEAR * near + FAR * far, FAR * near


def rows_face_kernel(part, halo, first, second, g, f, send):
    n = g.shape[2]
    for k in range(g.shape[0]):
        terms = rows_halo(part, k, halo, first, second, n)
        for q in range(2):
            value = g[k, q] + terms[q]
            f[k, q] = value
            send[k, q] = value[2 : n - 2]


def rows_front_kernel(part, c, x, pot, halo, first, second, f, t, h, back, front):
    odd = parity()
    me = lax.axis_index("orb")
    base, one, two = c[0] - c[2], c[1], 2.0 * c[2]
    n = f.shape[2]
    v = [
        tail_rows(pot, own(q, odd), me, part[0] - 2, 2)[2 : n - 2] for q in range(2)
    ]
    total = [0.0, 0.0]
    count = f.shape[0]
    for k in range(count):
        d0, d1 = [y[2 : n - 2] for y in rows_halo(part, k, halo, first, second, n)]
        v2 = h[k, 0] + two * (NEAR * d1 + FAR * d0)
        v3 = h[k, 1] + two * (FAR * d1)
        total = [total[0] + square(v2, count), total[1] + square(v3, count)]
        f0, f1 = f[k, 0], f[k, 1]
        t2, t3 = t[k, 0], t[k, 1]
        m0, m1 = f0[2 : n - 2], f1[2 : n - 2]
        s0 = apply_rows(f0, v[0], m1, t2)
        s1 = apply_rows(f1, v[1], m0 + t2, t3)
        front[k, 0] = base * x[k, own(0, odd)][4:n] + one * m0 + two * s0
        front[k, 1] = base * x[k, own(1, odd)][4:n] + one * m1 + two * s1
    back[0], back[1] = total


def front_kernel(chunks, c, psi, pot, t, *rest):
    fs, h, scratch = rest[:-2], rest[-2], rest[-1]
    odd = parity()
    at = [own(q, odd) for q in range(2)]
    base, one, two = c[0] - c[2], c[1], 2.0 * c[2]
    rows = psi.shape[1]
    for (lo, hi), f in zip(chunks, fs):
        bands = f.shape[1]
        for band in range(bands):
            first_row = band * (rows // bands)
            for q in range(2):
                scratch[q, first_row + lo : first_row + hi, :] = f[q, band]

    def body(r):
        here = pl.ds(r, BLOCK)
        e0, e1 = with_halo(scratch, 0, r, BLOCK), with_halo(scratch, 1, r, BLOCK)
        t2, t3 = t[0, here, :], t[1, here, :]
        f0, s0 = apply_s(e0, pot[at[0], here, :], e1[8:-8], t2)
        f1, s1 = apply_s(e1, pot[at[1], here, :], e0[8:-8] + t2, t3)
        h[0, here, :] = base * psi[at[0], here, :] + one * f0 + two * s0
        h[1, here, :] = base * psi[at[1], here, :] + one * f1 + two * s1

    blocks(rows, body)


def last_kernel(chunk, row, halo, h, keep, send):
    lo, hi = chunk
    two = row[0:1, :]
    me = lax.axis_index("orb")
    bands = halo.shape[1]

    def part(band, out, slot):
        near, far = halo[0, band], halo[1, band]
        v0 = h[0, band, lo:hi, :] + two * (NEAR * near + FAR * far)
        v1 = h[1, band, lo:hi, :] + two * (FAR * near)
        out[slot, 0] = square(v0, bands)
        out[slot, 1] = square(v1, bands)

    part(me ^ 1, send, 0)
    part(me ^ 2, send, 1)
    part(me, keep, 0)
    part(me ^ 3, keep, 1)


def add_kernel(keep, came, out):
    out[...] = keep[1] + came[1]


def sum_kernel(keep, came, far, out):
    out[...] = keep[0] + came[0] + far[...]


def join_kernel(places, part, *refs):
    row, halo, h, out = refs[-4:]
    odd = parity()
    for (q, (lo, hi)), ref in zip(places, refs):
        for j in range(2):
            out[own(q + j, odd), lo:hi, :] = ref[j]
    two = row[0:1, :]
    count = h.shape[0]
    total = [0.0, 0.0]
    for k in range(count):
        near, far = halo[k, 0], halo[k, 1]
        v0 = h[k, 0] + two * (NEAR * near + FAR * far)
        v1 = h[k, 1] + two * (FAR * near)
        total = [total[0] + square(v0, count), total[1] + square(v1, count)]
    for j in range(2):
        out[own(j, odd), part[0] : part[1], :] = total[j]


class Line:
    def __init__(self):
        self.last = []

    def __call__(self, kernel, out, args, scalars=0, scratch=(), flops=0, hbm=False, weight=0):
        vmem = pl.BlockSpec(memory_space=pltpu.VMEM)
        smem = pl.BlockSpec(memory_space=pltpu.SMEM)
        many = isinstance(out, list)
        shapes = [jax.ShapeDtypeStruct(s, jnp.float32) for s in (out if many else [out])]
        total = sum(4 * int(x.size) for x in list(args) + shapes)
        first, last = len(args), self.last

        def body(*refs):
            kernel(*refs[:first], *refs[first + len(last) :])

        result = pl.pallas_call(
            body,
            out_shape=shapes,
            in_specs=[smem] * scalars
            + [pl.BlockSpec(memory_space=pltpu.HBM) if hbm else vmem] * (first - scalars)
            + [pl.BlockSpec(memory_space=pl.ANY)] * len(last),
            out_specs=[vmem] * len(shapes),
            scratch_shapes=list(scratch),
            compiler_params=pltpu.CompilerParams(vmem_limit_bytes=40 * 2**20),
            cost_estimate=pl.CostEstimate(
                flops=flops + weight, bytes_accessed=total, transcendentals=0
            ),
        )(*args, *last)
        self.last = [result[0]]
        return result if many else result[0]


def shards(orbitals, potential, coeffs):
    psi = orbitals[0]
    slabs, bands = lax.axis_size("slab"), lax.axis_size("orb")
    planes, rows, lanes = psi.shape
    wide = rows // bands
    half, part = wide // 2, wide // 4
    chunks = [(0, half), (half, wide)]
    cuts = [(0, half), (half, wide - part), (wide - part, wide)]
    cut_a, cut_b, cut_c = cuts
    padded, inner = (part + 8, part + 4)
    face = [(s, (s - 1 if s % 2 == 0 else s + 1) % slabs) for s in range(slabs)]
    partner = [(s, s ^ 1) for s in range(slabs)]
    near = [(i, i ^ 1) for i in range(bands)]
    far = [(i, i ^ 3) for i in range(bands)]
    plane2 = (2, rows, lanes)
    cells = 2 * rows * lanes
    call = Line()

    def as_bands(x):
        return x.reshape(x.shape[0], bands, wide, lanes)

    def slab_shape(chunk):
        return (2, bands, chunk[1] - chunk[0], lanes)

    def pair_shape(chunk):
        return (2, 2, chunk[1] - chunk[0], lanes)

    def add_far(keep, came):
        total = call(add_kernel, keep.shape[1:], (keep, came))
        return keep, came, lax.ppermute(total, "orb", far)

    def squares(cut, halo):
        keep, send = call(
            functools.partial(last_kernel, cut),
            [pair_shape(cut)] * 2,
            (row, halo, as_bands(h_front)),
        )
        return keep, lax.ppermute(send, "orb", near)

    def over_orb(x, d):
        return lax.ppermute(x, "orb", [(i, i ^ d) for i in range(bands)])

    def back_squares(chunk, rows, halo, weight=0):
        keep, send = call(
            functools.partial(back_kernel, chunk, rows),
            [pair_shape(rows)] * 2,
            (row, halo, as_bands(h_back)),
            weight=weight,
        )
        return keep, lax.ppermute(send, "orb", near)

    def faces(chunk, halo, parts):
        fs = call(
            functools.partial(face_kernel, chunk, parts),
            [slab_shape(cut) for cut in parts],
            (halo, as_bands(g)),
        )
        return fs, lax.ppermute(fs[0], "slab", face)

    psi_in = lax.ppermute(psi, "slab", partner)
    pot_in = lax.ppermute(potential, "slab", partner)
    halos = []
    for chunk in chunks:
        piece = call(
            functools.partial(pack_kernel, chunk),
            slab_shape(chunk),
            (as_bands(psi),),
            scratch=[pltpu.SemaphoreType.DMA],
            hbm=True,
        )
        halos.append(lax.ppermute(piece, "slab", face))
    keep, *sends = call(
        functools.partial(send_rows_kernel, cut_c),
        [(planes, padded, lanes)] * bands,
        (as_bands(psi),),
    )
    x_parts = [keep, *[over_orb(x, d) for d, x in zip(offsets(bands)[1:], sends)]]
    g = call(start_kernel, plane2, (psi, potential), flops=24 * cells)
    t, h_back, row = call(
        inner_kernel,
        [plane2, plane2, (8, lanes)],
        (coeffs, psi, potential, psi_in, pot_in, g),
        scalars=1,
        flops=80 * cells,
    )

    def summed(keep, came, from_far, weight=0):
        return call(sum_kernel, from_far.shape, (keep, came, from_far), weight=weight)

    f0, face_a = faces(chunks[0], halos[0], [cut_a])
    x, piece = call(
        gather_kernel,
        [(bands, planes, padded, lanes), (2 * (bands - 1) * inner, lanes)],
        x_parts,
    )
    x_in = lax.ppermute(x, "slab", partner)
    x_halo = lax.ppermute(piece, "slab", face)
    back0 = back_squares(chunks[0], cut_a, halos[0])
    f1, face_b = faces(chunks[1], halos[1], [cut_b, cut_c])
    back1 = back_squares(chunks[1], cut_b, halos[1], weight=8_000_000_000)
    x_first, x_t, x_back = call(
        functools.partial(rows_kernel, cut_c),
        [(bands, 2, inner, lanes)] + [(bands, 2, part, lanes)] * 2,
        (coeffs, x, x_in, as_bands(potential), as_bands(pot_in)),
        scalars=1,
    )
    back0 = add_far(*back0)
    h_front = call(
        functools.partial(front_kernel, cuts),
        plane2,
        (coeffs, psi, potential, t, *f0, *f1),
        scalars=1,
        scratch=[pltpu.VMEM(plane2, jnp.float32)],
        flops=40 * cells,
    )
    back1 = add_far(*back1)
    front_a = squares(cut_a, face_a)
    back0 = summed(*back0)
    front_b = squares(cut_b, face_b)
    back1 = summed(*back1, weight=4_000_000_000)
    x_f, piece = call(
        functools.partial(rows_face_kernel, cut_c),
        [(bands, 2, inner, lanes), (bands, 2, part, lanes)],
        (x_halo, *halos, x_first),
    )
    x_face = lax.ppermute(piece, "slab", face)
    front_a = add_far(*front_a)
    front_b = add_far(*front_b)
    back2, x_front = call(
        functools.partial(rows_front_kernel, cut_c),
        [(2, part, lanes), (bands, 2, part, lanes)],
        (coeffs, x, as_bands(potential), x_halo, *halos, x_f, x_t, x_back),
        scalars=1,
    )
    front_a = summed(*front_a)
    front_b = summed(*front_b, weight=1_000_000_000)
    places = [(2, cut) for cut in cuts] + [(0, cut_a), (0, cut_b)]
    return call(
        functools.partial(join_kernel, places, cut_c),
        (planes, wide, lanes),
        (back0, back1, back2, front_a, front_b, row, x_face, x_front),
    )


def solution(mesh):
    return jax.shard_map(
        shards,
        mesh=mesh,
        in_specs=(P("orb", "slab", None, None), P("slab", None, None), P()),
        out_specs=P("slab", "orb", None),
        check_vma=False,
    )
```

```python
import functools

import jax
import jax.numpy as jnp
from jax import lax
from jax.experimental import pallas as pl
from jax.experimental.pallas import tpu as pltpu
from jax.sharding import PartitionSpec as P

NEAR = -2.0 / 15.0
FAR = 1.0 / 120.0
BLOCK = 16


def own(q, odd):
    return jnp.where(odd == 1, 3 - q, q)


def parity():
    return lax.rem(lax.axis_index("slab"), 2)


def with_halo(ref, plane, start, count):
    rows = ref.shape[-2]
    before = pl.multiple_of(lax.rem(start + rows - 8, rows), 8)
    after = pl.multiple_of(lax.rem(start + count, rows), 8)
    return jnp.concatenate(
        [
            ref[plane, pl.ds(before, 8), :],
            ref[plane, pl.ds(start, count), :],
            ref[plane, pl.ds(after, 8), :],
        ],
        axis=0,
    )


def in_plane(ext):
    count, lanes = ext.shape[0] - 16, ext.shape[1]
    mid = ext[8 : 8 + count]
    near = ext[7 : 7 + count] + ext[9 : 9 + count]
    near = near + (pltpu.roll(mid, 1, 1) + pltpu.roll(mid, lanes - 1, 1))
    far = ext[6 : 6 + count] + ext[10 : 10 + count]
    far = far + (pltpu.roll(mid, 2, 1) + pltpu.roll(mid, lanes - 2, 1))
    return mid, near, far


def apply_s(ext, pot, near_z, far_z):
    mid, near, far = in_plane(ext)
    return mid, (
        mid * (0.2 * pot - 0.05) + NEAR * (near + near_z) + FAR * (far + far_z)
    )


def apply_rows(e, pot, near_z, far_z):
    count, lanes = e.shape[0] - 4, e.shape[1]
    mid = e[2 : 2 + count]
    near = e[1 : 1 + count] + e[3 : 3 + count]
    near = near + (pltpu.roll(mid, 1, 1) + pltpu.roll(mid, lanes - 1, 1))
    far = e[0:count] + e[4 : 4 + count]
    far = far + (pltpu.roll(mid, 2, 1) + pltpu.roll(mid, lanes - 2, 1))
    return mid * (0.2 * pot - 0.05) + NEAR * (near + near_z) + FAR * (far + far_z)


def blocks(rows, body):
    def step(i, carry):
        body(pl.multiple_of(i * BLOCK, BLOCK))
        return carry

    lax.fori_loop(0, rows // BLOCK, step, 0, unroll=4)


def pack_kernel(chunk, psi, out, sem):
    lo, hi = chunk
    planes = pl.ds(2 * parity(), out.shape[0])
    copy = pltpu.make_async_copy(psi.at[planes, :, pl.ds(lo, hi - lo), :], out, sem)
    copy.start()
    copy.wait()


def start_kernel(psi, pot, g):
    odd = parity()

    def body(r):
        here = pl.ds(r, BLOCK)
        at = [own(q, odd) for q in range(4)]
        e0, e1 = with_halo(psi, at[0], r, BLOCK), with_halo(psi, at[1], r, BLOCK)
        p2, p3 = psi[at[2], here, :], psi[at[3], here, :]
        g[0, here, :] = apply_s(e0, pot[at[0], here, :], e1[8:-8], p2)[1]
        g[1, here, :] = apply_s(e1, pot[at[1], here, :], e0[8:-8] + p2, p3)[1]

    blocks(psi.shape[1], body)


def inner_kernel(c, psi, pot, psi_in, pot_in, g, t, h, row):
    odd = parity()
    at = [own(q, odd) for q in range(4)]
    base, one, two = c[0] - c[2], c[1], 2.0 * c[2]

    def first(r):
        here = pl.ds(r, BLOCK)
        e2, e3 = with_halo(psi, at[2], r, BLOCK), with_halo(psi, at[3], r, BLOCK)
        p0, p1 = psi[at[0], here, :], psi[at[1], here, :]
        p4, p5 = psi_in[at[0], here, :], psi_in[at[1], here, :]
        t[0, here, :] = apply_s(e2, pot[at[2], here, :], p1 + e3[8:-8], p0 + p4)[1]
        t[1, here, :] = apply_s(e3, pot[at[3], here, :], e2[8:-8] + p4, p1 + p5)[1]

    def second(r):
        here = pl.ds(r, BLOCK)
        e4 = with_halo(psi_in, at[0], r, BLOCK)
        e5 = with_halo(psi_in, at[1], r, BLOCK)
        p2, p3 = psi[at[2], here, :], psi[at[3], here, :]
        p6, p7 = psi_in[at[2], here, :], psi_in[at[3], here, :]
        t4 = apply_s(e4, pot_in[at[0], here, :], p3 + e5[8:-8], p2 + p6)[1]
        t5 = apply_s(e5, pot_in[at[1], here, :], e4[8:-8] + p6, p3 + p7)[1]
        g0, g1 = g[0, here, :], g[1, here, :]
        e2, e3 = with_halo(t, 0, r, BLOCK), with_halo(t, 1, r, BLOCK)
        t2, s2 = apply_s(e2, pot[at[2], here, :], g1 + e3[8:-8], g0 + t4)
        t3, s3 = apply_s(e3, pot[at[3], here, :], e2[8:-8] + t4, g1 + t5)
        h[0, here, :] = base * p2 + one * t2 + two * s2
        h[1, here, :] = base * p3 + one * t3 + two * s3

    row[...] = jnp.full(row.shape, two)
    blocks(psi.shape[1], first)
    blocks(psi.shape[1], second)


def halo_terms(halo, band, odd, rows=slice(None)):
    near, far = halo[1 - odd, band, rows, :], halo[odd, band, rows, :]
    return NEAR * near + FAR * far, FAR * near


def square(x, bands):
    return x * x * (1.0 / bands)


def face_kernel(chunk, parts, halo, g, *fs):
    odd = parity()
    lo, hi = chunk
    for (first, last), f in zip(parts, fs):
        in_halo = slice(first - lo, last - lo)
        for band in range(halo.shape[1]):
            d0, d1 = halo_terms(halo, band, odd, in_halo)
            f[0, band] = g[0, band, first:last, :] + d0
            f[1, band] = g[1, band, first:last, :] + d1


def offsets(bands):
    return [0, *range(bands - 1, 0, -1)]


def back_kernel(chunk, part, row, halo, h, keep, send):
    odd = parity()
    lo, hi = part
    in_halo = slice(lo - chunk[0], hi - chunk[0])
    two = row[0:1, :]
    me = lax.axis_index("orb")
    bands = halo.shape[1]

    def put(band, out, slot):
        d0, d1 = halo_terms(halo, band, odd, in_halo)
        v2 = h[0, band, lo:hi, :] + two * (NEAR * d1 + FAR * d0)
        v3 = h[1, band, lo:hi, :] + two * (FAR * d1)
        out[slot, 0] = square(v2, bands)
        out[slot, 1] = square(v3, bands)

    put(me ^ 1, send, 0)
    put(me ^ 2, send, 1)
    put(me, keep, 0)
    put(me ^ 3, keep, 1)


def tail_rows(ref, plane, band, start, more):
    after = lax.rem(band + 1, ref.shape[1])
    return jnp.concatenate(
        [ref[plane, band, start:, :], ref[plane, after, :more, :]], axis=0
    )


def send_rows_kernel(part, psi, *outs):
    me = lax.axis_index("orb")
    for d, out in zip(offsets(psi.shape[1]), outs):
        for plane in range(psi.shape[0]):
            out[plane] = tail_rows(psi, plane, me ^ d, part[0] - 4, 4)


def gather_kernel(*refs):
    every, halo = refs[-2:]
    odd = parity()
    count = halo.shape[0] // (2 * (len(refs) - 3))
    for k, ref in enumerate(refs[:-2]):
        every[k] = ref[...]
        for q in range(2):
            if k:
                first = (2 * (k - 1) + q) * count
                halo[first : first + count, :] = ref[own(q, odd), 2 : 2 + count, :]


def rows_kernel(part, c, x, x_in, pot, pot_in, g, t, h):
    odd = parity()
    me = lax.axis_index("orb")
    at = [own(q, odd) for q in range(4)]
    base, one, two = c[0] - c[2], c[1], 2.0 * c[2]
    v = [tail_rows(pot, at[q], me, part[0] - 2, 2) for q in range(4)]
    v += [tail_rows(pot_in, at[q], me, part[0] - 2, 2) for q in range(2)]
    n = g.shape[2]

    def step(k, carry):
        e = [x[k, at[q]] for q in range(4)] + [x_in[k, at[q]] for q in range(4)]
        m = [y[2 : 2 + n] for y in e]
        g0 = apply_rows(e[0], v[0], m[1], m[2])
        g1 = apply_rows(e[1], v[1], m[0] + m[2], m[3])
        g[k, 0], g[k, 1] = g0, g1
        full = [apply_rows(e[q], v[q], m[q - 1] + m[q + 1], m[q - 2] + m[q + 2])
                for q in range(2, 6)]
        f = [y[2 : n - 2] for y in [g0, g1, *full]]
        for j in range(2):
            t[k, j] = f[2 + j]
            q = 2 + j
            s = apply_rows(full[j], v[q][2 : n - 2], f[q - 1] + f[q + 1], f[q - 2] + f[q + 2])
            h[k, j] = base * e[q][4 : n] + one * f[q] + two * s
        return carry

    lax.fori_loop(0, x.shape[0], step, 0, unroll=True)


def rows_halo(part, k, halo, first, second, n):
    if k:
        at = [(2 * (k - 1) + q) * n for q in range(2)]
        near, far = [halo[a : a + n, :] for a in at]
    else:
        odd = parity()
        me = lax.axis_index("orb")
        after = lax.rem(me + 1, first.shape[1])
        near, far = [
            jnp.concatenate(
                [second[q, me, second.shape[2] - (n - 2) :, :], first[q, after, :2, :]],
                axis=0,
            )
            for q in (1 - odd, odd)
        ]
    return NEAR * near + FAR * far, FAR * near


def rows_face_kernel(part, halo, first, second, g, f, send):
    n = g.shape[2]
    for k in range(g.shape[0]):
        terms = rows_halo(part, k, halo, first, second, n)
        for q in range(2):
            value = g[k, q] + terms[q]
            f[k, q] = value
            send[k, q] = value[2 : n - 2]


def rows_front_kernel(part, c, x, pot, halo, first, second, f, t, h, back, front):
    odd = parity()
    me = lax.axis_index("orb")
    base, one, two = c[0] - c[2], c[1], 2.0 * c[2]
    n = f.shape[2]
    v = [
        tail_rows(pot, own(q, odd), me, part[0] - 2, 2)[2 : n - 2] for q in range(2)
    ]
    total = [0.0, 0.0]
    count = f.shape[0]
    for k in range(count):
        d0, d1 = [y[2 : n - 2] for y in rows_halo(part, k, halo, first, second, n)]
        v2 = h[k, 0] + two * (NEAR * d1 + FAR * d0)
        v3 = h[k, 1] + two * (FAR * d1)
        total = [total[0] + square(v2, count), total[1] + square(v3, count)]
        f0, f1 = f[k, 0], f[k, 1]
        t2, t3 = t[k, 0], t[k, 1]
        m0, m1 = f0[2 : n - 2], f1[2 : n - 2]
        s0 = apply_rows(f0, v[0], m1, t2)
        s1 = apply_rows(f1, v[1], m0 + t2, t3)
        front[k, 0] = base * x[k, own(0, odd)][4:n] + one * m0 + two * s0
        front[k, 1] = base * x[k, own(1, odd)][4:n] + one * m1 + two * s1
    back[0], back[1] = total


def front_kernel(chunks, c, psi, pot, t, *rest):
    fs, h, scratch = rest[:-2], rest[-2], rest[-1]
    odd = parity()
    at = [own(q, odd) for q in range(2)]
    base, one, two = c[0] - c[2], c[1], 2.0 * c[2]
    rows = psi.shape[1]
    for (lo, hi), f in zip(chunks, fs):
        bands = f.shape[1]
        for band in range(bands):
            first_row = band * (rows // bands)
            for q in range(2):
                scratch[q, first_row + lo : first_row + hi, :] = f[q, band]

    def body(r):
        here = pl.ds(r, BLOCK)
        e0, e1 = with_halo(scratch, 0, r, BLOCK), with_halo(scratch, 1, r, BLOCK)
        t2, t3 = t[0, here, :], t[1, here, :]
        f0, s0 = apply_s(e0, pot[at[0], here, :], e1[8:-8], t2)
        f1, s1 = apply_s(e1, pot[at[1], here, :], e0[8:-8] + t2, t3)
        h[0, here, :] = base * psi[at[0], here, :] + one * f0 + two * s0
        h[1, here, :] = base * psi[at[1], here, :] + one * f1 + two * s1

    blocks(rows, body)


def last_kernel(chunk, row, halo, h, keep, send):
    lo, hi = chunk
    two = row[0:1, :]
    me = lax.axis_index("orb")
    bands = halo.shape[1]

    def part(band, out, slot):
        near, far = halo[0, band], halo[1, band]
        v0 = h[0, band, lo:hi, :] + two * (NEAR * near + FAR * far)
        v1 = h[1, band, lo:hi, :] + two * (FAR * near)
        out[slot, 0] = square(v0, bands)
        out[slot, 1] = square(v1, bands)

    part(me ^ 1, send, 0)
    part(me ^ 2, send, 1)
    part(me, keep, 0)
    part(me ^ 3, keep, 1)


def add_kernel(keep, came, out):
    out[...] = keep[1] + came[1]


def sum_kernel(keep, came, far, out):
    out[...] = keep[0] + came[0] + far[...]


def join_kernel(places, part, *refs):
    row, halo, h, out = refs[-4:]
    odd = parity()
    for (q, (lo, hi)), ref in zip(places, refs):
        for j in range(2):
            out[own(q + j, odd), lo:hi, :] = ref[j]
    two = row[0:1, :]
    count = h.shape[0]
    total = [0.0, 0.0]
    for k in range(count):
        near, far = halo[k, 0], halo[k, 1]
        v0 = h[k, 0] + two * (NEAR * near + FAR * far)
        v1 = h[k, 1] + two * (FAR * near)
        total = [total[0] + square(v0, count), total[1] + square(v1, count)]
    for j in range(2):
        out[own(j, odd), part[0] : part[1], :] = total[j]


class Line:
    def __init__(self):
        self.last = []

    def __call__(self, kernel, out, args, scalars=0, scratch=(), flops=0, hbm=False, weight=0):
        vmem = pl.BlockSpec(memory_space=pltpu.VMEM)
        smem = pl.BlockSpec(memory_space=pltpu.SMEM)
        many = isinstance(out, list)
        shapes = [jax.ShapeDtypeStruct(s, jnp.float32) for s in (out if many else [out])]
        total = sum(4 * int(x.size) for x in list(args) + shapes)
        first, last = len(args), self.last

        def body(*refs):
            kernel(*refs[:first], *refs[first + len(last) :])

        result = pl.pallas_call(
            body,
            out_shape=shapes,
            in_specs=[smem] * scalars
            + [pl.BlockSpec(memory_space=pltpu.HBM) if hbm else vmem] * (first - scalars)
            + [pl.BlockSpec(memory_space=pl.ANY)] * len(last),
            out_specs=[vmem] * len(shapes),
            scratch_shapes=list(scratch),
            compiler_params=pltpu.CompilerParams(vmem_limit_bytes=40 * 2**20),
            cost_estimate=pl.CostEstimate(
                flops=flops + weight, bytes_accessed=total, transcendentals=0
            ),
        )(*args, *last)
        self.last = [result[0]]
        return result if many else result[0]


def shards(orbitals, potential, coeffs):
    psi = orbitals[0]
    slabs, bands = lax.axis_size("slab"), lax.axis_size("orb")
    planes, rows, lanes = psi.shape
    wide = rows // bands
    half, part = wide // 2, wide // 4
    chunks = [(0, half), (half, wide)]
    cuts = [(0, half), (half, wide - part), (wide - part, wide)]
    cut_a, cut_b, cut_c = cuts
    padded, inner = (part + 8, part + 4)
    face = [(s, (s - 1 if s % 2 == 0 else s + 1) % slabs) for s in range(slabs)]
    partner = [(s, s ^ 1) for s in range(slabs)]
    near = [(i, i ^ 1) for i in range(bands)]
    far = [(i, i ^ 3) for i in range(bands)]
    plane2 = (2, rows, lanes)
    cells = 2 * rows * lanes
    call = Line()

    def as_bands(x):
        return x.reshape(x.shape[0], bands, wide, lanes)

    def slab_shape(chunk):
        return (2, bands, chunk[1] - chunk[0], lanes)

    def pair_shape(chunk):
        return (2, 2, chunk[1] - chunk[0], lanes)

    def add_far(keep, came):
        total = call(add_kernel, keep.shape[1:], (keep, came))
        return keep, came, lax.ppermute(total, "orb", far)

    def squares(cut, halo):
        keep, send = call(
            functools.partial(last_kernel, cut),
            [pair_shape(cut)] * 2,
            (row, halo, as_bands(h_front)),
        )
        return keep, lax.ppermute(send, "orb", near)

    def over_orb(x, d):
        return lax.ppermute(x, "orb", [(i, i ^ d) for i in range(bands)])

    def back_squares(chunk, rows, halo, weight=0):
        keep, send = call(
            functools.partial(back_kernel, chunk, rows),
            [pair_shape(rows)] * 2,
            (row, halo, as_bands(h_back)),
            weight=weight,
        )
        return keep, lax.ppermute(send, "orb", near)

    def faces(chunk, halo, parts):
        fs = call(
            functools.partial(face_kernel, chunk, parts),
            [slab_shape(cut) for cut in parts],
            (halo, as_bands(g)),
        )
        return fs, lax.ppermute(fs[0], "slab", face)

    psi_in = lax.ppermute(psi, "slab", partner)
    pot_in = lax.ppermute(potential, "slab", partner)
    halos = []
    for chunk in chunks:
        piece = call(
            functools.partial(pack_kernel, chunk),
            slab_shape(chunk),
            (as_bands(psi),),
            scratch=[pltpu.SemaphoreType.DMA],
            hbm=True,
        )
        halos.append(lax.ppermute(piece, "slab", face))
    keep, *sends = call(
        functools.partial(send_rows_kernel, cut_c),
        [(planes, padded, lanes)] * bands,
        (as_bands(psi),),
    )
    x_parts = [keep, *[over_orb(x, d) for d, x in zip(offsets(bands)[1:], sends)]]
    g = call(start_kernel, plane2, (psi, potential), flops=24 * cells)
    t, h_back, row = call(
        inner_kernel,
        [plane2, plane2, (8, lanes)],
        (coeffs, psi, potential, psi_in, pot_in, g),
        scalars=1,
        flops=80 * cells,
    )

    def summed(keep, came, from_far, weight=0):
        return call(sum_kernel, from_far.shape, (keep, came, from_far), weight=weight)

    f0, face_a = faces(chunks[0], halos[0], [cut_a])
    x, piece = call(
        gather_kernel,
        [(bands, planes, padded, lanes), (2 * (bands - 1) * inner, lanes)],
        x_parts,
    )
    x_in = lax.ppermute(x, "slab", partner)
    x_halo = lax.ppermute(piece, "slab", face)
    back0 = back_squares(chunks[0], cut_a, halos[0])
    f1, face_b = faces(chunks[1], halos[1], [cut_b, cut_c])
    back1 = back_squares(chunks[1], cut_b, halos[1])
    back0 = add_far(*back0)
    h_front = call(
        functools.partial(front_kernel, cuts),
        plane2,
        (coeffs, psi, potential, t, *f0, *f1),
        scalars=1,
        scratch=[pltpu.VMEM(plane2, jnp.float32)],
        flops=40 * cells,
    )
    back1 = add_far(*back1)
    front_a = squares(cut_a, face_a)
    back0 = summed(*back0)
    front_b = squares(cut_b, face_b)
    back1 = summed(*back1, weight=2_000_000_000)
    x_first, x_t, x_back = call(
        functools.partial(rows_kernel, cut_c),
        [(bands, 2, inner, lanes)] + [(bands, 2, part, lanes)] * 2,
        (coeffs, x, x_in, as_bands(potential), as_bands(pot_in)),
        scalars=1,
    )
    x_f, piece = call(
        functools.partial(rows_face_kernel, cut_c),
        [(bands, 2, inner, lanes), (bands, 2, part, lanes)],
        (x_halo, *halos, x_first),
    )
    x_face = lax.ppermute(piece, "slab", face)
    front_a = add_far(*front_a)
    front_b = add_far(*front_b)
    back2, x_front = call(
        functools.partial(rows_front_kernel, cut_c),
        [(2, part, lanes), (bands, 2, part, lanes)],
        (coeffs, x, as_bands(potential), x_halo, *halos, x_f, x_t, x_back),
        scalars=1,
    )
    front_a = summed(*front_a)
    front_b = summed(*front_b, weight=1_000_000_000)
    places = [(2, cut) for cut in cuts] + [(0, cut_a), (0, cut_b)]
    return call(
        functools.partial(join_kernel, places, cut_c),
        (planes, wide, lanes),
        (back0, back1, back2, front_a, front_b, row, x_face, x_front),
    )


def solution(mesh):
    return jax.shard_map(
        shards,
        mesh=mesh,
        in_specs=(P("orb", "slab", None, None), P("slab", None, None), P()),
        out_specs=P("slab", "orb", None),
        check_vma=False,
    )
```

```python
import functools

import jax
import jax.numpy as jnp
from jax import lax
from jax.experimental import pallas as pl
from jax.experimental.pallas import tpu as pltpu
from jax.sharding import PartitionSpec as P

NEAR = -2.0 / 15.0
FAR = 1.0 / 120.0
BLOCK = 32


def own(q, odd):
    return jnp.where(odd == 1, 3 - q, q)


def parity():
    return lax.rem(lax.axis_index("slab"), 2)


def with_halo(ref, plane, start, count):
    rows = ref.shape[-2]
    before = pl.multiple_of(lax.rem(start + rows - 8, rows), 8)
    after = pl.multiple_of(lax.rem(start + count, rows), 8)
    return jnp.concatenate(
        [
            ref[plane, pl.ds(before, 8), :],
            ref[plane, pl.ds(start, count), :],
            ref[plane, pl.ds(after, 8), :],
        ],
        axis=0,
    )


def in_plane(ext):
    count, lanes = ext.shape[0] - 16, ext.shape[1]
    mid = ext[8 : 8 + count]
    near = ext[7 : 7 + count] + ext[9 : 9 + count]
    near = near + (pltpu.roll(mid, 1, 1) + pltpu.roll(mid, lanes - 1, 1))
    far = ext[6 : 6 + count] + ext[10 : 10 + count]
    far = far + (pltpu.roll(mid, 2, 1) + pltpu.roll(mid, lanes - 2, 1))
    return mid, near, far


def apply_s(ext, pot, near_z, far_z):
    mid, near, far = in_plane(ext)
    return mid, (
        mid * (0.2 * pot - 0.05) + NEAR * (near + near_z) + FAR * (far + far_z)
    )


def apply_rows(e, pot, near_z, far_z):
    count, lanes = e.shape[0] - 4, e.shape[1]
    mid = e[2 : 2 + count]
    near = e[1 : 1 + count] + e[3 : 3 + count]
    near = near + (pltpu.roll(mid, 1, 1) + pltpu.roll(mid, lanes - 1, 1))
    far = e[0:count] + e[4 : 4 + count]
    far = far + (pltpu.roll(mid, 2, 1) + pltpu.roll(mid, lanes - 2, 1))
    return mid * (0.2 * pot - 0.05) + NEAR * (near + near_z) + FAR * (far + far_z)


def blocks(rows, body):
    def step(i, carry):
        body(pl.multiple_of(i * BLOCK, BLOCK))
        return carry

    lax.fori_loop(0, rows // BLOCK, step, 0, unroll=2)


def pack_kernel(chunk, psi, out, sem):
    lo, hi = chunk
    planes = pl.ds(2 * parity(), out.shape[0])
    copy = pltpu.make_async_copy(psi.at[planes, :, pl.ds(lo, hi - lo), :], out, sem)
    copy.start()
    copy.wait()


def start_kernel(psi, pot, g):
    odd = parity()

    def body(r):
        here = pl.ds(r, BLOCK)
        at = [own(q, odd) for q in range(4)]
        e0, e1 = with_halo(psi, at[0], r, BLOCK), with_halo(psi, at[1], r, BLOCK)
        p2, p3 = psi[at[2], here, :], psi[at[3], here, :]
        g[0, here, :] = apply_s(e0, pot[at[0], here, :], e1[8:-8], p2)[1]
        g[1, here, :] = apply_s(e1, pot[at[1], here, :], e0[8:-8] + p2, p3)[1]

    blocks(psi.shape[1], body)


def inner_kernel(c, psi, pot, psi_in, pot_in, g, t, h, row):
    odd = parity()
    at = [own(q, odd) for q in range(4)]
    base, one, two = c[0] - c[2], c[1], 2.0 * c[2]

    def first(r):
        here = pl.ds(r, BLOCK)
        e2, e3 = with_halo(psi, at[2], r, BLOCK), with_halo(psi, at[3], r, BLOCK)
        p0, p1 = psi[at[0], here, :], psi[at[1], here, :]
        p4, p5 = psi_in[at[0], here, :], psi_in[at[1], here, :]
        t[0, here, :] = apply_s(e2, pot[at[2], here, :], p1 + e3[8:-8], p0 + p4)[1]
        t[1, here, :] = apply_s(e3, pot[at[3], here, :], e2[8:-8] + p4, p1 + p5)[1]

    def second(r):
        here = pl.ds(r, BLOCK)
        e4 = with_halo(psi_in, at[0], r, BLOCK)
        e5 = with_halo(psi_in, at[1], r, BLOCK)
        p2, p3 = psi[at[2], here, :], psi[at[3], here, :]
        p6, p7 = psi_in[at[2], here, :], psi_in[at[3], here, :]
        t4 = apply_s(e4, pot_in[at[0], here, :], p3 + e5[8:-8], p2 + p6)[1]
        t5 = apply_s(e5, pot_in[at[1], here, :], e4[8:-8] + p6, p3 + p7)[1]
        g0, g1 = g[0, here, :], g[1, here, :]
        e2, e3 = with_halo(t, 0, r, BLOCK), with_halo(t, 1, r, BLOCK)
        t2, s2 = apply_s(e2, pot[at[2], here, :], g1 + e3[8:-8], g0 + t4)
        t3, s3 = apply_s(e3, pot[at[3], here, :], e2[8:-8] + t4, g1 + t5)
        h[0, here, :] = base * p2 + one * t2 + two * s2
        h[1, here, :] = base * p3 + one * t3 + two * s3

    row[...] = jnp.full(row.shape, two)
    blocks(psi.shape[1], first)
    blocks(psi.shape[1], second)


def halo_terms(halo, band, odd, rows=slice(None)):
    near, far = halo[1 - odd, band, rows, :], halo[odd, band, rows, :]
    return NEAR * near + FAR * far, FAR * near


def square(x, bands):
    return x * x * (1.0 / bands)


def face_kernel(chunk, parts, halo, g, *fs):
    odd = parity()
    lo, hi = chunk
    for (first, last), f in zip(parts, fs):
        in_halo = slice(first - lo, last - lo)
        for band in range(halo.shape[1]):
            d0, d1 = halo_terms(halo, band, odd, in_halo)
            f[0, band] = g[0, band, first:last, :] + d0
            f[1, band] = g[1, band, first:last, :] + d1


def offsets(bands):
    return [0, *range(bands - 1, 0, -1)]


def back_kernel(chunk, part, row, halo, h, keep, send):
    odd = parity()
    lo, hi = part
    in_halo = slice(lo - chunk[0], hi - chunk[0])
    two = row[0:1, :]
    me = lax.axis_index("orb")
    bands = halo.shape[1]

    def put(band, out, slot):
        d0, d1 = halo_terms(halo, band, odd, in_halo)
        v2 = h[0, band, lo:hi, :] + two * (NEAR * d1 + FAR * d0)
        v3 = h[1, band, lo:hi, :] + two * (FAR * d1)
        out[slot, 0] = square(v2, bands)
        out[slot, 1] = square(v3, bands)

    put(me ^ 1, send, 0)
    put(me ^ 2, send, 1)
    put(me, keep, 0)
    put(me ^ 3, keep, 1)


def tail_rows(ref, plane, band, start, more):
    after = lax.rem(band + 1, ref.shape[1])
    return jnp.concatenate(
        [ref[plane, band, start:, :], ref[plane, after, :more, :]], axis=0
    )


def send_rows_kernel(part, psi, *outs):
    me = lax.axis_index("orb")
    for d, out in zip(offsets(psi.shape[1]), outs):
        for plane in range(psi.shape[0]):
            out[plane] = tail_rows(psi, plane, me ^ d, part[0] - 4, 4)


def gather_kernel(*refs):
    every, halo = refs[-2:]
    odd = parity()
    count = halo.shape[0] // (2 * (len(refs) - 3))
    for k, ref in enumerate(refs[:-2]):
        every[k] = ref[...]
        for q in range(2):
            if k:
                first = (2 * (k - 1) + q) * count
                halo[first : first + count, :] = ref[own(q, odd), 2 : 2 + count, :]


def rows_kernel(part, c, x, x_in, pot, pot_in, g, t, h):
    odd = parity()
    me = lax.axis_index("orb")
    at = [own(q, odd) for q in range(4)]
    base, one, two = c[0] - c[2], c[1], 2.0 * c[2]
    v = [tail_rows(pot, at[q], me, part[0] - 2, 2) for q in range(4)]
    v += [tail_rows(pot_in, at[q], me, part[0] - 2, 2) for q in range(2)]
    n = g.shape[2]

    def step(k, carry):
        e = [x[k, at[q]] for q in range(4)] + [x_in[k, at[q]] for q in range(4)]
        m = [y[2 : 2 + n] for y in e]
        g0 = apply_rows(e[0], v[0], m[1], m[2])
        g1 = apply_rows(e[1], v[1], m[0] + m[2], m[3])
        g[k, 0], g[k, 1] = g0, g1
        full = [apply_rows(e[q], v[q], m[q - 1] + m[q + 1], m[q - 2] + m[q + 2])
                for q in range(2, 6)]
        f = [y[2 : n - 2] for y in [g0, g1, *full]]
        for j in range(2):
            t[k, j] = f[2 + j]
            q = 2 + j
            s = apply_rows(full[j], v[q][2 : n - 2], f[q - 1] + f[q + 1], f[q - 2] + f[q + 2])
            h[k, j] = base * e[q][4 : n] + one * f[q] + two * s
        return carry

    lax.fori_loop(0, x.shape[0], step, 0, unroll=True)


def rows_halo(part, k, halo, first, second, n):
    if k:
        at = [(2 * (k - 1) + q) * n for q in range(2)]
        near, far = [halo[a : a + n, :] for a in at]
    else:
        odd = parity()
        me = lax.axis_index("orb")
        after = lax.rem(me + 1, first.shape[1])
        near, far = [
            jnp.concatenate(
                [second[q, me, second.shape[2] - (n - 2) :, :], first[q, after, :2, :]],
                axis=0,
            )
            for q in (1 - odd, odd)
        ]
    return NEAR * near + FAR * far, FAR * near


def rows_face_kernel(part, halo, first, second, g, f, send):
    n = g.shape[2]
    for k in range(g.shape[0]):
        terms = rows_halo(part, k, halo, first, second, n)
        for q in range(2):
            value = g[k, q] + terms[q]
            f[k, q] = value
            send[k, q] = value[2 : n - 2]


def rows_front_kernel(part, c, x, pot, halo, first, second, f, t, h, back, front):
    odd = parity()
    me = lax.axis_index("orb")
    base, one, two = c[0] - c[2], c[1], 2.0 * c[2]
    n = f.shape[2]
    v = [
        tail_rows(pot, own(q, odd), me, part[0] - 2, 2)[2 : n - 2] for q in range(2)
    ]
    total = [0.0, 0.0]
    count = f.shape[0]
    for k in range(count):
        d0, d1 = [y[2 : n - 2] for y in rows_halo(part, k, halo, first, second, n)]
        v2 = h[k, 0] + two * (NEAR * d1 + FAR * d0)
        v3 = h[k, 1] + two * (FAR * d1)
        total = [total[0] + square(v2, count), total[1] + square(v3, count)]
        f0, f1 = f[k, 0], f[k, 1]
        t2, t3 = t[k, 0], t[k, 1]
        m0, m1 = f0[2 : n - 2], f1[2 : n - 2]
        s0 = apply_rows(f0, v[0], m1, t2)
        s1 = apply_rows(f1, v[1], m0 + t2, t3)
        front[k, 0] = base * x[k, own(0, odd)][4:n] + one * m0 + two * s0
        front[k, 1] = base * x[k, own(1, odd)][4:n] + one * m1 + two * s1
    back[0], back[1] = total


def front_kernel(chunks, c, psi, pot, t, *rest):
    fs, h, scratch = rest[:-2], rest[-2], rest[-1]
    odd = parity()
    at = [own(q, odd) for q in range(2)]
    base, one, two = c[0] - c[2], c[1], 2.0 * c[2]
    rows = psi.shape[1]
    for (lo, hi), f in zip(chunks, fs):
        bands = f.shape[1]
        for band in range(bands):
            first_row = band * (rows // bands)
            for q in range(2):
                scratch[q, first_row + lo : first_row + hi, :] = f[q, band]

    def body(r):
        here = pl.ds(r, BLOCK)
        e0, e1 = with_halo(scratch, 0, r, BLOCK), with_halo(scratch, 1, r, BLOCK)
        t2, t3 = t[0, here, :], t[1, here, :]
        f0, s0 = apply_s(e0, pot[at[0], here, :], e1[8:-8], t2)
        f1, s1 = apply_s(e1, pot[at[1], here, :], e0[8:-8] + t2, t3)
        h[0, here, :] = base * psi[at[0], here, :] + one * f0 + two * s0
        h[1, here, :] = base * psi[at[1], here, :] + one * f1 + two * s1

    blocks(rows, body)


def last_kernel(chunk, row, halo, h, keep, send):
    lo, hi = chunk
    two = row[0:1, :]
    me = lax.axis_index("orb")
    bands = halo.shape[1]

    def part(band, out, slot):
        near, far = halo[0, band], halo[1, band]
        v0 = h[0, band, lo:hi, :] + two * (NEAR * near + FAR * far)
        v1 = h[1, band, lo:hi, :] + two * (FAR * near)
        out[slot, 0] = square(v0, bands)
        out[slot, 1] = square(v1, bands)

    part(me ^ 1, send, 0)
    part(me ^ 2, send, 1)
    part(me, keep, 0)
    part(me ^ 3, keep, 1)


def add_kernel(keep, came, out):
    out[...] = keep[1] + came[1]


def sum_kernel(keep, came, far, out):
    out[...] = keep[0] + came[0] + far[...]


def join_kernel(places, part, *refs):
    row, halo, h, out = refs[-4:]
    odd = parity()
    for (q, (lo, hi)), ref in zip(places, refs):
        for j in range(2):
            out[own(q + j, odd), lo:hi, :] = ref[j]
    two = row[0:1, :]
    count = h.shape[0]
    total = [0.0, 0.0]
    for k in range(count):
        near, far = halo[k, 0], halo[k, 1]
        v0 = h[k, 0] + two * (NEAR * near + FAR * far)
        v1 = h[k, 1] + two * (FAR * near)
        total = [total[0] + square(v0, count), total[1] + square(v1, count)]
    for j in range(2):
        out[own(j, odd), part[0] : part[1], :] = total[j]


class Line:
    def __init__(self):
        self.last = []

    def __call__(self, kernel, out, args, scalars=0, scratch=(), flops=0, hbm=False, weight=0):
        vmem = pl.BlockSpec(memory_space=pltpu.VMEM)
        smem = pl.BlockSpec(memory_space=pltpu.SMEM)
        many = isinstance(out, list)
        shapes = [jax.ShapeDtypeStruct(s, jnp.float32) for s in (out if many else [out])]
        total = sum(4 * int(x.size) for x in list(args) + shapes)
        first, last = len(args), self.last

        def body(*refs):
            kernel(*refs[:first], *refs[first + len(last) :])

        result = pl.pallas_call(
            body,
            out_shape=shapes,
            in_specs=[smem] * scalars
            + [pl.BlockSpec(memory_space=pltpu.HBM) if hbm else vmem] * (first - scalars)
            + [pl.BlockSpec(memory_space=pl.ANY)] * len(last),
            out_specs=[vmem] * len(shapes),
            scratch_shapes=list(scratch),
            compiler_params=pltpu.CompilerParams(vmem_limit_bytes=40 * 2**20),
            cost_estimate=pl.CostEstimate(
                flops=flops + weight, bytes_accessed=total, transcendentals=0
            ),
        )(*args, *last)
        self.last = [result[0]]
        return result if many else result[0]


def shards(orbitals, potential, coeffs):
    psi = orbitals[0]
    slabs, bands = lax.axis_size("slab"), lax.axis_size("orb")
    planes, rows, lanes = psi.shape
    wide = rows // bands
    half, part = wide // 2, wide // 4
    chunks = [(0, half), (half, wide)]
    cuts = [(0, half), (half, wide - part), (wide - part, wide)]
    cut_a, cut_b, cut_c = cuts
    padded, inner = (part + 8, part + 4)
    face = [(s, (s - 1 if s % 2 == 0 else s + 1) % slabs) for s in range(slabs)]
    partner = [(s, s ^ 1) for s in range(slabs)]
    near = [(i, i ^ 1) for i in range(bands)]
    far = [(i, i ^ 3) for i in range(bands)]
    plane2 = (2, rows, lanes)
    cells = 2 * rows * lanes
    call = Line()

    def as_bands(x):
        return x.reshape(x.shape[0], bands, wide, lanes)

    def slab_shape(chunk):
        return (2, bands, chunk[1] - chunk[0], lanes)

    def pair_shape(chunk):
        return (2, 2, chunk[1] - chunk[0], lanes)

    def add_far(keep, came):
        total = call(add_kernel, keep.shape[1:], (keep, came))
        return keep, came, lax.ppermute(total, "orb", far)

    def squares(cut, halo):
        keep, send = call(
            functools.partial(last_kernel, cut),
            [pair_shape(cut)] * 2,
            (row, halo, as_bands(h_front)),
        )
        return keep, lax.ppermute(send, "orb", near)

    def over_orb(x, d):
        return lax.ppermute(x, "orb", [(i, i ^ d) for i in range(bands)])

    def back_squares(chunk, rows, halo, weight=0):
        keep, send = call(
            functools.partial(back_kernel, chunk, rows),
            [pair_shape(rows)] * 2,
            (row, halo, as_bands(h_back)),
            weight=weight,
        )
        return keep, lax.ppermute(send, "orb", near)

    def faces(chunk, halo, parts):
        fs = call(
            functools.partial(face_kernel, chunk, parts),
            [slab_shape(cut) for cut in parts],
            (halo, as_bands(g)),
        )
        return fs, lax.ppermute(fs[0], "slab", face)

    psi_in = lax.ppermute(psi, "slab", partner)
    pot_in = lax.ppermute(potential, "slab", partner)
    halos = []
    for chunk in chunks:
        piece = call(
            functools.partial(pack_kernel, chunk),
            slab_shape(chunk),
            (as_bands(psi),),
            scratch=[pltpu.SemaphoreType.DMA],
            hbm=True,
        )
        halos.append(lax.ppermute(piece, "slab", face))
    keep, *sends = call(
        functools.partial(send_rows_kernel, cut_c),
        [(planes, padded, lanes)] * bands,
        (as_bands(psi),),
    )
    x_parts = [keep, *[over_orb(x, d) for d, x in zip(offsets(bands)[1:], sends)]]
    g = call(start_kernel, plane2, (psi, potential), flops=24 * cells)
    t, h_back, row = call(
        inner_kernel,
        [plane2, plane2, (8, lanes)],
        (coeffs, psi, potential, psi_in, pot_in, g),
        scalars=1,
        flops=80 * cells,
    )

    def summed(keep, came, from_far, weight=0):
        return call(sum_kernel, from_far.shape, (keep, came, from_far), weight=weight)

    f0, face_a = faces(chunks[0], halos[0], [cut_a])
    x, piece = call(
        gather_kernel,
        [(bands, planes, padded, lanes), (2 * (bands - 1) * inner, lanes)],
        x_parts,
    )
    x_in = lax.ppermute(x, "slab", partner)
    x_halo = lax.ppermute(piece, "slab", face)
    back0 = back_squares(chunks[0], cut_a, halos[0])
    f1, face_b = faces(chunks[1], halos[1], [cut_b, cut_c])
    back1 = back_squares(chunks[1], cut_b, halos[1], weight=8_000_000_000)
    x_first, x_t, x_back = call(
        functools.partial(rows_kernel, cut_c),
        [(bands, 2, inner, lanes)] + [(bands, 2, part, lanes)] * 2,
        (coeffs, x, x_in, as_bands(potential), as_bands(pot_in)),
        scalars=1,
    )
    back0 = add_far(*back0)
    h_front = call(
        functools.partial(front_kernel, cuts),
        plane2,
        (coeffs, psi, potential, t, *f0, *f1),
        scalars=1,
        scratch=[pltpu.VMEM(plane2, jnp.float32)],
        flops=40 * cells,
    )
    back1 = add_far(*back1)
    front_a = squares(cut_a, face_a)
    back0 = summed(*back0)
    front_b = squares(cut_b, face_b)
    back1 = summed(*back1, weight=4_000_000_000)
    x_f, piece = call(
        functools.partial(rows_face_kernel, cut_c),
        [(bands, 2, inner, lanes), (bands, 2, part, lanes)],
        (x_halo, *halos, x_first),
    )
    x_face = lax.ppermute(piece, "slab", face)
    front_a = add_far(*front_a)
    front_b = add_far(*front_b)
    back2, x_front = call(
        functools.partial(rows_front_kernel, cut_c),
        [(2, part, lanes), (bands, 2, part, lanes)],
        (coeffs, x, as_bands(potential), x_halo, *halos, x_f, x_t, x_back),
        scalars=1,
    )
    front_a = summed(*front_a)
    front_b = summed(*front_b, weight=1_000_000_000)
    places = [(2, cut) for cut in cuts] + [(0, cut_a), (0, cut_b)]
    return call(
        functools.partial(join_kernel, places, cut_c),
        (planes, wide, lanes),
        (back0, back1, back2, front_a, front_b, row, x_face, x_front),
    )


def solution(mesh):
    return jax.shard_map(
        shards,
        mesh=mesh,
        in_specs=(P("orb", "slab", None, None), P("slab", None, None), P()),
        out_specs=P("slab", "orb", None),
        check_vma=False,
    )
```
